128 devices in a mesh: blk: 16 (over x_lo, z, core), head: 4 (over y), dp: 2 (over x_hi).
Axes of the slice: x: 4 (x_hi: 2, x_lo: 2; x = x_hi * 2 + x_lo), y: 4, z: 4, core: 2. Of those that a mesh axis runs over, the one named last changes fastest.
Arguments:
- queries: bfloat16 [10240, 2560], P(('dp', 'blk'), 'head'), parts along dimension 0, may hold values from -6 to 6
- keys: bfloat16 [10240, 2560], P(('dp', 'blk'), 'head'), parts along dimension 0, may hold values from -6 to 6
- values: bfloat16 [10240, 2560], P(('dp', 'blk'), 'head'), parts along dimension 0, may hold values from -6 to 6
- t_queries: bfloat16 [10240, 2560], P(('dp', 'blk'), 'head'), parts along dimension 0, may hold values from -6 to 6
- t_keys: bfloat16 [10240, 2560], P(('dp', 'blk'), 'head'), parts along dimension 0, may hold values from -6 to 6
- t_values: bfloat16 [10240, 2560], P(('dp', 'blk'), 'head'), parts along dimension 0, may hold values from -6 to 6
- out_weight: bfloat16 [2560, 5120], P('head'), may hold values from -6 to 6
- stream: bfloat16 [10240, 5120], P(('dp', 'blk', 'head')), parts along dimension 0, may hold values from -6 to 6
- t_stream: bfloat16 [10240, 5120], P(('dp', 'blk', 'head')), parts along dimension 0, may hold values from -6 to 6
- gate: bfloat16 [5120], replicated, may hold values from -4 to 4
- t_gate: bfloat16 [5120], replicated, may hold values from -4 to 4
Outputs:
- result: bfloat16 [10240, 5120], P(('dp', 'blk', 'head')), parts along dimension 0
- t_result: bfloat16 [10240, 5120], P(('dp', 'blk', 'head')), parts along dimension 0
The draws below stay inside these ranges and needn't reach their ends.
There are 2 independent parts, one for each index of `dp`. The reference program is written for one: setup_inputs(seed, part) draws one part's arguments, and reference() takes and returns one part's arrays. A program takes and returns all parts, laid end to end along the dimension named above; an argument that names none is the same for every part. Nothing has to cross between parts.
All inputs are finite; a program needn't handle non-finite values.
Results may differ from the reference program's by a relative error of at most 0.04.
Values may be sent and summed in bfloat16 or wider, within the bound.
No kernel may reach another device: no remote copies, remote signals or barrier semaphores. Data moves between devices by JAX's collectives and lax.ppermute only.
A program may use at most 128 MiB of HBM per device.

```python
import math
import jax
import jax.numpy as jnp
from jax import lax

D = 5120
HEADS = 20
HD = 128
TOKENS = 5120


def draw_queries(key, part):
    key = jax.random.fold_in(key, 1)
    first = jax.random.fold_in(key, 0)
    sample = jax.random.normal(first, (TOKENS, HEADS * HD), jnp.float32)
    sample = jnp.clip(sample, -6.0, 6.0)
    return sample.astype(jnp.bfloat16)


def draw_keys(key, part):
    key = jax.random.fold_in(key, 2)
    first = jax.random.fold_in(key, 0)
    sample = jax.random.normal(first, (TOKENS, HEADS * HD), jnp.float32)
    sample = jnp.clip(sample, -6.0, 6.0)
    return sample.astype(jnp.bfloat16)


def draw_values(key, part):
    key = jax.random.fold_in(key, 3)
    first = jax.random.fold_in(key, 0)
    sample = jnp.clip(jax.random.normal(first, (TOKENS, HEADS * HD), jnp.float32), -6.0, 6.0)
    return sample.astype(jnp.bfloat16)


def level_of(stream_key, extent, shards, least, top_value):
    def one(dim, parts):
        steps = jax.random.uniform(jax.random.fold_in(jax.random.fold_in(stream_key, 6), dim), (parts,), jnp.float32, least / len(shards), top_value / len(shards))
        return jnp.repeat(jnp.exp(steps), extent[dim] // parts).reshape((-1,) + (1,) * (len(extent) - dim - 1))

    level = one(*shards[0])
    for cut in shards[1:]:
        level = level * one(*cut)
    return level


def normal_values(own_key, shape, width, reach, pieces=(), kind=jnp.bfloat16):
    gain = level_of(own_key, shape, pieces, -0.22, 0.18) if pieces else 1.0
    values = jax.random.normal(own_key, shape, jnp.float32) * width * gain
    return jnp.minimum(jnp.maximum(values, -reach), reach).astype(kind)


def setup_inputs(seed: int = 0, part: int = 0) -> dict:
    key_list = jax.random.split(jax.random.key(seed), 12)
    part_splits = jax.random.split(jax.random.fold_in(key_list[11], part), 12)
    return {
        "queries": draw_queries(jax.random.fold_in(jax.random.fold_in(key_list[11], part), 71), part),
        "keys": draw_keys(jax.random.fold_in(jax.random.fold_in(key_list[11], part), 71), part),
        "values": draw_values(jax.random.fold_in(jax.random.fold_in(key_list[11], part), 71), part),
        "t_queries": normal_values(part_splits[3], (TOKENS, HEADS * HD), 1.0, 6.0, ((0, 16), (1, 4))),
        "t_keys": normal_values(part_splits[4], (TOKENS, HEADS * HD), 1.0, 6.0, ((0, 16), (1, 4))),
        "t_values": normal_values(part_splits[5], (TOKENS, HEADS * HD), 1.0, 6.0, ((0, 16), (1, 4))),
        "out_weight": normal_values(key_list[6], (HEADS * HD, D), (max(1, 3 * HEADS * HD // TOKENS)) ** -0.5, 6.0, ((0, 4),)),
        "stream": normal_values(part_splits[7], (TOKENS, D), 1.0, 6.0, ((0, 64),)),
        "t_stream": normal_values(part_splits[8], (TOKENS, D), 1.0, 6.0, ((0, 64),)),
        "gate": normal_values(key_list[9], (D,), 1.0, 4.0),
        "t_gate": normal_values(key_list[10], (D,), 1.0, 4.0),
    }


def head_tangent(operands):
    query, key_part, value_part, t_query, t_key, t_value = operands
    factor = 1.0 / math.sqrt(HD)
    scores = jnp.dot(query, key_part.T, preferred_element_type=jnp.float32) * factor
    slopes = (jnp.dot(t_query, key_part.T, preferred_element_type=jnp.float32) + jnp.dot(query, t_key.T, preferred_element_type=jnp.float32)) * factor
    peak = lax.optimization_barrier(jnp.max(scores, axis=1, keepdims=True))
    weights = jnp.exp(scores - peak)
    probs = weights / lax.optimization_barrier(jnp.sum(weights, axis=1, keepdims=True))
    tilted = probs * slopes
    mean_slope = lax.optimization_barrier(jnp.sum(tilted, axis=1, keepdims=True))
    probs_low = probs.astype(jnp.bfloat16)
    tilted_low = tilted.astype(jnp.bfloat16)
    output = jnp.dot(probs_low, value_part, preferred_element_type=jnp.float32)
    t_output = jnp.dot(tilted_low, value_part, preferred_element_type=jnp.float32) + jnp.dot(probs_low, t_value, preferred_element_type=jnp.float32) - mean_slope * output
    return (output.astype(jnp.bfloat16), t_output.astype(jnp.bfloat16))

def split_heads(array):
    return jnp.transpose(array.reshape(TOKENS, HEADS, HD), (1, 0, 2))

def reference(queries, keys, values, t_queries, t_keys, t_values, out_weight, stream, t_stream, gate, t_gate):
    operands = tuple((split_heads(item) for item in (queries, keys, values, t_queries, t_keys, t_values)))
    output, t_output = lax.map(head_tangent, operands)
    attended = jnp.transpose(output, (1, 0, 2)).reshape(TOKENS, HEADS * HD)
    t_attended = jnp.transpose(t_output, (1, 0, 2)).reshape(TOKENS, HEADS * HD)
    branch = jnp.dot(attended, out_weight, preferred_element_type=jnp.float32)
    t_branch = jnp.dot(t_attended, out_weight, preferred_element_type=jnp.float32)
    gate_wide = gate.astype(jnp.float32)
    result = stream.astype(jnp.float32) + gate_wide * branch
    t_result = t_stream.astype(jnp.float32) + t_gate.astype(jnp.float32) * branch + gate_wide * t_branch
    return (result.astype(jnp.bfloat16), t_result.astype(jnp.bfloat16))
```

```python
import functools

import jax
import jax.numpy as jnp
from jax import lax
from jax.experimental import pallas as pl
from jax.experimental.pallas import tpu as pltpu
from jax.sharding import PartitionSpec as P

HD = 128
LOG2E = 1.4426950408889634
SCALE = HD**-0.5
CHUNK = 512
X_LO, Z, CORE = 2, 4, 2


def along(axis, step):
    pairs = []
    for x in range(X_LO):
        for z in range(Z):
            for c in range(CORE):
                to = {
                    "x": ((x + step) % X_LO, z, c),
                    "z": (x, (z + step) % Z, c),
                    "core": (x, z, (c + step) % CORE),
                }[axis]
                pairs.append(((x * Z + z) * CORE + c, (to[0] * Z + to[1]) * CORE + to[2]))
    return pairs


def shift(value, axis, step):
    return lax.ppermute(value, "blk", along(axis, step))


def attend_kernel(sizes, rows, *refs):
    n = len(sizes)
    near_q, far_q = refs[:2]
    pieces = refs[2 : 2 + n]
    near_ref, far_ref, near_stat, far_stat = refs[2 + n : 6 + n]
    kk, vv, scores = refs[6 + n :]
    at = 0
    for size, piece in zip(sizes, pieces):
        kk[at : at + size, :] = piece[0, :, : 2 * HD]
        vv[at : at + size, :] = piece[0, :, 2 * HD :]
        at += size
    keys = at
    across = (((1,), (1,)), ((), ()))
    for q_ref, out_ref, stat_ref in ((near_q, near_ref, near_stat), (far_q, far_ref, far_stat)):
        query = q_ref[0, :, :HD]
        mixed = jnp.concatenate([q_ref[0, :, HD:], query], axis=1)
        peak = None
        for c in range(0, keys, CHUNK):
            s = lax.dot_general(
                query, kk[c : c + CHUNK, :HD], across, preferred_element_type=jnp.float32
            )
            scores[:, c : c + CHUNK] = s
            for lane in range(0, CHUNK, 128):
                part = s[:, lane : lane + 128]
                peak = part if peak is None else jnp.maximum(peak, part)
        top = jnp.max(peak, axis=1, keepdims=True) * (SCALE * LOG2E)
        den = jnp.zeros((rows, 128), jnp.float32)
        mass = jnp.zeros((rows, 128), jnp.float32)
        wide = jnp.zeros((rows, 2 * HD), jnp.float32)
        tilt = jnp.zeros((rows, HD), jnp.float32)
        for c in range(0, keys, CHUNK):
            slope = lax.dot_general(
                mixed, kk[c : c + CHUNK, :], across, preferred_element_type=jnp.float32
            )
            w = jnp.exp2(scores[:, c : c + CHUNK] * (SCALE * LOG2E) - top)
            g = w * slope
            for lane in range(0, CHUNK, 128):
                den = den + w[:, lane : lane + 128]
                mass = mass + g[:, lane : lane + 128]
            wide = wide + jnp.dot(
                w.astype(jnp.bfloat16), vv[c : c + CHUNK, :], preferred_element_type=jnp.float32
            )
            tilt = tilt + jnp.dot(
                g.astype(jnp.bfloat16), vv[c : c + CHUNK, :HD], preferred_element_type=jnp.float32
            )
        den = jnp.sum(den, axis=1, keepdims=True)
        inverse = 1.0 / den
        mean = jnp.sum(mass, axis=1, keepdims=True) * (inverse * SCALE)
        out = wide[:, :HD] * inverse
        t_out = (tilt * SCALE + wide[:, HD:]) * inverse - mean * out
        out_ref[0, :, :HD] = out.astype(out_ref.dtype)
        out_ref[0, :, HD:] = t_out.astype(out_ref.dtype)
        lane = lax.broadcasted_iota(jnp.int32, (rows, 128), 1)
        both = jnp.where(lane == 0, top + jnp.log2(den), mean)
        stat_ref[0] = jnp.transpose(both)[:8, :]


def attend(near_q, far_q, pieces):
    heads, rows, _ = near_q.shape
    sizes = tuple(p.shape[1] for p in pieces)
    keys = sum(sizes)

    def spec(r, c):
        return pl.BlockSpec((1, r, c), lambda h: (h, 0, 0))

    return pl.pallas_call(
        functools.partial(attend_kernel, sizes, rows),
        grid=(heads,),
        in_specs=[spec(rows, 2 * HD)] * 2 + [spec(s, 4 * HD) for s in sizes],
        out_specs=[spec(rows, 2 * HD), spec(rows, 2 * HD), spec(8, rows), spec(8, rows)],
        out_shape=[
            jax.ShapeDtypeStruct((heads, rows, 2 * HD), jnp.float32),
            jax.ShapeDtypeStruct((heads, rows, 2 * HD), jnp.bfloat16),
            jax.ShapeDtypeStruct((heads, 8, rows), jnp.float32),
            jax.ShapeDtypeStruct((heads, 8, rows), jnp.float32),
        ],
        scratch_shapes=[
            pltpu.VMEM((keys, 2 * HD), jnp.bfloat16),
            pltpu.VMEM((keys, 2 * HD), jnp.bfloat16),
            pltpu.VMEM((rows, keys), jnp.float32),
        ],
        compiler_params=pltpu.CompilerParams(vmem_limit_bytes=48 * 1024 * 1024),
        cost_estimate=pl.CostEstimate(
            flops=heads * 2 * rows * keys * HD * 16,
            bytes_accessed=heads * keys * 1024,
            transcendentals=heads * 2 * rows * keys,
        ),
    )(near_q, far_q, *pieces)


def merge_kernel(near_ref, far_ref, near_stat, far_stat, out_ref):
    a = jnp.transpose(near_stat[0])
    b = jnp.transpose(far_stat[0])
    lse_a, mean_a = a[:, 0:1], a[:, 1:2]
    lse_b, mean_b = b[:, 0:1], b[:, 1:2]
    top = jnp.maximum(lse_a, lse_b)
    wa = jnp.exp2(lse_a - top)
    wb = jnp.exp2(lse_b - top)
    inverse = 1.0 / (wa + wb)
    wa = wa * inverse
    wb = wb * inverse
    mean = wa * mean_a + wb * mean_b
    near = near_ref[0]
    far = far_ref[0].astype(jnp.float32)
    oa, ob = near[:, :HD], far[:, :HD]
    out = wa * oa + wb * ob
    t_out = (
        wa * near[:, HD:]
        + wb * far[:, HD:]
        + (wa * (mean_a - mean)) * oa
        + (wb * (mean_b - mean)) * ob
    )
    out_ref[0] = out.astype(out_ref.dtype)
    out_ref[1] = t_out.astype(out_ref.dtype)


def merge(near, far, near_stat, far_stat):
    heads, rows, _ = near.shape

    def spec(r, c):
        return pl.BlockSpec((1, r, c), lambda h: (h, 0, 0))

    return pl.pallas_call(
        merge_kernel,
        grid=(heads,),
        in_specs=[spec(rows, 2 * HD)] * 2 + [spec(8, rows)] * 2,
        out_specs=pl.BlockSpec((2, rows, HD), lambda h: (0, 0, h)),
        out_shape=jax.ShapeDtypeStruct((2, rows, heads * HD), jnp.bfloat16),
    )(near, far, near_stat, far_stat)


def by_head(arrays, first, last):
    return jnp.stack(
        [
            jnp.concatenate([a[:, h * HD : (h + 1) * HD] for a in arrays], axis=1)
            for h in range(first, last)
        ]
    )


def gather_keys(own, after):
    if after is not None:
        own, _ = lax.optimization_barrier((own, after))
    half = own.shape[1] // 2
    up = shift(own, "z", 1)
    down = shift(own, "z", -1)
    up_two = shift(up[:, :half], "z", 1)
    down_two = shift(down[:, half:], "z", -1)
    mine = [own, up, down, up_two, down_two]
    return mine + [shift(piece, "core", 1) for piece in mine], up


def on_device(
    queries, keys, values, t_queries, t_keys, t_values, out_weight, stream, t_stream, gate, t_gate
):
    heads = queries.shape[1] // HD
    cut = (heads + 1) // 2
    near_q = by_head((queries, t_queries), 0, heads)
    far_q = shift(near_q, "x", 1)
    kv = (keys, t_keys, values, t_values)
    parts = []
    after = None
    for first, last in ((0, cut), (cut, heads)):
        pieces, after = gather_keys(by_head(kv, first, last), after)
        near, far, near_stat, far_stat = attend(near_q[first:last], far_q[first:last], pieces)
        far = shift(far, "x", 1)
        far_stat = shift(far_stat, "x", 1)
        parts.append(merge(near, far, near_stat, far_stat))
    both = jnp.concatenate(parts, axis=2)
    branch, t_branch = (
        lax.psum_scatter(
            jnp.dot(both[i], out_weight, preferred_element_type=jnp.float32).astype(jnp.bfloat16),
            "head",
            scatter_dimension=0,
            tiled=True,
        ).astype(jnp.float32)
        for i in range(2)
    )
    gate_wide = gate.astype(jnp.float32)
    result = stream.astype(jnp.float32) + gate_wide * branch
    t_result = (
        t_stream.astype(jnp.float32) + t_gate.astype(jnp.float32) * branch + gate_wide * t_branch
    )
    return (result.astype(jnp.bfloat16), t_result.astype(jnp.bfloat16))


def solution(mesh):
    return jax.shard_map(
        on_device,
        mesh=mesh,
        in_specs=(
            P(("dp", "blk"), "head"),
            P(("dp", "blk"), "head"),
            P(("dp", "blk"), "head"),
            P(("dp", "blk"), "head"),
            P(("dp", "blk"), "head"),
            P(("dp", "blk"), "head"),
            P("head", None),
            P(("dp", "blk", "head"), None),
            P(("dp", "blk", "head"), None),
            P(),
            P(),
        ),
        out_specs=(P(("dp", "blk", "head"), None), P(("dp", "blk", "head"), None)),
        check_vma=False,
    )
```

```python
import functools

import jax
import jax.numpy as jnp
from jax import lax
from jax.experimental import pallas as pl
from jax.experimental.pallas import tpu as pltpu
from jax.sharding import Mesh
from jax.sharding import PartitionSpec as P

HD = 128
LOG2E = 1.4426950408889634
SCALE = HD**-0.5
CHUNK = 512
SIZES = {"xl": 2, "z": 4, "core": 2, "head": 4}
WIDE = 512
FACTOR = 1.0


def shift(value, axis, step):
    size = SIZES[axis]
    return lax.ppermute(value, axis, [(i, (i + step) % size) for i in range(size)])


def swap_parts(value):
    return lax.ppermute(value, ("xl", "dp"), [(1, 2), (2, 1), (3, 0), (0, 3)])


def attend_kernel(sizes, rows, q_ref, *refs):
    pieces = refs[: len(sizes)]
    *outs, kk, vv, scores = refs[len(sizes) :]
    at = 0
    for size, piece in zip(sizes, pieces):
        kk[at : at + size, :] = piece[0, :, : 2 * HD]
        vv[at : at + size, :] = piece[0, :, 2 * HD :]
        at += size
    keys = at
    across = (((1,), (1,)), ((), ()))
    query = q_ref[0, :, :HD]
    mixed = jnp.concatenate([q_ref[0, :, HD:], query], axis=1)
    peak = None
    for c in range(0, keys, CHUNK):
        s = lax.dot_general(
            query, kk[c : c + CHUNK, :HD], across, preferred_element_type=jnp.float32
        )
        scores[:, c : c + CHUNK] = s
        for lane in range(0, CHUNK, 128):
            part = s[:, lane : lane + 128]
            peak = part if peak is None else jnp.maximum(peak, part)
    top = jnp.max(peak, axis=1, keepdims=True) * (SCALE * LOG2E)
    den = jnp.zeros((rows, 128), jnp.float32)
    mass = jnp.zeros((rows, 128), jnp.float32)
    wide = jnp.zeros((rows, 2 * HD), jnp.float32)
    tilt = jnp.zeros((rows, HD), jnp.float32)
    for c in range(0, keys, CHUNK):
        slope = lax.dot_general(
            mixed, kk[c : c + CHUNK, :], across, preferred_element_type=jnp.float32
        )
        w = jnp.exp2(scores[:, c : c + CHUNK] * (SCALE * LOG2E) - top)
        g = w * slope
        for lane in range(0, CHUNK, 128):
            den = den + w[:, lane : lane + 128]
            mass = mass + g[:, lane : lane + 128]
        wide = wide + jnp.dot(
            w.astype(jnp.bfloat16), vv[c : c + CHUNK, :], preferred_element_type=jnp.float32
        )
        tilt = tilt + jnp.dot(
            g.astype(jnp.bfloat16), vv[c : c + CHUNK, :HD], preferred_element_type=jnp.float32
        )
    den = jnp.sum(den, axis=1, keepdims=True)
    inverse = 1.0 / den
    mean = jnp.sum(mass, axis=1, keepdims=True) * (inverse * SCALE)
    out = wide[:, :HD] * inverse
    t_out = (tilt * SCALE + wide[:, HD:]) * inverse - mean * out
    outs[0][0, :rows, :HD] = out.astype(outs[0].dtype)
    outs[0][0, :rows, HD:] = t_out.astype(outs[0].dtype)
    lane = lax.broadcasted_iota(jnp.int32, (rows, 128), 1)
    stats = jnp.transpose(jnp.where(lane == 0, top + jnp.log2(den), mean))[:8, :]
    if len(outs) == 2:
        outs[1][0] = stats
    else:
        stats = stats[:2, :]
        high = stats.astype(jnp.bfloat16).astype(jnp.float32)
        middle = (stats - high).astype(jnp.bfloat16).astype(jnp.float32)
        low = stats - high - middle
        terms = jnp.concatenate([high, middle, low, jnp.zeros_like(low)], axis=0)
        over = 2 * HD
        rest = jnp.concatenate(
            [terms[:, over:], jnp.zeros((8, 2 * over - rows), jnp.float32)], axis=1
        )
        outs[0][0, rows:, :] = jnp.concatenate([terms[:, :over], rest], axis=0).astype(jnp.bfloat16)


def attend(q, first, last, pieces, sent):
    rows = q.shape[1]
    heads = last - first
    sizes = tuple(p.shape[1] for p in pieces)
    keys = sum(sizes)

    def spec(r, c, at=0):
        return pl.BlockSpec((1, r, c), lambda h: (h + at, 0, 0))

    return pl.pallas_call(
        functools.partial(attend_kernel, sizes, rows),
        grid=(heads,),
        in_specs=[spec(rows, 2 * HD, first)] + [spec(s, 4 * HD) for s in sizes],
        out_specs=[spec(rows + 16, 2 * HD)] if sent else [spec(rows, 2 * HD), spec(8, rows)],
        out_shape=[jax.ShapeDtypeStruct((heads, rows + 16, 2 * HD), jnp.bfloat16)]
        if sent
        else [
            jax.ShapeDtypeStruct((heads, rows, 2 * HD), jnp.float32),
            jax.ShapeDtypeStruct((heads, 8, rows), jnp.float32),
        ],
        scratch_shapes=[
            pltpu.VMEM((keys, 2 * HD), jnp.bfloat16),
            pltpu.VMEM((keys, 2 * HD), jnp.bfloat16),
            pltpu.VMEM((rows, keys), jnp.float32),
        ],
        compiler_params=pltpu.CompilerParams(vmem_limit_bytes=40 * 1024 * 1024),
        cost_estimate=pl.CostEstimate(
            flops=int(FACTOR * heads * rows * keys * HD * 12),
            bytes_accessed=1000,
            transcendentals=0,
        ),
    )(q, *pieces)


def merge_kernel(near_ref, near_stat, far_ref, out_ref, both):
    heads, count, _ = near_ref.shape
    for h in range(heads):
        a = jnp.transpose(near_stat[h])
        terms = far_ref[h, count:, :].astype(jnp.float32)
        b = jnp.transpose(jnp.concatenate([terms[:8], terms[8:]], axis=1))[:count]
        lse_a, mean_a = a[:, 0:1], a[:, 1:2]
        lse_b = b[:, 0:1] + b[:, 2:3] + b[:, 4:5]
        mean_b = b[:, 1:2] + b[:, 3:4] + b[:, 5:6]
        top = jnp.maximum(lse_a, lse_b)
        wa = jnp.exp2(lse_a - top)
        wb = jnp.exp2(lse_b - top)
        inverse = 1.0 / (wa + wb)
        wa = wa * inverse
        wb = wb * inverse
        mean = wa * mean_a + wb * mean_b
        near = near_ref[h]
        far = far_ref[h, :count, :].astype(jnp.float32)
        oa, ob = near[:, :HD], far[:, :HD]
        out = wa * oa + wb * ob
        t_out = (
            wa * near[:, HD:]
            + wb * far[:, HD:]
            + (wa * (mean_a - mean)) * oa
            + (wb * (mean_b - mean)) * ob
        )
        both[0, :, h * HD : (h + 1) * HD] = out.astype(both.dtype)
        both[1, :, h * HD : (h + 1) * HD] = t_out.astype(both.dtype)
    rows = out_ref.shape[2]
    for owner in range(4):
        out_ref[owner] = both[:, owner * rows : (owner + 1) * rows, :]


def merge(near, near_stat, far):
    heads, rows, _ = near.shape
    whole = pl.BlockSpec(memory_space=pltpu.VMEM)
    return pl.pallas_call(
        merge_kernel,
        in_specs=[whole] * 3,
        out_specs=whole,
        out_shape=jax.ShapeDtypeStruct((4, 2, rows // 4, heads * HD), jnp.bfloat16),
        scratch_shapes=[pltpu.VMEM((2, rows, heads * HD), jnp.bfloat16)],
        cost_estimate=pl.CostEstimate(flops=1000, bytes_accessed=1000, transcendentals=0),
    )(near, near_stat, far)


def by_head(arrays, first, last):
    return jnp.stack(
        [
            jnp.concatenate([a[:, h * HD : (h + 1) * HD] for a in arrays], axis=1)
            for h in range(first, last)
        ]
    )


def project_kernel(parts, place_ref, *refs):
    atts, refs = refs[:parts], refs[parts:]
    stream, t_stream, gate, t_gate, weight = refs[:5]
    own, lo, lo_, hi, hi_, fourth, fifth = refs[5:12]
    own2, lo2, lo2_, hi2, hi2_, fourth2, fifth2 = refs[12:19]
    lots = (own, (lo, lo_), (hi, hi_), fourth, fifth)
    lots += (own2, (lo2, lo2_), (hi2, hi2_), fourth2, fifth2)
    result, t_result, att, slots, sems = refs[19:]
    rows = stream.shape[0]
    depth = weight.shape[0]
    me, core = place_ref[0], place_ref[1]
    copies = []
    for slot in range(10):
        half, lot = divmod(slot, 5)
        base = lax.rem(core + half, 2) * (5 * WIDE)
        col = pl.multiple_of(base + place_ref[2 + lot] * WIDE, WIDE)
        pieces = [(weight.at[:, pl.ds(col, WIDE)], 0)]
        for step in range(1, 4):
            at = step * depth
            if lot in (1, 2):
                first, second = lots[slot]
                pieces.append((first.at[step - 1], at))
                pieces.append((second.at[step - 1], at + first.shape[1]))
            else:
                block = step - 1 if lot == 0 else lax.rem(me + step, 4)
                pieces.append((lots[slot].at[block], at))
        group = []
        for i, (source, at) in enumerate(pieces):
            copy = pltpu.make_async_copy(
                source, slots.at[slot, pl.ds(at, source.shape[0]), :], sems.at[slot, i]
            )
            copy.start()
            group.append(copy)
        copies.append((col, slot, group))
    for step in range(4):
        block = lax.rem(me + step, 4)
        at = step * depth
        for ref in atts:
            size = ref.shape[3]
            att[:rows, at : at + size] = ref[block, 0]
            att[rows:, at : at + size] = ref[block, 1]
            at += size
    for col, slot, group in copies:
        for copy in group:
            copy.wait()
        sums = jnp.dot(att[...], slots[slot], preferred_element_type=jnp.float32)
        branch, t_branch = sums[:rows], sums[rows:]
        cols = pl.ds(col, WIDE)
        g = gate[:, cols].astype(jnp.float32)
        tg = t_gate[:, cols].astype(jnp.float32)
        result[:, cols] = (stream[:, cols].astype(jnp.float32) + g * branch).astype(result.dtype)
        t_result[:, cols] = (
            t_stream[:, cols].astype(jnp.float32) + tg * branch + g * t_branch
        ).astype(t_result.dtype)


def project(place, atts, stream, t_stream, gate, t_gate, weight, lots):
    rows, columns = stream.shape
    depth = weight.shape[0]
    whole = pl.BlockSpec(memory_space=pltpu.VMEM)
    away = pl.BlockSpec(memory_space=pl.ANY)
    return pl.pallas_call(
        functools.partial(project_kernel, len(atts)),
        in_specs=[pl.BlockSpec(memory_space=pltpu.SMEM)]
        + [whole] * (len(atts) + 4)
        + [away] * (1 + len(lots)),
        out_specs=[whole] * 2,
        out_shape=[jax.ShapeDtypeStruct((rows, columns), stream.dtype)] * 2,
        scratch_shapes=[
            pltpu.VMEM((2 * rows, 4 * depth), jnp.bfloat16),
            pltpu.VMEM((10, 4 * depth, WIDE), jnp.bfloat16),
            pltpu.SemaphoreType.DMA((10, 7)),
        ],
        compiler_params=pltpu.CompilerParams(vmem_limit_bytes=48 * 1024 * 1024),
        cost_estimate=pl.CostEstimate(flops=1000, bytes_accessed=1000, transcendentals=0),
    )(place, *atts, stream, t_stream, gate, t_gate, weight, *lots)


def on_device(
    queries, keys, values, t_queries, t_keys, t_values, out_weight, stream, t_stream, gate, t_gate
):
    heads = queries.shape[1] // HD
    depth = out_weight.shape[0]
    half_width = out_weight.shape[1] // 2
    cut = (heads + 1) // 2
    core, side, me = lax.axis_index("core"), lax.axis_index("xl"), lax.axis_index("head")
    x = 2 * lax.axis_index("dp") + side
    places = [x, x ^ 1, 3 - x, 3 - (x ^ 1), 4]

    def lot(place):
        return lax.dynamic_slice(
            out_weight, (0, core * half_width + place * WIDE), (depth, WIDE)
        )

    def tie(value, *earlier):
        return lax.optimization_barrier((value, *earlier))[0]

    def with_core(pieces):
        return pieces + [shift(piece, "core", 1) for piece in pieces]

    kv = (keys, t_keys, values, t_values)
    first_kv = by_head(kv, 0, cut)
    rows = first_kv.shape[1]
    up, down = shift(first_kv, "z", 1), shift(first_kv, "z", -1)
    own_all = lax.all_gather(lot(places[0]), "head")
    near_q = by_head((queries, t_queries), 0, heads)
    far_q = shift(near_q, "xl", 1)
    fourth_all = lax.all_gather(tie(lot(places[3]), near_q), "head")
    second_kv = by_head(kv, cut, heads)
    fifth_all = lax.all_gather(tie(lot(places[4]), near_q, second_kv), "head")

    up_two, down_two = shift(up[:, : rows // 2], "z", 1), shift(down[:, rows // 2 :], "z", -1)
    second_out = tie(second_kv, up, down)
    next_up, next_down = shift(second_out, "z", 1), shift(second_out, "z", -1)

    own_all = tie(own_all, up, down)
    own = jnp.concatenate(
        [lax.dynamic_slice(own_all, ((me + step) % 4, 0, 0), (1, depth, WIDE)) for step in (1, 2, 3)]
    )
    middle = depth // 2
    lo, hi = shift(own[:, :middle], "xl", 1), swap_parts(own[:, :middle])
    lo_, hi_ = shift(own[:, middle:], "xl", 1), swap_parts(own[:, middle:])

    up_two, down_two = tie(up_two, own), tie(down_two, own)
    first_all = with_core([first_kv, up, down, up_two, down_two])
    next_up_two = shift(next_up[:, : rows // 2], "z", 1)
    next_down_two = shift(next_down[:, rows // 2 :], "z", -1)

    own2 = shift(own, "core", 1)
    (far_a,) = attend(tie(far_q, next_up, next_down, lo, hi, fourth_all), 0, cut, first_all, True)
    sent_a = shift(far_a, "xl", 1)
    next_up_two, next_down_two = tie(next_up_two, far_a), tie(next_down_two, far_a)
    near_a = attend(tie(near_q, next_up_two, next_down_two, own2), 0, cut, first_all, False)
    second_all = with_core([second_kv, next_up, next_down, next_up_two, next_down_two])
    (far_b,) = attend(tie(far_q, near_a[1], lo_, hi_), cut, heads, second_all, True)
    sent_b = shift(far_b, "xl", 1)
    fourth2 = shift(tie(fourth_all, near_a[1]), "core", 1)
    owners_a = merge(*near_a, sent_a)
    lo2, hi2 = shift(tie(lo, near_a[1]), "core", 1), shift(tie(hi, near_a[1]), "core", 1)
    near_b = attend(tie(near_q, owners_a, fourth2, lo2, hi2), cut, heads, second_all, False)
    owners_b = merge(*near_b, sent_b)
    atts = [lax.all_to_all(owners, "head", 0, 0) for owners in (owners_a, owners_b)]
    lo2_, hi2_ = shift(tie(lo_, near_b[1]), "core", 1), shift(tie(hi_, near_b[1]), "core", 1)
    fifth2 = shift(tie(fifth_all, owners_b), "core", 1)
    lots = [own, lo, lo_, hi, hi_, fourth_all, fifth_all]
    lots += [own2, lo2, lo2_, hi2, hi2_, fourth2, fifth2]
    place = jnp.stack([me, core, *places]).astype(jnp.int32)
    return project(
        place,
        atts,
        stream,
        t_stream,
        gate.reshape(1, -1),
        t_gate.reshape(1, -1),
        out_weight,
        lots,
    )


def solution(mesh):
    fine = Mesh(
        mesh.devices.reshape(SIZES["xl"], SIZES["z"], SIZES["core"], SIZES["head"], -1),
        ("xl", "z", "core", "head", "dp"),
    )
    tokens = ("dp", "xl", "z", "core")
    spread = P(tokens, "head")
    rows = P((*tokens, "head"), None)
    return jax.shard_map(
        on_device,
        mesh=fine,
        in_specs=(spread,) * 6 + (P("head", None), rows, rows, P(), P()),
        out_specs=(rows, rows),
        check_vma=False,
    )
```

```python
import functools

import jax
import jax.numpy as jnp
from jax import lax
from jax.experimental import pallas as pl
from jax.experimental.pallas import tpu as pltpu
from jax.sharding import Mesh
from jax.sharding import PartitionSpec as P

HD = 128
LOG2E = 1.4426950408889634
SCALE = HD**-0.5
CHUNK = 512
SIZES = {"xl": 2, "z": 4, "core": 2, "head": 4}
WIDE = 640
VMEM = 60 * 1024 * 1024


def shift(value, axis, step):
    size = SIZES[axis]
    return lax.ppermute(value, axis, [(i, (i + step) % size) for i in range(size)])


def swap_parts(value):
    return lax.ppermute(value, ("xl", "dp"), [(1, 2), (2, 1), (3, 0), (0, 3)])


def attend_kernel(rows, q_ref, kv, *refs):
    *outs, kk, vv, scores = refs
    blocks, _, size, _ = kv.shape
    keys = blocks * size
    for i in range(blocks):
        kk[i * size : (i + 1) * size, :] = kv[i, 0, :, : 2 * HD]
        vv[i * size : (i + 1) * size, :] = kv[i, 0, :, 2 * HD :]
    across = (((1,), (1,)), ((), ()))
    query = q_ref[0, :, :HD]
    mixed = jnp.concatenate([q_ref[0, :, HD:], query], axis=1)
    peak = None
    for c in range(0, keys, CHUNK):
        s = lax.dot_general(
            query, kk[c : c + CHUNK, :HD], across, preferred_element_type=jnp.float32
        )
        scores[:, c : c + CHUNK] = s
        for lane in range(0, CHUNK, 128):
            part = s[:, lane : lane + 128]
            peak = part if peak is None else jnp.maximum(peak, part)
    top = jnp.max(peak, axis=1, keepdims=True) * (SCALE * LOG2E)
    den = jnp.zeros((rows, 128), jnp.float32)
    mass = jnp.zeros((rows, 128), jnp.float32)
    wide = jnp.zeros((rows, 2 * HD), jnp.float32)
    tilt = jnp.zeros((rows, HD), jnp.float32)
    for c in range(0, keys, CHUNK):
        slope = lax.dot_general(
            mixed, kk[c : c + CHUNK, :], across, preferred_element_type=jnp.float32
        )
        w = jnp.exp2(scores[:, c : c + CHUNK] * (SCALE * LOG2E) - top)
        g = w * slope
        for lane in range(0, CHUNK, 128):
            den = den + w[:, lane : lane + 128]
            mass = mass + g[:, lane : lane + 128]
        wide = wide + jnp.dot(
            w.astype(jnp.bfloat16), vv[c : c + CHUNK, :], preferred_element_type=jnp.float32
        )
        tilt = tilt + jnp.dot(
            g.astype(jnp.bfloat16), vv[c : c + CHUNK, :HD], preferred_element_type=jnp.float32
        )
    den = jnp.sum(den, axis=1, keepdims=True)
    inverse = 1.0 / den
    mean = jnp.sum(mass, axis=1, keepdims=True) * (inverse * SCALE)
    out = wide[:, :HD] * inverse
    t_out = (tilt * SCALE + wide[:, HD:]) * inverse - mean * out
    outs[0][0, :rows, :HD] = out.astype(outs[0].dtype)
    outs[0][0, :rows, HD:] = t_out.astype(outs[0].dtype)
    lane = lax.broadcasted_iota(jnp.int32, (rows, 128), 1)
    stats = jnp.transpose(jnp.where(lane == 0, top + jnp.log2(den), mean))[:8, :]
    if len(outs) == 2:
        outs[1][0] = stats
    else:
        stats = stats[:2, :]
        high = stats.astype(jnp.bfloat16).astype(jnp.float32)
        middle = (stats - high).astype(jnp.bfloat16).astype(jnp.float32)
        low = stats - high - middle
        terms = jnp.concatenate([high, middle, low, jnp.zeros_like(low)], axis=0)
        over = 2 * HD
        rest = jnp.concatenate(
            [terms[:, over:], jnp.zeros((8, 2 * over - rows), jnp.float32)], axis=1
        )
        outs[0][0, rows:, :] = jnp.concatenate([terms[:, :over], rest], axis=0).astype(jnp.bfloat16)


def attend(q, first, last, kv, sent):
    rows = q.shape[1]
    heads = last - first
    blocks, _, size, _ = kv.shape
    keys = blocks * size

    def spec(r, c, at=0):
        return pl.BlockSpec((1, r, c), lambda h: (h + at, 0, 0))

    return pl.pallas_call(
        functools.partial(attend_kernel, rows),
        grid=(heads,),
        in_specs=[
            spec(rows, 2 * HD, first),
            pl.BlockSpec((blocks, 1, size, 4 * HD), lambda h: (0, h + first, 0, 0)),
        ],
        out_specs=[spec(rows + 16, 2 * HD)] if sent else [spec(rows, 2 * HD), spec(8, rows)],
        out_shape=[jax.ShapeDtypeStruct((heads, rows + 16, 2 * HD), jnp.bfloat16)]
        if sent
        else [
            jax.ShapeDtypeStruct((heads, rows, 2 * HD), jnp.float32),
            jax.ShapeDtypeStruct((heads, 8, rows), jnp.float32),
        ],
        scratch_shapes=[
            pltpu.VMEM((keys, 2 * HD), jnp.bfloat16),
            pltpu.VMEM((keys, 2 * HD), jnp.bfloat16),
            pltpu.VMEM((rows, keys), jnp.float32),
        ],
        compiler_params=pltpu.CompilerParams(vmem_limit_bytes=VMEM),
        cost_estimate=pl.CostEstimate(
            flops=heads * rows * keys * HD * 12, bytes_accessed=1000, transcendentals=0
        ),
    )(q, kv)


def merge_kernel(me_ref, near_ref, near_stat, far_ref, *refs):
    outs, both = refs[:4], refs[4]
    heads, count, _ = near_ref.shape
    for h in range(heads):
        a = jnp.transpose(near_stat[h])
        terms = far_ref[h, count:, :].astype(jnp.float32)
        b = jnp.transpose(jnp.concatenate([terms[:8], terms[8:]], axis=1))[:count]
        lse_a, mean_a = a[:, 0:1], a[:, 1:2]
        lse_b = b[:, 0:1] + b[:, 2:3] + b[:, 4:5]
        mean_b = b[:, 1:2] + b[:, 3:4] + b[:, 5:6]
        top = jnp.maximum(lse_a, lse_b)
        wa = jnp.exp2(lse_a - top)
        wb = jnp.exp2(lse_b - top)
        inverse = 1.0 / (wa + wb)
        wa = wa * inverse
        wb = wb * inverse
        mean = wa * mean_a + wb * mean_b
        near = near_ref[h]
        far = far_ref[h, :count, :].astype(jnp.float32)
        oa, ob = near[:, :HD], far[:, :HD]
        out = wa * oa + wb * ob
        t_out = (
            wa * near[:, HD:]
            + wb * far[:, HD:]
            + (wa * (mean_a - mean)) * oa
            + (wb * (mean_b - mean)) * ob
        )
        both[0, :, h * HD : (h + 1) * HD] = out.astype(both.dtype)
        both[1, :, h * HD : (h + 1) * HD] = t_out.astype(both.dtype)
    rows = outs[0].shape[1]
    for step in range(4):
        at = pl.multiple_of(lax.rem(me_ref[0] + step, 4) * rows, 16)
        outs[step][...] = both[:, pl.ds(at, rows), :]


def merge(me, near, near_stat, far):
    heads, rows, _ = near.shape
    whole = pl.BlockSpec(memory_space=pltpu.VMEM)
    return pl.pallas_call(
        merge_kernel,
        in_specs=[pl.BlockSpec(memory_space=pltpu.SMEM)] + [whole] * 3,
        out_specs=[whole] * 4,
        out_shape=[jax.ShapeDtypeStruct((2, rows // 4, heads * HD), jnp.bfloat16)] * 4,
        scratch_shapes=[pltpu.VMEM((2, rows, heads * HD), jnp.bfloat16)],
        compiler_params=pltpu.CompilerParams(vmem_limit_bytes=VMEM),
        cost_estimate=pl.CostEstimate(flops=1000, bytes_accessed=1000, transcendentals=0),
    )(me, near, near_stat, far)


def by_head(arrays, first, last):
    return jnp.stack(
        [
            jnp.concatenate([a[:, h * HD : (h + 1) * HD] for a in arrays], axis=1)
            for h in range(first, last)
        ]
    )


def project_kernel(parts, place_ref, *refs):
    atts, refs = refs[: 4 * parts], refs[4 * parts :]
    stream, t_stream, gate, t_gate, weight = refs[:5]
    pieces = refs[5:29]
    result, t_result, att, slots, sems = refs[29:]
    rows = stream.shape[0]
    depth = weight.shape[0]
    core = place_ref[0]

    def copy(slot, step, source):
        return pltpu.make_async_copy(
            source, slots.at[slot, pl.ds(step * depth, depth), :], sems.at[slot, step]
        )

    copies = []
    for slot in range(8):
        half, lot = divmod(slot, 4)
        below, above, far = (pieces[12 * half + 4 * i : 12 * half + 4 * i + 4] for i in range(3))
        col = pl.multiple_of((lax.rem(core + half, 2) * 4 + lot) * WIDE, WIDE)
        for step, source in enumerate((weight.at[:, pl.ds(col, WIDE)], below[lot], above[lot])):
            copy(slot, step, source).start()
        for i in range(4):

            @pl.when(place_ref[1 + i] == lot)
            def _():
                copy(slot, 3, far[i]).start()

        copies.append((slot, lot, col, far[0]))
    at = 0
    for ref in atts:
        size = ref.shape[2]
        att[:rows, at : at + size] = ref[0]
        att[rows:, at : at + size] = ref[1]
        at += size
    for slot, lot, col, like in copies:
        for step in range(4):
            copy(slot, step, like).wait()
        sums = jnp.dot(att[...], slots[slot], preferred_element_type=jnp.float32)
        branch, t_branch = sums[:rows], sums[rows:]
        cols = pl.ds(col, WIDE)
        g = gate[:, cols].astype(jnp.float32)
        tg = t_gate[:, cols].astype(jnp.float32)
        result[:, cols] = (stream[:, cols].astype(jnp.float32) + g * branch).astype(result.dtype)
        t_result[:, cols] = (
            t_stream[:, cols].astype(jnp.float32) + tg * branch + g * t_branch
        ).astype(t_result.dtype)


def project(place, atts, stream, t_stream, gate, t_gate, weight, pieces):
    rows, columns = stream.shape
    depth = weight.shape[0]
    whole = pl.BlockSpec(memory_space=pltpu.VMEM)
    away = pl.BlockSpec(memory_space=pl.ANY)
    return pl.pallas_call(
        functools.partial(project_kernel, len(atts) // 4),
        in_specs=[pl.BlockSpec(memory_space=pltpu.SMEM)]
        + [whole] * (len(atts) + 4)
        + [away] * (1 + len(pieces)),
        out_specs=[whole] * 2,
        out_shape=[jax.ShapeDtypeStruct((rows, columns), stream.dtype)] * 2,
        scratch_shapes=[
            pltpu.VMEM((2 * rows, 4 * depth), jnp.bfloat16),
            pltpu.VMEM((8, 4 * depth, WIDE), jnp.bfloat16),
            pltpu.SemaphoreType.DMA((8, 4)),
        ],
        compiler_params=pltpu.CompilerParams(vmem_limit_bytes=VMEM),
        cost_estimate=pl.CostEstimate(flops=1000, bytes_accessed=1000, transcendentals=0),
    )(place, *atts, stream, t_stream, gate, t_gate, weight, *pieces)


def on_device(
    queries, keys, values, t_queries, t_keys, t_values, out_weight, stream, t_stream, gate, t_gate
):
    heads = queries.shape[1] // HD
    depth = out_weight.shape[0]
    half_width = out_weight.shape[1] // 2
    cut = (heads + 1) // 2
    core, side, me = lax.axis_index("core"), lax.axis_index("xl"), lax.axis_index("head")
    x = 2 * lax.axis_index("dp") + side
    places = [x, x ^ 1, 3 - x, 3 - (x ^ 1)]

    def quarter(place):
        return lax.dynamic_slice(
            out_weight, (0, core * half_width + place * WIDE), (depth, WIDE)
        )

    def tie(value, *earlier):
        return lax.optimization_barrier((value, *earlier))[0]

    def neighbours(lot, *earlier):
        value = quarter(lot)
        if earlier:
            value = tie(value, *earlier)
        return shift(value, "head", 1), shift(value, "head", -1)

    def other_core(*pieces):
        return [shift(piece, "core", 1) for piece in pieces]

    kv = lax.all_gather(by_head((keys, t_keys, values, t_values), 0, heads), ("z", "core"))
    near_q = by_head((queries, t_queries), 0, heads)
    far_q = shift(near_q, "xl", 1)

    far0 = shift(quarter(places[0]), "head", 2)
    first = neighbours(0)
    second = neighbours(1, far0)
    far1, far2 = shift(far0, "xl", 1), swap_parts(far0)
    third = neighbours(2, *first)
    fourth = neighbours(3, *second)
    far3 = shift(far2, "xl", 1)

    (far_a,) = attend(tie(far_q, *first, *second, far1, far2), 0, cut, kv, True)
    sent_a = shift(far_a, "xl", 1)
    first2, second2 = other_core(*tie(first, far_a)), other_core(*tie(second, far_a))
    (far_b,) = attend(tie(far_q, *third, far_a), cut, heads, kv, True)
    sent_b = shift(far_b, "xl", 1)
    fars = other_core(*tie((far0, far1, far2), far_b))
    near_a = attend(tie(near_q, far3, far_b, *first2, *second2), 0, cut, kv, False)
    third2 = other_core(*tie(third, near_a[1]))
    fars += other_core(tie(far3, near_a[1]))
    where = me.astype(jnp.int32).reshape(1)
    owners_a = merge(where, *near_a, sent_a)
    near_b = attend(tie(near_q, owners_a[0], *fars[:3]), cut, heads, kv, False)
    fourth2 = other_core(*tie(fourth, near_b[1]))
    owners_b = merge(where, *near_b, sent_b)
    moved = [
        [owners[0]] + [shift(owners[step], "head", step) for step in (1, 2, 3)]
        for owners in (owners_a, owners_b)
    ]
    atts = [moved[part][step] for step in (0, 1, 3, 2) for part in range(2)]
    pieces = [lot[way] for way in range(2) for lot in (first, second, third, fourth)]
    pieces += [far0, far1, far2, far3]
    pieces += [lot[way] for way in range(2) for lot in (first2, second2, third2, fourth2)]
    pieces += fars
    place = jnp.stack([core, *places]).astype(jnp.int32)
    return project(
        place,
        atts,
        stream,
        t_stream,
        gate.reshape(1, -1),
        t_gate.reshape(1, -1),
        out_weight,
        pieces,
    )


def solution(mesh):
    fine = Mesh(
        mesh.devices.reshape(SIZES["xl"], SIZES["z"], SIZES["core"], SIZES["head"], -1),
        ("xl", "z", "core", "head", "dp"),
    )
    tokens = ("dp", "xl", "z", "core")
    spread = P(tokens, "head")
    rows = P((*tokens, "head"), None)
    return jax.shard_map(
        on_device,
        mesh=fine,
        in_specs=(spread,) * 6 + (P("head", None), rows, rows, P(), P()),
        out_specs=(rows, rows),
        check_vma=False,
    )
```

```python
import functools

import jax
import jax.numpy as jnp
from jax import lax
from jax.experimental import pallas as pl
from jax.experimental.pallas import tpu as pltpu
from jax.sharding import Mesh
from jax.sharding import PartitionSpec as P

HD = 128
LOG2E = 1.4426950408889634
SCALE = HD**-0.5
CHUNK = 512
SIZES = {"xl": 2, "z": 4, "core": 2, "head": 4}
WIDE = 640
VMEM = 60 * 1024 * 1024


def shift(value, axis, step):
    size = SIZES[axis]
    return lax.ppermute(value, axis, [(i, (i + step) % size) for i in range(size)])


def swap_parts(value):
    return lax.ppermute(value, ("xl", "dp"), [(1, 2), (2, 1), (3, 0), (0, 3)])


def attend_kernel(rows, q_ref, kv, *refs):
    *outs, kk, vv, scores = refs
    blocks, _, size, _ = kv.shape
    keys = blocks * size
    for i in range(blocks):
        kk[i * size : (i + 1) * size, :] = kv[i, 0, :, : 2 * HD]
        vv[i * size : (i + 1) * size, :] = kv[i, 0, :, 2 * HD :]
    across = (((1,), (1,)), ((), ()))
    query = q_ref[0, :, :HD]
    mixed = jnp.concatenate([q_ref[0, :, HD:], query], axis=1)
    peak = None
    for c in range(0, keys, CHUNK):
        s = lax.dot_general(
            query, kk[c : c + CHUNK, :HD], across, preferred_element_type=jnp.float32
        )
        scores[:, c : c + CHUNK] = s
        for lane in range(0, CHUNK, 128):
            part = s[:, lane : lane + 128]
            peak = part if peak is None else jnp.maximum(peak, part)
    top = jnp.max(peak, axis=1, keepdims=True) * (SCALE * LOG2E)
    den = jnp.zeros((rows, 128), jnp.float32)
    mass = jnp.zeros((rows, 128), jnp.float32)
    wide = jnp.zeros((rows, 2 * HD), jnp.float32)
    tilt = jnp.zeros((rows, HD), jnp.float32)
    for c in range(0, keys, CHUNK):
        slope = lax.dot_general(
            mixed, kk[c : c + CHUNK, :], across, preferred_element_type=jnp.float32
        )
        w = jnp.exp2(scores[:, c : c + CHUNK] * (SCALE * LOG2E) - top)
        g = w * slope
        for lane in range(0, CHUNK, 128):
            den = den + w[:, lane : lane + 128]
            mass = mass + g[:, lane : lane + 128]
        wide = wide + jnp.dot(
            w.astype(jnp.bfloat16), vv[c : c + CHUNK, :], preferred_element_type=jnp.float32
        )
        tilt = tilt + jnp.dot(
            g.astype(jnp.bfloat16), vv[c : c + CHUNK, :HD], preferred_element_type=jnp.float32
        )
    den = jnp.sum(den, axis=1, keepdims=True)
    inverse = 1.0 / den
    mean = jnp.sum(mass, axis=1, keepdims=True) * (inverse * SCALE)
    out = wide[:, :HD] * inverse
    t_out = (tilt * SCALE + wide[:, HD:]) * inverse - mean * out
    outs[0][0, :rows, :HD] = out.astype(outs[0].dtype)
    outs[0][0, :rows, HD:] = t_out.astype(outs[0].dtype)
    lane = lax.broadcasted_iota(jnp.int32, (rows, 128), 1)
    stats = jnp.transpose(jnp.where(lane == 0, top + jnp.log2(den), mean))[:8, :]
    if len(outs) == 2:
        outs[1][0] = stats
    else:
        stats = stats[:2, :]
        high = stats.astype(jnp.bfloat16).astype(jnp.float32)
        middle = (stats - high).astype(jnp.bfloat16).astype(jnp.float32)
        low = stats - high - middle
        terms = jnp.concatenate([high, middle, low, jnp.zeros_like(low)], axis=0)
        over = 2 * HD
        rest = jnp.concatenate(
            [terms[:, over:], jnp.zeros((8, 2 * over - rows), jnp.float32)], axis=1
        )
        outs[0][0, rows:, :] = jnp.concatenate([terms[:, :over], rest], axis=0).astype(jnp.bfloat16)


def attend(q, first, kv, sent):
    rows = q.shape[1]
    blocks, heads, size, _ = kv.shape
    keys = blocks * size

    def spec(r, c, at=0):
        return pl.BlockSpec((1, r, c), lambda h: (h + at, 0, 0))

    return pl.pallas_call(
        functools.partial(attend_kernel, rows),
        grid=(heads,),
        in_specs=[
            spec(rows, 2 * HD, first),
            pl.BlockSpec((blocks, 1, size, 4 * HD), lambda h: (0, h, 0, 0)),
        ],
        out_specs=[spec(rows + 16, 2 * HD)] if sent else [spec(rows, 2 * HD), spec(8, rows)],
        out_shape=[jax.ShapeDtypeStruct((heads, rows + 16, 2 * HD), jnp.bfloat16)]
        if sent
        else [
            jax.ShapeDtypeStruct((heads, rows, 2 * HD), jnp.float32),
            jax.ShapeDtypeStruct((heads, 8, rows), jnp.float32),
        ],
        scratch_shapes=[
            pltpu.VMEM((keys, 2 * HD), jnp.bfloat16),
            pltpu.VMEM((keys, 2 * HD), jnp.bfloat16),
            pltpu.VMEM((rows, keys), jnp.float32),
        ],
        compiler_params=pltpu.CompilerParams(vmem_limit_bytes=VMEM),
        cost_estimate=pl.CostEstimate(
            flops=heads * rows * keys * HD * 12, bytes_accessed=1000, transcendentals=0
        ),
    )(q, kv)


def merge_kernel(me_ref, near_ref, near_stat, far_ref, *refs):
    outs, both = refs[:4], refs[4]
    heads, count, _ = near_ref.shape
    for h in range(heads):
        lse_a, mean_a = near_stat[h, 0:1, :], near_stat[h, 1:2, :]
        terms = far_ref[h, count:, :].astype(jnp.float32)
        terms = jnp.concatenate([terms[:8], terms[8:, : count - 2 * HD]], axis=1)
        lse_b = terms[0:1] + terms[2:3] + terms[4:5]
        mean_b = terms[1:2] + terms[3:4] + terms[5:6]
        top = jnp.maximum(lse_a, lse_b)
        wa = jnp.exp2(lse_a - top)
        wb = jnp.exp2(lse_b - top)
        inverse = 1.0 / (wa + wb)
        wa = wa * inverse
        wb = wb * inverse
        mean = wa * mean_a + wb * mean_b
        terms = [wa, wb, wa * (mean_a - mean), wb * (mean_b - mean)]
        terms = jnp.transpose(jnp.concatenate(terms + terms, axis=0))
        wa, wb, da, db = (terms[:, i : i + 1] for i in range(4))
        near = near_ref[h]
        far = far_ref[h, :count, :].astype(jnp.float32)
        oa, ob = near[:, :HD], far[:, :HD]
        out = wa * oa + wb * ob
        t_out = wa * near[:, HD:] + wb * far[:, HD:] + da * oa + db * ob
        both[0, :, h * HD : (h + 1) * HD] = out.astype(both.dtype)
        both[1, :, h * HD : (h + 1) * HD] = t_out.astype(both.dtype)
    rows = outs[0].shape[1]
    for step in range(4):
        at = pl.multiple_of(lax.rem(me_ref[0] + step, 4) * rows, 16)
        outs[step][...] = both[:, pl.ds(at, rows), :]


def merge(me, near, near_stat, far):
    heads, rows, _ = near.shape
    whole = pl.BlockSpec(memory_space=pltpu.VMEM)
    return pl.pallas_call(
        merge_kernel,
        in_specs=[pl.BlockSpec(memory_space=pltpu.SMEM)] + [whole] * 3,
        out_specs=[whole] * 4,
        out_shape=[jax.ShapeDtypeStruct((2, rows // 4, heads * HD), jnp.bfloat16)] * 4,
        scratch_shapes=[pltpu.VMEM((2, rows, heads * HD), jnp.bfloat16)],
        compiler_params=pltpu.CompilerParams(vmem_limit_bytes=VMEM),
        cost_estimate=pl.CostEstimate(flops=1000, bytes_accessed=1000, transcendentals=0),
    )(me, near, near_stat, far)


def by_head(arrays, first, last):
    return jnp.stack(
        [
            jnp.concatenate([a[:, h * HD : (h + 1) * HD] for a in arrays], axis=1)
            for h in range(first, last)
        ]
    )


def project_kernel(parts, place_ref, *refs):
    atts, refs = refs[: 4 * parts], refs[4 * parts :]
    stream, t_stream, gate, t_gate, weight = refs[:5]
    pieces = refs[5:29]
    result, t_result, att, slots, sems = refs[29:]
    rows = stream.shape[0]
    depth = weight.shape[0]
    core = place_ref[0]

    def copy(slot, step, source):
        return pltpu.make_async_copy(
            source, slots.at[slot, pl.ds(step * depth, depth), :], sems.at[slot, step]
        )

    copies = []
    for slot in range(8):
        half, lot = divmod(slot, 4)
        below, above, far = (pieces[12 * half + 4 * i : 12 * half + 4 * i + 4] for i in range(3))
        col = pl.multiple_of((lax.rem(core + half, 2) * 4 + lot) * WIDE, WIDE)
        for step, source in enumerate((weight.at[:, pl.ds(col, WIDE)], below[lot], above[lot])):
            copy(slot, step, source).start()
        for i in range(4):

            @pl.when(place_ref[1 + i] == lot)
            def _():
                copy(slot, 3, far[i]).start()

        copies.append((slot, lot, col, far[0]))
    at = 0
    for ref in atts:
        size = ref.shape[2]
        att[:rows, at : at + size] = ref[0]
        att[rows:, at : at + size] = ref[1]
        at += size
    for slot, lot, col, like in copies:
        for step in range(4):
            copy(slot, step, like).wait()
        sums = jnp.dot(att[...], slots[slot], preferred_element_type=jnp.float32)
        branch, t_branch = sums[:rows], sums[rows:]
        cols = pl.ds(col, WIDE)
        g = gate[:, cols].astype(jnp.float32)
        tg = t_gate[:, cols].astype(jnp.float32)
        result[:, cols] = (stream[:, cols].astype(jnp.float32) + g * branch).astype(result.dtype)
        t_result[:, cols] = (
            t_stream[:, cols].astype(jnp.float32) + tg * branch + g * t_branch
        ).astype(t_result.dtype)


def project(place, atts, stream, t_stream, gate, t_gate, weight, pieces):
    rows, columns = stream.shape
    depth = weight.shape[0]
    whole = pl.BlockSpec(memory_space=pltpu.VMEM)
    away = pl.BlockSpec(memory_space=pl.ANY)
    return pl.pallas_call(
        functools.partial(project_kernel, len(atts) // 4),
        in_specs=[pl.BlockSpec(memory_space=pltpu.SMEM)]
        + [whole] * (len(atts) + 4)
        + [away] * (1 + len(pieces)),
        out_specs=[whole] * 2,
        out_shape=[jax.ShapeDtypeStruct((rows, columns), stream.dtype)] * 2,
        scratch_shapes=[
            pltpu.VMEM((2 * rows, 4 * depth), jnp.bfloat16),
            pltpu.VMEM((8, 4 * depth, WIDE), jnp.bfloat16),
            pltpu.SemaphoreType.DMA((8, 4)),
        ],
        compiler_params=pltpu.CompilerParams(vmem_limit_bytes=VMEM),
        cost_estimate=pl.CostEstimate(flops=1000, bytes_accessed=1000, transcendentals=0),
    )(place, *atts, stream, t_stream, gate, t_gate, weight, *pieces)


def on_device(
    queries, keys, values, t_queries, t_keys, t_values, out_weight, stream, t_stream, gate, t_gate
):
    heads = queries.shape[1] // HD
    depth = out_weight.shape[0]
    half_width = out_weight.shape[1] // 2
    cut = (heads + 1) // 2
    core, side, me = lax.axis_index("core"), lax.axis_index("xl"), lax.axis_index("head")
    x = 2 * lax.axis_index("dp") + side
    places = [x, x ^ 1, 3 - x, 3 - (x ^ 1)]

    def quarter(place):
        return lax.dynamic_slice(
            out_weight, (0, core * half_width + place * WIDE), (depth, WIDE)
        )

    def tie(value, *earlier):
        return lax.optimization_barrier((value, *earlier))[0]

    def neighbours(lot, *earlier):
        value = quarter(lot)
        if earlier:
            value = tie(value, *earlier)
        return shift(value, "head", 1), shift(value, "head", -1)

    def other_core(*pieces):
        return [shift(piece, "core", 1) for piece in pieces]

    def to_owners(parts):
        return [parts[0]] + [shift(parts[step], "head", step) for step in (1, 2, 3)]

    kv = (keys, t_keys, values, t_values)
    kv_a = lax.all_gather(by_head(kv, 0, cut), ("z", "core"))
    kv_b = lax.all_gather(by_head(kv, cut, heads), ("z", "core"))
    near_q = by_head((queries, t_queries), 0, heads)
    far_q = shift(near_q, "xl", 1)
    gates = gate.reshape(1, -1), t_gate.reshape(1, -1)
    place = jnp.stack([core, *places]).astype(jnp.int32)
    where = me.astype(jnp.int32).reshape(1)

    far0 = shift(quarter(places[0]), "head", 2)
    first = neighbours(0)
    second = neighbours(1, far0)
    far1, far2 = shift(far0, "xl", 1), swap_parts(far0)

    (far_a,) = attend(tie(far_q, *first, *gates, place, where), 0, kv_a, True)
    sent_a = shift(far_a, "xl", 1)
    near_a = attend(tie(near_q, far_a), 0, kv_a, False)
    third = neighbours(2, near_a[1])
    far3 = shift(tie(far2, near_a[1]), "xl", 1)
    first2, fars = other_core(*tie(first, near_a[1])), other_core(tie(far0, near_a[1]))
    owners_a = merge(tie(where, *second, far1, far2), *near_a, sent_a)
    second2 = other_core(*tie(second, owners_a[0]))
    fars += other_core(*tie((far1, far2), owners_a[0]))
    (far_b,) = attend(tie(far_q, *third, *first2, fars[0], owners_a[0]), cut, kv_b, True)
    fourth = neighbours(3, *third)
    sent_b = shift(far_b, "xl", 1)
    third2 = other_core(*tie(third, far_b))
    moved_a = to_owners(tie(owners_a, *third))
    near_b = attend(
        tie(near_q, *second2, *fars[1:], far3, far_b, *moved_a), cut, kv_b, False
    )
    fars += other_core(tie(far3, near_b[1]))
    owners_b = merge(tie(where, *third2), *near_b, sent_b)
    moved_b = to_owners(owners_b)
    fourth2 = other_core(*tie(fourth, *moved_b[1:]))
    moved = [moved_a, moved_b]
    atts = [moved[part][step] for step in (0, 1, 3, 2) for part in range(2)]
    pieces = [lot[way] for way in range(2) for lot in (first, second, third, fourth)]
    pieces += [far0, far1, far2, far3]
    twins = (first2, second2, third2, fourth2)
    pieces += [lot[way] for way in range(2) for lot in twins]
    pieces += fars
    return project(place, atts, stream, t_stream, *gates, out_weight, pieces)


def solution(mesh):
    fine = Mesh(
        mesh.devices.reshape(SIZES["xl"], SIZES["z"], SIZES["core"], SIZES["head"], -1),
        ("xl", "z", "core", "head", "dp"),
    )
    tokens = ("dp", "xl", "z", "core")
    spread = P(tokens, "head")
    rows = P((*tokens, "head"), None)
    return jax.shard_map(
        on_device,
        mesh=fine,
        in_specs=(spread,) * 6 + (P("head", None), rows, rows, P(), P()),
        out_specs=(rows, rows),
        check_vma=False,
    )
```

```python
import functools

import jax
import jax.numpy as jnp
from jax import lax
from jax.experimental import pallas as pl
from jax.experimental.pallas import tpu as pltpu
from jax.sharding import Mesh
from jax.sharding import PartitionSpec as P

HD = 128
LOG2E = 1.4426950408889634
SCALE = HD**-0.5
CHUNK = 512
SIZES = {"xl": 2, "z": 4, "core": 2, "head": 4}
WIDE = 640
VMEM = 60 * 1024 * 1024


def shift(value, axis, step):
    size = SIZES[axis]
    return lax.ppermute(value, axis, [(i, (i + step) % size) for i in range(size)])


def swap_parts(value):
    return lax.ppermute(value, ("xl", "dp"), [(1, 2), (2, 1), (3, 0), (0, 3)])


def attend_kernel(rows, q_ref, kv, *refs):
    *outs, kk, vv, scores = refs
    blocks, _, size, _ = kv.shape
    keys = blocks * size
    for i in range(blocks):
        kk[i * size : (i + 1) * size, :] = kv[i, 0, :, : 2 * HD]
        vv[i * size : (i + 1) * size, :] = kv[i, 0, :, 2 * HD :]
    across = (((1,), (1,)), ((), ()))
    query = q_ref[0, :, :HD]
    mixed = jnp.concatenate([q_ref[0, :, HD:], query], axis=1)
    peak = None
    for c in range(0, keys, CHUNK):
        s = lax.dot_general(
            query, kk[c : c + CHUNK, :HD], across, preferred_element_type=jnp.float32
        )
        scores[:, c : c + CHUNK] = s
        for lane in range(0, CHUNK, 128):
            part = s[:, lane : lane + 128]
            peak = part if peak is None else jnp.maximum(peak, part)
    top = jnp.max(peak, axis=1, keepdims=True) * (SCALE * LOG2E)
    den = jnp.zeros((rows, 128), jnp.float32)
    mass = jnp.zeros((rows, 128), jnp.float32)
    wide = jnp.zeros((rows, 2 * HD), jnp.float32)
    tilt = jnp.zeros((rows, HD), jnp.float32)
    for c in range(0, keys, CHUNK):
        slope = lax.dot_general(
            mixed, kk[c : c + CHUNK, :], across, preferred_element_type=jnp.float32
        )
        w = jnp.exp2(scores[:, c : c + CHUNK] * (SCALE * LOG2E) - top)
        g = w * slope
        for lane in range(0, CHUNK, 128):
            den = den + w[:, lane : lane + 128]
            mass = mass + g[:, lane : lane + 128]
        wide = wide + jnp.dot(
            w.astype(jnp.bfloat16), vv[c : c + CHUNK, :], preferred_element_type=jnp.float32
        )
        tilt = tilt + jnp.dot(
            g.astype(jnp.bfloat16), vv[c : c + CHUNK, :HD], preferred_element_type=jnp.float32
        )
    den = jnp.sum(den, axis=1, keepdims=True)
    inverse = 1.0 / den
    mean = jnp.sum(mass, axis=1, keepdims=True) * (inverse * SCALE)
    out = wide[:, :HD] * inverse
    t_out = (tilt * SCALE + wide[:, HD:]) * inverse - mean * out
    outs[0][0, :rows, :HD] = out.astype(outs[0].dtype)
    outs[0][0, :rows, HD:] = t_out.astype(outs[0].dtype)
    lane = lax.broadcasted_iota(jnp.int32, (rows, 128), 1)
    stats = jnp.transpose(jnp.where(lane == 0, top + jnp.log2(den), mean))[:8, :]
    if len(outs) == 2:
        outs[1][0] = stats
    else:
        stats = stats[:2, :]
        high = stats.astype(jnp.bfloat16).astype(jnp.float32)
        middle = (stats - high).astype(jnp.bfloat16).astype(jnp.float32)
        low = stats - high - middle
        terms = jnp.concatenate([high, middle, low, jnp.zeros_like(low)], axis=0)
        over = 2 * HD
        rest = jnp.concatenate(
            [terms[:, over:], jnp.zeros((8, 2 * over - rows), jnp.float32)], axis=1
        )
        outs[0][0, rows:, :] = jnp.concatenate([terms[:, :over], rest], axis=0).astype(jnp.bfloat16)


def attend(q, first, kv, sent):
    rows = q.shape[1]
    blocks, heads, size, _ = kv.shape
    keys = blocks * size

    def spec(r, c, at=0):
        return pl.BlockSpec((1, r, c), lambda h: (h + at, 0, 0))

    return pl.pallas_call(
        functools.partial(attend_kernel, rows),
        grid=(heads,),
        in_specs=[
            spec(rows, 2 * HD, first),
            pl.BlockSpec((blocks, 1, size, 4 * HD), lambda h: (0, h, 0, 0)),
        ],
        out_specs=[spec(rows + 16, 2 * HD)] if sent else [spec(rows, 2 * HD), spec(8, rows)],
        out_shape=[jax.ShapeDtypeStruct((heads, rows + 16, 2 * HD), jnp.bfloat16)]
        if sent
        else [
            jax.ShapeDtypeStruct((heads, rows, 2 * HD), jnp.float32),
            jax.ShapeDtypeStruct((heads, 8, rows), jnp.float32),
        ],
        scratch_shapes=[
            pltpu.VMEM((keys, 2 * HD), jnp.bfloat16),
            pltpu.VMEM((keys, 2 * HD), jnp.bfloat16),
            pltpu.VMEM((rows, keys), jnp.float32),
        ],
        compiler_params=pltpu.CompilerParams(vmem_limit_bytes=VMEM),
        cost_estimate=pl.CostEstimate(
            flops=heads * rows * keys * HD * 12, bytes_accessed=1000, transcendentals=0
        ),
    )(q, kv)


def merge_kernel(me_ref, near_ref, near_stat, far_ref, *refs):
    outs, both = refs[:4], refs[4]
    heads, count, _ = near_ref.shape
    for h in range(heads):
        lse_a, mean_a = near_stat[h, 0:1, :], near_stat[h, 1:2, :]
        terms = far_ref[h, count:, :].astype(jnp.float32)
        terms = jnp.concatenate([terms[:8], terms[8:, : count - 2 * HD]], axis=1)
        lse_b = terms[0:1] + terms[2:3] + terms[4:5]
        mean_b = terms[1:2] + terms[3:4] + terms[5:6]
        top = jnp.maximum(lse_a, lse_b)
        wa = jnp.exp2(lse_a - top)
        wb = jnp.exp2(lse_b - top)
        inverse = 1.0 / (wa + wb)
        wa = wa * inverse
        wb = wb * inverse
        mean = wa * mean_a + wb * mean_b
        terms = [wa, wb, wa * (mean_a - mean), wb * (mean_b - mean)]
        terms = jnp.transpose(jnp.concatenate(terms + terms, axis=0))
        wa, wb, da, db = (terms[:, i : i + 1] for i in range(4))
        near = near_ref[h]
        far = far_ref[h, :count, :].astype(jnp.float32)
        oa, ob = near[:, :HD], far[:, :HD]
        out = wa * oa + wb * ob
        t_out = wa * near[:, HD:] + wb * far[:, HD:] + da * oa + db * ob
        both[0, :, h * HD : (h + 1) * HD] = out.astype(both.dtype)
        both[1, :, h * HD : (h + 1) * HD] = t_out.astype(both.dtype)
    rows = outs[0].shape[1]
    for step in range(4):
        at = pl.multiple_of(lax.rem(me_ref[0] + step, 4) * rows, 16)
        outs[step][...] = both[:, pl.ds(at, rows), :]


def merge(me, near, near_stat, far):
    heads, rows, _ = near.shape
    whole = pl.BlockSpec(memory_space=pltpu.VMEM)
    return pl.pallas_call(
        merge_kernel,
        in_specs=[pl.BlockSpec(memory_space=pltpu.SMEM)] + [whole] * 3,
        out_specs=[whole] * 4,
        out_shape=[jax.ShapeDtypeStruct((2, rows // 4, heads * HD), jnp.bfloat16)] * 4,
        scratch_shapes=[pltpu.VMEM((2, rows, heads * HD), jnp.bfloat16)],
        compiler_params=pltpu.CompilerParams(vmem_limit_bytes=VMEM),
        cost_estimate=pl.CostEstimate(flops=1000, bytes_accessed=1000, transcendentals=0),
    )(me, near, near_stat, far)


def pack_kernel(cut, q, t_q, k, t_k, v, t_v, first_ref, second_ref, q_ref):
    heads = q.shape[1] // HD
    for h in range(heads):
        cols = slice(h * HD, (h + 1) * HD)
        out, at = (first_ref, h) if h < cut else (second_ref, h - cut)
        for i, ref in enumerate((k, t_k, v, t_v)):
            out[at, :, i * HD : (i + 1) * HD] = ref[:, cols]
        q_ref[h, :, :HD] = q[:, cols]
        q_ref[h, :, HD:] = t_q[:, cols]


def pack(cut, *arrays):
    rows, width = arrays[0].shape
    heads = width // HD
    whole = pl.BlockSpec(memory_space=pltpu.VMEM)
    return pl.pallas_call(
        functools.partial(pack_kernel, cut),
        in_specs=[whole] * 6,
        out_specs=[whole] * 3,
        out_shape=[
            jax.ShapeDtypeStruct((cut, rows, 4 * HD), jnp.bfloat16),
            jax.ShapeDtypeStruct((heads - cut, rows, 4 * HD), jnp.bfloat16),
            jax.ShapeDtypeStruct((heads, rows, 2 * HD), jnp.bfloat16),
        ],
        compiler_params=pltpu.CompilerParams(vmem_limit_bytes=VMEM),
        cost_estimate=pl.CostEstimate(flops=1000, bytes_accessed=1000, transcendentals=0),
    )(*arrays)


def project_kernel(parts, place_ref, *refs):
    atts, refs = refs[: 4 * parts], refs[4 * parts :]
    stream, t_stream, gate, t_gate, weight = refs[:5]
    pieces = refs[5:29]
    result, t_result, att, slots, sems = refs[29:]
    rows = stream.shape[0]
    depth = weight.shape[0]
    core = place_ref[0]

    def copy(slot, step, source):
        return pltpu.make_async_copy(
            source, slots.at[slot, pl.ds(step * depth, depth), :], sems.at[slot, step]
        )

    copies = []
    for slot in range(8):
        half, lot = divmod(slot, 4)
        below, above, far = (pieces[12 * half + 4 * i : 12 * half + 4 * i + 4] for i in range(3))
        col = pl.multiple_of((lax.rem(core + half, 2) * 4 + lot) * WIDE, WIDE)
        for step, source in enumerate((weight.at[:, pl.ds(col, WIDE)], below[lot], above[lot])):
            copy(slot, step, source).start()
        for i in range(4):

            @pl.when(place_ref[1 + i] == lot)
            def _():
                copy(slot, 3, far[i]).start()

        copies.append((slot, lot, col, far[0]))
    at = 0
    for ref in atts:
        size = ref.shape[2]
        att[:rows, at : at + size] = ref[0]
        att[rows:, at : at + size] = ref[1]
        at += size
    for slot, lot, col, like in copies:
        for step in range(4):
            copy(slot, step, like).wait()
        sums = jnp.dot(att[...], slots[slot], preferred_element_type=jnp.float32)
        branch, t_branch = sums[:rows], sums[rows:]
        cols = pl.ds(col, WIDE)
        g = gate[:, cols].astype(jnp.float32)
        tg = t_gate[:, cols].astype(jnp.float32)
        result[:, cols] = (stream[:, cols].astype(jnp.float32) + g * branch).astype(result.dtype)
        t_result[:, cols] = (
            t_stream[:, cols].astype(jnp.float32) + tg * branch + g * t_branch
        ).astype(t_result.dtype)


def project(place, atts, stream, t_stream, gate, t_gate, weight, pieces):
    rows, columns = stream.shape
    depth = weight.shape[0]
    whole = pl.BlockSpec(memory_space=pltpu.VMEM)
    away = pl.BlockSpec(memory_space=pl.ANY)
    return pl.pallas_call(
        functools.partial(project_kernel, len(atts) // 4),
        in_specs=[pl.BlockSpec(memory_space=pltpu.SMEM)]
        + [whole] * (len(atts) + 4)
        + [away] * (1 + len(pieces)),
        out_specs=[whole] * 2,
        out_shape=[jax.ShapeDtypeStruct((rows, columns), stream.dtype)] * 2,
        scratch_shapes=[
            pltpu.VMEM((2 * rows, 4 * depth), jnp.bfloat16),
            pltpu.VMEM((8, 4 * depth, WIDE), jnp.bfloat16),
            pltpu.SemaphoreType.DMA((8, 4)),
        ],
        compiler_params=pltpu.CompilerParams(vmem_limit_bytes=VMEM),
        cost_estimate=pl.CostEstimate(flops=1000, bytes_accessed=1000, transcendentals=0),
    )(place, *atts, stream, t_stream, gate, t_gate, weight, *pieces)


def on_device(
    queries, keys, values, t_queries, t_keys, t_values, out_weight, stream, t_stream, gate, t_gate
):
    heads = queries.shape[1] // HD
    depth = out_weight.shape[0]
    half_width = out_weight.shape[1] // 2
    cut = (heads + 1) // 2
    core, side, me = lax.axis_index("core"), lax.axis_index("xl"), lax.axis_index("head")
    x = 2 * lax.axis_index("dp") + side
    places = [x, x ^ 1, 3 - x, 3 - (x ^ 1)]

    def quarter(place):
        return lax.dynamic_slice(
            out_weight, (0, core * half_width + place * WIDE), (depth, WIDE)
        )

    def tie(value, *earlier):
        return lax.optimization_barrier((value, *earlier))[0]

    def neighbours(lot, *earlier):
        value = quarter(lot)
        if earlier:
            value = tie(value, *earlier)
        return shift(value, "head", 1), shift(value, "head", -1)

    def other_core(*pieces):
        return [shift(piece, "core", 1) for piece in pieces]

    def to_owners(parts):
        return [parts[0]] + [shift(parts[step], "head", step) for step in (1, 2, 3)]

    lot_a, lot_b, near_q = pack(cut, queries, t_queries, keys, t_keys, values, t_values)
    kv_a = lax.all_gather(lot_a, ("z", "core"))
    kv_b = lax.all_gather(lot_b, ("z", "core"))
    far_q = shift(near_q, "xl", 1)
    gates = gate.reshape(1, -1), t_gate.reshape(1, -1)
    place = jnp.stack([core, *places]).astype(jnp.int32)
    where = me.astype(jnp.int32).reshape(1)

    far0 = shift(quarter(places[0]), "head", 2)
    first = neighbours(0)
    second = neighbours(1, far0)
    far1, far2 = shift(far0, "xl", 1), swap_parts(far0)

    (far_a,) = attend(tie(far_q, *first, *gates, place, where), 0, kv_a, True)
    sent_a = shift(far_a, "xl", 1)
    third = neighbours(2, *second)
    far3 = swap_parts(far1)
    near_a = attend(tie(near_q, far_a, *second, far1, far2), 0, kv_a, False)
    first2, fars = other_core(*tie(first, near_a[1])), other_core(tie(far0, near_a[1]))
    owners_a = merge(where, *near_a, sent_a)
    second2 = other_core(*tie(second, owners_a[0]))
    fars += other_core(*tie((far1, far2), owners_a[0]))
    (far_b,) = attend(
        tie(far_q, *third, *first2, fars[0], owners_a[0]), cut, kv_b, True
    )
    sent_b = shift(far_b, "xl", 1)
    fourth = neighbours(3, *third)
    third2 = other_core(*tie(third, far_b))
    moved_a = to_owners(owners_a)
    near_b = attend(tie(near_q, *second2, *fars[1:], far_b, *moved_a), cut, kv_b, False)
    fars += other_core(tie(far3, near_b[1]))
    owners_b = merge(tie(where, *third2), *near_b, sent_b)
    moved_b = to_owners(owners_b)
    fourth2 = other_core(*tie(fourth, *moved_b[1:]))
    moved = [moved_a, moved_b]
    atts = [moved[part][step] for step in (0, 1, 3, 2) for part in range(2)]
    pieces = [lot[way] for way in range(2) for lot in (first, second, third, fourth)]
    pieces += [far0, far1, far2, far3]
    twins = (first2, second2, third2, fourth2)
    pieces += [lot[way] for way in range(2) for lot in twins]
    pieces += fars
    return project(place, atts, stream, t_stream, *gates, out_weight, pieces)


def solution(mesh):
    fine = Mesh(
        mesh.devices.reshape(SIZES["xl"], SIZES["z"], SIZES["core"], SIZES["head"], -1),
        ("xl", "z", "core", "head", "dp"),
    )
    tokens = ("dp", "xl", "z", "core")
    spread = P(tokens, "head")
    rows = P((*tokens, "head"), None)
    return jax.shard_map(
        on_device,
        mesh=fine,
        in_specs=(spread,) * 6 + (P("head", None), rows, rows, P(), P()),
        out_specs=(rows, rows),
        check_vma=False,
    )
```

```python
import functools

import jax
import jax.numpy as jnp
from jax import lax
from jax.experimental import pallas as pl
from jax.experimental.pallas import tpu as pltpu
from jax.sharding import Mesh
from jax.sharding import PartitionSpec as P

HD = 128
LOG2E = 1.4426950408889634
SCALE = HD**-0.5
CHUNK = 512
SIZES = {"xl": 2, "z": 4, "core": 2, "head": 4}
WIDE = 640
VMEM = 60 * 1024 * 1024


def shift(value, axis, step):
    size = SIZES[axis]
    return lax.ppermute(value, axis, [(i, (i + step) % size) for i in range(size)])


def swap_parts(value):
    return lax.ppermute(value, ("xl", "dp"), [(1, 2), (2, 1), (3, 0), (0, 3)])


def attend_kernel(rows, q_ref, kv, *refs):
    *outs, kk, vv, scores = refs
    blocks, _, size, _ = kv.shape
    keys = blocks * size
    for i in range(blocks):
        kk[i * size : (i + 1) * size, :] = kv[i, 0, :, : 2 * HD]
        vv[i * size : (i + 1) * size, :] = kv[i, 0, :, 2 * HD :]
    across = (((1,), (1,)), ((), ()))
    query = q_ref[0, :, :HD]
    mixed = jnp.concatenate([q_ref[0, :, HD:], query], axis=1)
    peak = None
    for c in range(0, keys, CHUNK):
        s = lax.dot_general(
            query, kk[c : c + CHUNK, :HD], across, preferred_element_type=jnp.float32
        )
        scores[:, c : c + CHUNK] = s
        for lane in range(0, CHUNK, 128):
            part = s[:, lane : lane + 128]
            peak = part if peak is None else jnp.maximum(peak, part)
    top = jnp.max(peak, axis=1, keepdims=True) * (SCALE * LOG2E)
    den = jnp.zeros((rows, 128), jnp.float32)
    mass = jnp.zeros((rows, 128), jnp.float32)
    wide = jnp.zeros((rows, 2 * HD), jnp.float32)
    tilt = jnp.zeros((rows, HD), jnp.float32)
    for c in range(0, keys, CHUNK):
        slope = lax.dot_general(
            mixed, kk[c : c + CHUNK, :], across, preferred_element_type=jnp.float32
        )
        w = jnp.exp2(scores[:, c : c + CHUNK] * (SCALE * LOG2E) - top)
        g = w * slope
        for lane in range(0, CHUNK, 128):
            den = den + w[:, lane : lane + 128]
            mass = mass + g[:, lane : lane + 128]
        wide = wide + jnp.dot(
            w.astype(jnp.bfloat16), vv[c : c + CHUNK, :], preferred_element_type=jnp.float32
        )
        tilt = tilt + jnp.dot(
            g.astype(jnp.bfloat16), vv[c : c + CHUNK, :HD], preferred_element_type=jnp.float32
        )
    den = jnp.sum(den, axis=1, keepdims=True)
    inverse = 1.0 / den
    mean = jnp.sum(mass, axis=1, keepdims=True) * (inverse * SCALE)
    out = wide[:, :HD] * inverse
    t_out = (tilt * SCALE + wide[:, HD:]) * inverse - mean * out
    outs[0][0, :rows, :HD] = out.astype(outs[0].dtype)
    outs[0][0, :rows, HD:] = t_out.astype(outs[0].dtype)
    lane = lax.broadcasted_iota(jnp.int32, (rows, 128), 1)
    stats = jnp.transpose(jnp.where(lane == 0, top + jnp.log2(den), mean))[:8, :]
    if len(outs) == 2:
        outs[1][0] = stats
    else:
        stats = stats[:2, :]
        high = stats.astype(jnp.bfloat16).astype(jnp.float32)
        middle = (stats - high).astype(jnp.bfloat16).astype(jnp.float32)
        low = stats - high - middle
        terms = jnp.concatenate([high, middle, low, jnp.zeros_like(low)], axis=0)
        over = 2 * HD
        rest = jnp.concatenate(
            [terms[:, over:], jnp.zeros((8, 2 * over - rows), jnp.float32)], axis=1
        )
        outs[0][0, rows:, :] = jnp.concatenate([terms[:, :over], rest], axis=0).astype(jnp.bfloat16)


def attend(q, first, kv, sent):
    rows = q.shape[1]
    blocks, heads, size, _ = kv.shape
    keys = blocks * size

    def spec(r, c, at=0):
        return pl.BlockSpec((1, r, c), lambda h: (h + at, 0, 0))

    return pl.pallas_call(
        functools.partial(attend_kernel, rows),
        grid=(heads,),
        in_specs=[
            spec(rows, 2 * HD, first),
            pl.BlockSpec((blocks, 1, size, 4 * HD), lambda h: (0, h, 0, 0)),
        ],
        out_specs=[spec(rows + 16, 2 * HD)] if sent else [spec(rows, 2 * HD), spec(8, rows)],
        out_shape=[jax.ShapeDtypeStruct((heads, rows + 16, 2 * HD), jnp.bfloat16)]
        if sent
        else [
            jax.ShapeDtypeStruct((heads, rows, 2 * HD), jnp.float32),
            jax.ShapeDtypeStruct((heads, 8, rows), jnp.float32),
        ],
        scratch_shapes=[
            pltpu.VMEM((keys, 2 * HD), jnp.bfloat16),
            pltpu.VMEM((keys, 2 * HD), jnp.bfloat16),
            pltpu.VMEM((rows, keys), jnp.float32),
        ],
        compiler_params=pltpu.CompilerParams(vmem_limit_bytes=VMEM),
        cost_estimate=pl.CostEstimate(
            flops=heads * rows * keys * HD * 12, bytes_accessed=1000, transcendentals=0
        ),
    )(q, kv)


def merge_kernel(me_ref, near_ref, near_stat, far_ref, *refs):
    before, (*outs, both) = refs[:-5], refs[-5:]
    heads, count, _ = near_ref.shape
    for h in range(heads):
        lse_a, mean_a = near_stat[h, 0:1, :], near_stat[h, 1:2, :]
        terms = far_ref[h, count:, :].astype(jnp.float32)
        terms = jnp.concatenate([terms[:8], terms[8:, : count - 2 * HD]], axis=1)
        lse_b = terms[0:1] + terms[2:3] + terms[4:5]
        mean_b = terms[1:2] + terms[3:4] + terms[5:6]
        top = jnp.maximum(lse_a, lse_b)
        wa = jnp.exp2(lse_a - top)
        wb = jnp.exp2(lse_b - top)
        inverse = 1.0 / (wa + wb)
        wa = wa * inverse
        wb = wb * inverse
        mean = wa * mean_a + wb * mean_b
        terms = [wa, wb, wa * (mean_a - mean), wb * (mean_b - mean)]
        terms = jnp.transpose(jnp.concatenate(terms + terms, axis=0))
        wa, wb, da, db = (terms[:, i : i + 1] for i in range(4))
        near = near_ref[h]
        far = far_ref[h, :count, :].astype(jnp.float32)
        oa, ob = near[:, :HD], far[:, :HD]
        out = wa * oa + wb * ob
        t_out = wa * near[:, HD:] + wb * far[:, HD:] + da * oa + db * ob
        both[0, :, h * HD : (h + 1) * HD] = out.astype(both.dtype)
        both[1, :, h * HD : (h + 1) * HD] = t_out.astype(both.dtype)
    rows = outs[0].shape[1]
    for step in range(4):
        at = pl.multiple_of(lax.rem(me_ref[0] + step, 4) * rows, 16)
        done = 0
        if before:
            done = before[step].shape[2]
            outs[step][:, :, :done] = before[step][...]
        outs[step][:, :, done:] = both[:, pl.ds(at, rows), :]


def merge(me, near, near_stat, far, *before):
    heads, rows, _ = near.shape
    width = heads * HD + (before[0].shape[2] if before else 0)
    whole = pl.BlockSpec(memory_space=pltpu.VMEM)
    return pl.pallas_call(
        merge_kernel,
        in_specs=[pl.BlockSpec(memory_space=pltpu.SMEM)] + [whole] * (3 + len(before)),
        out_specs=[whole] * 4,
        out_shape=[jax.ShapeDtypeStruct((2, rows // 4, width), jnp.bfloat16)] * 4,
        scratch_shapes=[pltpu.VMEM((2, rows, heads * HD), jnp.bfloat16)],
        compiler_params=pltpu.CompilerParams(vmem_limit_bytes=VMEM),
        cost_estimate=pl.CostEstimate(flops=1000, bytes_accessed=1000, transcendentals=0),
    )(me, near, near_stat, far, *before)


def pack_kernel(cut, q, t_q, k, t_k, v, t_v, first_ref, second_ref, q_ref):
    heads = q.shape[1] // HD
    for h in range(heads):
        cols = slice(h * HD, (h + 1) * HD)
        out, at = (first_ref, h) if h < cut else (second_ref, h - cut)
        for i, ref in enumerate((k, t_k, v, t_v)):
            out[at, :, i * HD : (i + 1) * HD] = ref[:, cols]
        q_ref[h, :, :HD] = q[:, cols]
        q_ref[h, :, HD:] = t_q[:, cols]


def pack(cut, *arrays):
    rows, width = arrays[0].shape
    heads = width // HD
    whole = pl.BlockSpec(memory_space=pltpu.VMEM)
    return pl.pallas_call(
        functools.partial(pack_kernel, cut),
        in_specs=[whole] * 6,
        out_specs=[whole] * 3,
        out_shape=[
            jax.ShapeDtypeStruct((cut, rows, 4 * HD), jnp.bfloat16),
            jax.ShapeDtypeStruct((heads - cut, rows, 4 * HD), jnp.bfloat16),
            jax.ShapeDtypeStruct((heads, rows, 2 * HD), jnp.bfloat16),
        ],
        compiler_params=pltpu.CompilerParams(vmem_limit_bytes=VMEM),
        cost_estimate=pl.CostEstimate(flops=1000, bytes_accessed=1000, transcendentals=0),
    )(*arrays)


def project_kernel(parts, place_ref, *refs):
    atts, refs = refs[: 4 * parts], refs[4 * parts :]
    stream, t_stream, gate, t_gate, weight = refs[:5]
    pieces = refs[5:29]
    result, t_result, att, slots, sems = refs[29:]
    rows = stream.shape[0]
    depth = weight.shape[0]
    core = place_ref[0]

    def copy(slot, step, source):
        return pltpu.make_async_copy(
            source, slots.at[slot, pl.ds(step * depth, depth), :], sems.at[slot, step]
        )

    copies = []
    for slot in range(8):
        half, lot = divmod(slot, 4)
        below, above, far = (pieces[12 * half + 4 * i : 12 * half + 4 * i + 4] for i in range(3))
        col = pl.multiple_of((lax.rem(core + half, 2) * 4 + lot) * WIDE, WIDE)
        for step, source in enumerate((weight.at[:, pl.ds(col, WIDE)], below[lot], above[lot])):
            copy(slot, step, source).start()
        for i in range(4):

            @pl.when(place_ref[1 + i] == lot)
            def _():
                copy(slot, 3, far[i]).start()

        copies.append((slot, lot, col, far[0]))
    at = 0
    for ref in atts:
        size = ref.shape[2]
        att[:rows, at : at + size] = ref[0]
        att[rows:, at : at + size] = ref[1]
        at += size
    for slot, lot, col, like in copies:
        for step in range(4):
            copy(slot, step, like).wait()
        sums = jnp.dot(att[...], slots[slot], preferred_element_type=jnp.float32)
        branch, t_branch = sums[:rows], sums[rows:]
        cols = pl.ds(col, WIDE)
        g = gate[:, cols].astype(jnp.float32)
        tg = t_gate[:, cols].astype(jnp.float32)
        result[:, cols] = (stream[:, cols].astype(jnp.float32) + g * branch).astype(result.dtype)
        t_result[:, cols] = (
            t_stream[:, cols].astype(jnp.float32) + tg * branch + g * t_branch
        ).astype(t_result.dtype)


def project(place, atts, stream, t_stream, gate, t_gate, weight, pieces):
    rows, columns = stream.shape
    depth = weight.shape[0]
    whole = pl.BlockSpec(memory_space=pltpu.VMEM)
    away = pl.BlockSpec(memory_space=pl.ANY)
    return pl.pallas_call(
        functools.partial(project_kernel, len(atts) // 4),
        in_specs=[pl.BlockSpec(memory_space=pltpu.SMEM)]
        + [whole] * (len(atts) + 4)
        + [away] * (1 + len(pieces)),
        out_specs=[whole] * 2,
        out_shape=[jax.ShapeDtypeStruct((rows, columns), stream.dtype)] * 2,
        scratch_shapes=[
            pltpu.VMEM((2 * rows, 4 * depth), jnp.bfloat16),
            pltpu.VMEM((8, 4 * depth, WIDE), jnp.bfloat16),
            pltpu.SemaphoreType.DMA((8, 4)),
        ],
        compiler_params=pltpu.CompilerParams(vmem_limit_bytes=VMEM),
        cost_estimate=pl.CostEstimate(flops=1000, bytes_accessed=1000, transcendentals=0),
    )(place, *atts, stream, t_stream, gate, t_gate, weight, *pieces)


def on_device(
    queries, keys, values, t_queries, t_keys, t_values, out_weight, stream, t_stream, gate, t_gate
):
    heads = queries.shape[1] // HD
    depth = out_weight.shape[0]
    half_width = out_weight.shape[1] // 2
    cut = heads - 1
    core, side, me = lax.axis_index("core"), lax.axis_index("xl"), lax.axis_index("head")
    x = 2 * lax.axis_index("dp") + side
    places = [x, x ^ 1, 3 - x, 3 - (x ^ 1)]

    def quarter(place):
        return lax.dynamic_slice(
            out_weight, (0, core * half_width + place * WIDE), (depth, WIDE)
        )

    def tie(value, *earlier):
        return lax.optimization_barrier((value, *earlier))[0]

    def neighbours(lot, *earlier):
        value = quarter(lot)
        if earlier:
            value = tie(value, *earlier)
        return shift(value, "head", 1), shift(value, "head", -1)

    def other_core(*pieces):
        return [shift(piece, "core", 1) for piece in pieces]

    lot_a, lot_b, near_q = pack(cut, queries, t_queries, keys, t_keys, values, t_values)
    kv_a = lax.all_gather(lot_a, ("z", "core"))
    kv_b = lax.all_gather(lot_b, ("z", "core"))
    far_q = shift(near_q, "xl", 1)
    gates = gate.reshape(1, -1), t_gate.reshape(1, -1)
    place = jnp.stack([core, *places]).astype(jnp.int32)
    where = me.astype(jnp.int32).reshape(1)

    far0 = shift(quarter(places[0]), "head", 2)
    first = neighbours(0)
    second = neighbours(1, far0)
    far1, far2 = shift(far0, "xl", 1), swap_parts(far0)

    first2, fars = other_core(*first), other_core(far0)
    third = neighbours(2, *second)
    far3 = swap_parts(far1)

    (far_a,) = attend(
        tie(far_q, *first2, *fars, *second, far1, far2, *gates, place, where), 0, kv_a, True
    )
    sent_a = shift(far_a, "xl", 1)
    second2 = other_core(*second)
    fars += other_core(far1, far2)
    near_a = attend(tie(near_q, far_a, *second2, *fars), 0, kv_a, False)
    (far_b,) = attend(tie(far_q, *third, far3, near_a[1]), cut, kv_b, True)
    sent_b = shift(far_b, "xl", 1)
    fourth = neighbours(3, *third)
    third2 = other_core(*tie(third, far_b))
    fars += other_core(tie(far3, far_b))
    owners_a = merge(tie(where, far_b), *near_a, sent_a)
    near_b = attend(tie(near_q, far_b, owners_a[0]), cut, kv_b, False)
    owners = merge(tie(where, *third2, fars[3]), *near_b, sent_b, *owners_a)
    moved = [owners[0]] + [shift(owners[step], "head", step) for step in (1, 2, 3)]
    fourth2 = other_core(*tie(fourth, *moved[1:]))
    atts = [moved[step] for step in (0, 1, 3, 2)]
    pieces = [lot[way] for way in range(2) for lot in (first, second, third, fourth)]
    pieces += [far0, far1, far2, far3]
    twins = (first2, second2, third2, fourth2)
    pieces += [lot[way] for way in range(2) for lot in twins]
    pieces += fars
    return project(place, atts, stream, t_stream, *gates, out_weight, pieces)


def solution(mesh):
    fine = Mesh(
        mesh.devices.reshape(SIZES["xl"], SIZES["z"], SIZES["core"], SIZES["head"], -1),
        ("xl", "z", "core", "head", "dp"),
    )
    tokens = ("dp", "xl", "z", "core")
    spread = P(tokens, "head")
    rows = P((*tokens, "head"), None)
    return jax.shard_map(
        on_device,
        mesh=fine,
        in_specs=(spread,) * 6 + (P("head", None), rows, rows, P(), P()),
        out_specs=(rows, rows),
        check_vma=False,
    )
```

```python
import functools

import jax
import jax.numpy as jnp
from jax import lax
from jax.experimental import pallas as pl
from jax.experimental.pallas import tpu as pltpu
from jax.sharding import Mesh
from jax.sharding import PartitionSpec as P

HD = 128
LOG2E = 1.4426950408889634
SCALE = HD**-0.5
CHUNK = 512
SIZES = {"xl": 2, "z": 4, "core": 2, "head": 4}
WIDE = 640
VMEM = 60 * 1024 * 1024


def shift(value, axis, step):
    size = SIZES[axis]
    return lax.ppermute(value, axis, [(i, (i + step) % size) for i in range(size)])


def swap_parts(value):
    return lax.ppermute(value, ("xl", "dp"), [(1, 2), (2, 1), (3, 0), (0, 3)])


def attend_kernel(rows, q_ref, kv, *refs):
    *outs, kk, vv, scores = refs
    blocks, _, size, _ = kv.shape
    keys = blocks * size
    for i in range(blocks):
        kk[i * size : (i + 1) * size, :] = kv[i, 0, :, : 2 * HD]
        vv[i * size : (i + 1) * size, :] = kv[i, 0, :, 2 * HD :]
    across = (((1,), (1,)), ((), ()))
    query = q_ref[0, :, :HD]
    mixed = jnp.concatenate([q_ref[0, :, HD:], query], axis=1)
    peak = None
    for c in range(0, keys, CHUNK):
        s = lax.dot_general(
            query, kk[c : c + CHUNK, :HD], across, preferred_element_type=jnp.float32
        )
        scores[:, c : c + CHUNK] = s
        for lane in range(0, CHUNK, 128):
            part = s[:, lane : lane + 128]
            peak = part if peak is None else jnp.maximum(peak, part)
    top = jnp.max(peak, axis=1, keepdims=True) * (SCALE * LOG2E)
    den = jnp.zeros((rows, 128), jnp.float32)
    mass = jnp.zeros((rows, 128), jnp.float32)
    wide = jnp.zeros((rows, 2 * HD), jnp.float32)
    tilt = jnp.zeros((rows, HD), jnp.float32)
    for c in range(0, keys, CHUNK):
        slope = lax.dot_general(
            mixed, kk[c : c + CHUNK, :], across, preferred_element_type=jnp.float32
        )
        w = jnp.exp2(scores[:, c : c + CHUNK] * (SCALE * LOG2E) - top)
        g = w * slope
        for lane in range(0, CHUNK, 128):
            den = den + w[:, lane : lane + 128]
            mass = mass + g[:, lane : lane + 128]
        wide = wide + jnp.dot(
            w.astype(jnp.bfloat16), vv[c : c + CHUNK, :], preferred_element_type=jnp.float32
        )
        tilt = tilt + jnp.dot(
            g.astype(jnp.bfloat16), vv[c : c + CHUNK, :HD], preferred_element_type=jnp.float32
        )
    den = jnp.sum(den, axis=1, keepdims=True)
    inverse = 1.0 / den
    mean = jnp.sum(mass, axis=1, keepdims=True) * (inverse * SCALE)
    out = wide[:, :HD] * inverse
    t_out = (tilt * SCALE + wide[:, HD:]) * inverse - mean * out
    outs[0][0, :rows, :HD] = out.astype(outs[0].dtype)
    outs[0][0, :rows, HD:] = t_out.astype(outs[0].dtype)
    lane = lax.broadcasted_iota(jnp.int32, (rows, 128), 1)
    stats = jnp.transpose(jnp.where(lane == 0, top + jnp.log2(den), mean))[:8, :]
    if len(outs) == 2:
        outs[1][0] = stats
    else:
        stats = stats[:2, :]
        high = stats.astype(jnp.bfloat16).astype(jnp.float32)
        middle = (stats - high).astype(jnp.bfloat16).astype(jnp.float32)
        low = stats - high - middle
        terms = jnp.concatenate([high, middle, low, jnp.zeros_like(low)], axis=0)
        over = 2 * HD
        rest = jnp.concatenate(
            [terms[:, over:], jnp.zeros((8, 2 * over - rows), jnp.float32)], axis=1
        )
        outs[0][0, rows:, :] = jnp.concatenate([terms[:, :over], rest], axis=0).astype(jnp.bfloat16)


def attend(q, first, kv, sent):
    rows = q.shape[1]
    blocks, heads, size, _ = kv.shape
    keys = blocks * size

    def spec(r, c, at=0):
        return pl.BlockSpec((1, r, c), lambda h: (h + at, 0, 0))

    return pl.pallas_call(
        functools.partial(attend_kernel, rows),
        grid=(heads,),
        in_specs=[
            spec(rows, 2 * HD, first),
            pl.BlockSpec((blocks, 1, size, 4 * HD), lambda h: (0, h, 0, 0)),
        ],
        out_specs=[spec(rows + 16, 2 * HD)] if sent else [spec(rows, 2 * HD), spec(8, rows)],
        out_shape=[jax.ShapeDtypeStruct((heads, rows + 16, 2 * HD), jnp.bfloat16)]
        if sent
        else [
            jax.ShapeDtypeStruct((heads, rows, 2 * HD), jnp.float32),
            jax.ShapeDtypeStruct((heads, 8, rows), jnp.float32),
        ],
        scratch_shapes=[
            pltpu.VMEM((keys, 2 * HD), jnp.bfloat16),
            pltpu.VMEM((keys, 2 * HD), jnp.bfloat16),
            pltpu.VMEM((rows, keys), jnp.float32),
        ],
        compiler_params=pltpu.CompilerParams(vmem_limit_bytes=VMEM),
        cost_estimate=pl.CostEstimate(
            flops=heads * rows * keys * HD * 12, bytes_accessed=1000, transcendentals=0
        ),
    )(q, kv)


def merge_kernel(me_ref, near_ref, near_stat, far_ref, *refs):
    before, (*outs, both) = refs[:-5], refs[-5:]
    heads, count, _ = near_ref.shape
    for h in range(heads):
        lse_a, mean_a = near_stat[h, 0:1, :], near_stat[h, 1:2, :]
        terms = far_ref[h, count:, :].astype(jnp.float32)
        terms = jnp.concatenate([terms[:8], terms[8:, : count - 2 * HD]], axis=1)
        lse_b = terms[0:1] + terms[2:3] + terms[4:5]
        mean_b = terms[1:2] + terms[3:4] + terms[5:6]
        top = jnp.maximum(lse_a, lse_b)
        wa = jnp.exp2(lse_a - top)
        wb = jnp.exp2(lse_b - top)
        inverse = 1.0 / (wa + wb)
        wa = wa * inverse
        wb = wb * inverse
        mean = wa * mean_a + wb * mean_b
        terms = [wa, wb, wa * (mean_a - mean), wb * (mean_b - mean)]
        terms = jnp.transpose(jnp.concatenate(terms + terms, axis=0))
        wa, wb, da, db = (terms[:, i : i + 1] for i in range(4))
        near = near_ref[h]
        far = far_ref[h, :count, :].astype(jnp.float32)
        oa, ob = near[:, :HD], far[:, :HD]
        out = wa * oa + wb * ob
        t_out = wa * near[:, HD:] + wb * far[:, HD:] + da * oa + db * ob
        both[0, :, h * HD : (h + 1) * HD] = out.astype(both.dtype)
        both[1, :, h * HD : (h + 1) * HD] = t_out.astype(both.dtype)
    rows = outs[0].shape[1]
    for step in range(4):
        at = pl.multiple_of(lax.rem(me_ref[0] + step, 4) * rows, 16)
        done = 0
        if before:
            done = before[step].shape[2]
            outs[step][:, :, :done] = before[step][...]
        outs[step][:, :, done:] = both[:, pl.ds(at, rows), :]


def merge(me, near, near_stat, far, *before):
    heads, rows, _ = near.shape
    width = heads * HD + (before[0].shape[2] if before else 0)
    whole = pl.BlockSpec(memory_space=pltpu.VMEM)
    return pl.pallas_call(
        merge_kernel,
        in_specs=[pl.BlockSpec(memory_space=pltpu.SMEM)] + [whole] * (3 + len(before)),
        out_specs=[whole] * 4,
        out_shape=[jax.ShapeDtypeStruct((2, rows // 4, width), jnp.bfloat16)] * 4,
        scratch_shapes=[pltpu.VMEM((2, rows, heads * HD), jnp.bfloat16)],
        compiler_params=pltpu.CompilerParams(vmem_limit_bytes=VMEM),
        cost_estimate=pl.CostEstimate(flops=1000, bytes_accessed=1000, transcendentals=0),
    )(me, near, near_stat, far, *before)


def pack_kernel(cut, q, t_q, k, t_k, v, t_v, first_ref, second_ref, q_ref):
    heads = q.shape[1] // HD
    for h in range(heads):
        cols = slice(h * HD, (h + 1) * HD)
        out, at = (first_ref, h) if h < cut else (second_ref, h - cut)
        for i, ref in enumerate((k, t_k, v, t_v)):
            out[at, :, i * HD : (i + 1) * HD] = ref[:, cols]
        q_ref[h, :, :HD] = q[:, cols]
        q_ref[h, :, HD:] = t_q[:, cols]


def pack(cut, *arrays):
    rows, width = arrays[0].shape
    heads = width // HD
    whole = pl.BlockSpec(memory_space=pltpu.VMEM)
    return pl.pallas_call(
        functools.partial(pack_kernel, cut),
        in_specs=[whole] * 6,
        out_specs=[whole] * 3,
        out_shape=[
            jax.ShapeDtypeStruct((cut, rows, 4 * HD), jnp.bfloat16),
            jax.ShapeDtypeStruct((heads - cut, rows, 4 * HD), jnp.bfloat16),
            jax.ShapeDtypeStruct((heads, rows, 2 * HD), jnp.bfloat16),
        ],
        compiler_params=pltpu.CompilerParams(vmem_limit_bytes=VMEM),
        cost_estimate=pl.CostEstimate(flops=1000, bytes_accessed=1000, transcendentals=0),
    )(*arrays)


def project_kernel(parts, place_ref, *refs):
    atts, refs = refs[: 4 * parts], refs[4 * parts :]
    stream, t_stream, gate, t_gate, weight = refs[:5]
    pieces = refs[5:29]
    result, t_result, att, slots, sems = refs[29:]
    rows = stream.shape[0]
    depth = weight.shape[0]
    core = place_ref[0]

    def copy(slot, step, source):
        place = slots.at[slot // 2, pl.ds(step * depth, depth), pl.ds(slot % 2 * WIDE, WIDE)]
        return pltpu.make_async_copy(source, place, sems.at[slot, step])

    copies = []
    for slot in range(8):
        half, lot = divmod(slot, 4)
        below, above, far = (pieces[12 * half + 4 * i : 12 * half + 4 * i + 4] for i in range(3))
        col = pl.multiple_of((lax.rem(core + half, 2) * 4 + lot) * WIDE, WIDE)
        for step, source in enumerate((weight.at[:, pl.ds(col, WIDE)], below[lot], above[lot])):
            copy(slot, step, source).start()
        for i in range(4):

            @pl.when(place_ref[1 + i] == lot)
            def _():
                copy(slot, 3, far[i]).start()

        copies.append((col, far[0]))
    at = 0
    for ref in atts:
        size = ref.shape[2]
        att[:rows, at : at + size] = ref[0]
        att[rows:, at : at + size] = ref[1]
        at += size
    for pair in range(4):
        col, like = copies[2 * pair]
        for slot in (2 * pair, 2 * pair + 1):
            for step in range(4):
                copy(slot, step, like).wait()
        sums = jnp.dot(att[...], slots[pair], preferred_element_type=jnp.float32)
        branch, t_branch = sums[:rows], sums[rows:]
        cols = pl.ds(col, 2 * WIDE)
        g = gate[:, cols].astype(jnp.float32)
        tg = t_gate[:, cols].astype(jnp.float32)
        result[:, cols] = (stream[:, cols].astype(jnp.float32) + g * branch).astype(result.dtype)
        t_result[:, cols] = (
            t_stream[:, cols].astype(jnp.float32) + tg * branch + g * t_branch
        ).astype(t_result.dtype)


def project(place, atts, stream, t_stream, gate, t_gate, weight, pieces):
    rows, columns = stream.shape
    depth = weight.shape[0]
    whole = pl.BlockSpec(memory_space=pltpu.VMEM)
    away = pl.BlockSpec(memory_space=pl.ANY)
    return pl.pallas_call(
        functools.partial(project_kernel, len(atts) // 4),
        in_specs=[pl.BlockSpec(memory_space=pltpu.SMEM)]
        + [whole] * (len(atts) + 4)
        + [away] * (1 + len(pieces)),
        out_specs=[whole] * 2,
        out_shape=[jax.ShapeDtypeStruct((rows, columns), stream.dtype)] * 2,
        scratch_shapes=[
            pltpu.VMEM((2 * rows, 4 * depth), jnp.bfloat16),
            pltpu.VMEM((4, 4 * depth, 2 * WIDE), jnp.bfloat16),
            pltpu.SemaphoreType.DMA((8, 4)),
        ],
        compiler_params=pltpu.CompilerParams(vmem_limit_bytes=VMEM),
        cost_estimate=pl.CostEstimate(flops=1000, bytes_accessed=1000, transcendentals=0),
    )(place, *atts, stream, t_stream, gate, t_gate, weight, *pieces)


def on_device(
    queries, keys, values, t_queries, t_keys, t_values, out_weight, stream, t_stream, gate, t_gate
):
    heads = queries.shape[1] // HD
    depth = out_weight.shape[0]
    half_width = out_weight.shape[1] // 2
    cut = heads - 1
    core, side, me = lax.axis_index("core"), lax.axis_index("xl"), lax.axis_index("head")
    x = 2 * lax.axis_index("dp") + side
    places = [x, x ^ 1, 3 - x, 3 - (x ^ 1)]

    def quarter(place):
        return lax.dynamic_slice(
            out_weight, (0, core * half_width + place * WIDE), (depth, WIDE)
        )

    def tie(value, *earlier):
        return lax.optimization_barrier((value, *earlier))[0]

    def neighbours(lot, *earlier):
        value = quarter(lot)
        if earlier:
            value = tie(value, *earlier)
        return shift(value, "head", 1), shift(value, "head", -1)

    def other_core(*pieces):
        return [shift(piece, "core", 1) for piece in pieces]

    lot_a, lot_b, near_q = pack(cut, queries, t_queries, keys, t_keys, values, t_values)
    kv_a = lax.all_gather(lot_a, ("z", "core"))
    kv_b = lax.all_gather(lot_b, ("z", "core"))
    far_q = shift(near_q, "xl", 1)
    gates = gate.reshape(1, -1), t_gate.reshape(1, -1)
    place = jnp.stack([core, *places]).astype(jnp.int32)
    where = me.astype(jnp.int32).reshape(1)

    far0 = tie(shift(quarter(places[0]), "head", 2), far_q)
    first = neighbours(0)
    far1, far2 = shift(far0, "xl", 1), swap_parts(far0)
    second = neighbours(1, *first, far1, far2)

    first2, fars = other_core(*first), other_core(far0)
    far3 = swap_parts(far1)

    (far_a,) = attend(
        tie(far_q, *first2, *fars, far1, far2, *gates, place, where), 0, kv_a, True
    )
    sent_a = shift(far_a, "xl", 1)
    third = neighbours(2, *second, far_a)
    second2 = other_core(*tie(second, far_a))
    fars += other_core(far1, far2)
    near_a = attend(tie(near_q, far_a, *second2, *fars), 0, kv_a, False)
    (far_b,) = attend(tie(far_q, *third, far3, near_a[1]), cut, kv_b, True)
    sent_b = shift(far_b, "xl", 1)
    fourth = neighbours(3, *third)
    third2 = other_core(*tie(third, far_b))
    fars += other_core(tie(far3, far_b))
    owners_a = merge(tie(where, far_b), *near_a, sent_a)
    near_b = attend(tie(near_q, far_b, owners_a[0]), cut, kv_b, False)
    owners = merge(tie(where, *third2, fars[3]), *near_b, sent_b, *owners_a)
    moved = [owners[0]] + [shift(owners[step], "head", step) for step in (1, 2, 3)]
    fourth2 = other_core(*tie(fourth, *moved[1:]))
    atts = [moved[step] for step in (0, 1, 3, 2)]
    pieces = [lot[way] for way in range(2) for lot in (first, second, third, fourth)]
    pieces += [far0, far1, far2, far3]
    twins = (first2, second2, third2, fourth2)
    pieces += [lot[way] for way in range(2) for lot in twins]
    pieces += fars
    return project(place, atts, stream, t_stream, *gates, out_weight, pieces)


def solution(mesh):
    fine = Mesh(
        mesh.devices.reshape(SIZES["xl"], SIZES["z"], SIZES["core"], SIZES["head"], -1),
        ("xl", "z", "core", "head", "dp"),
    )
    tokens = ("dp", "xl", "z", "core")
    spread = P(tokens, "head")
    rows = P((*tokens, "head"), None)
    return jax.shard_map(
        on_device,
        mesh=fine,
        in_specs=(spread,) * 6 + (P("head", None), rows, rows, P(), P()),
        out_specs=(rows, rows),
        check_vma=False,
    )
```

```python
import functools

import jax
import jax.numpy as jnp
from jax import lax
from jax.experimental import pallas as pl
from jax.experimental.pallas import tpu as pltpu
from jax.sharding import Mesh
from jax.sharding import PartitionSpec as P

HD = 128
LOG2E = 1.4426950408889634
SCALE = HD**-0.5
CHUNK = 512
SIZES = {"xl": 2, "z": 4, "core": 2, "head": 4}
WIDE = 640
VMEM = 60 * 1024 * 1024


def shift(value, axis, step):
    size = SIZES[axis]
    return lax.ppermute(value, axis, [(i, (i + step) % size) for i in range(size)])


def swap_parts(value):
    return lax.ppermute(value, ("xl", "dp"), [(1, 2), (2, 1), (3, 0), (0, 3)])


def attend_kernel(sent, *refs):
    count = len(sent)
    queries, kv = refs[:count], refs[count]
    *outs, kk, vv, scores = refs[count + 1 :]
    blocks, _, size, _ = kv.shape
    keys = blocks * size
    for i in range(blocks):
        kk[i * size : (i + 1) * size, :] = kv[i, 0, :, : 2 * HD]
        vv[i * size : (i + 1) * size, :] = kv[i, 0, :, 2 * HD :]
    across = (((1,), (1,)), ((), ()))
    size = queries[0].shape[1]
    rows = count * size
    query = jnp.concatenate([q[0, :, :HD] for q in queries], axis=0)
    mixed = jnp.concatenate([q[0, :, HD:] for q in queries], axis=0)
    mixed = jnp.concatenate([mixed, query], axis=1)
    peak = None
    for c in range(0, keys, CHUNK):
        s = lax.dot_general(
            query, kk[c : c + CHUNK, :HD], across, preferred_element_type=jnp.float32
        )
        scores[:, c : c + CHUNK] = s
        for lane in range(0, CHUNK, 128):
            part = s[:, lane : lane + 128]
            peak = part if peak is None else jnp.maximum(peak, part)
    top = jnp.max(peak, axis=1, keepdims=True) * (SCALE * LOG2E)
    den = jnp.zeros((rows, 128), jnp.float32)
    mass = jnp.zeros((rows, 128), jnp.float32)
    wide = jnp.zeros((rows, 2 * HD), jnp.float32)
    tilt = jnp.zeros((rows, HD), jnp.float32)
    for c in range(0, keys, CHUNK):
        slope = lax.dot_general(
            mixed, kk[c : c + CHUNK, :], across, preferred_element_type=jnp.float32
        )
        w = jnp.exp2(scores[:, c : c + CHUNK] * (SCALE * LOG2E) - top)
        g = w * slope
        for lane in range(0, CHUNK, 128):
            den = den + w[:, lane : lane + 128]
            mass = mass + g[:, lane : lane + 128]
        wide = wide + jnp.dot(
            w.astype(jnp.bfloat16), vv[c : c + CHUNK, :], preferred_element_type=jnp.float32
        )
        tilt = tilt + jnp.dot(
            g.astype(jnp.bfloat16), vv[c : c + CHUNK, :HD], preferred_element_type=jnp.float32
        )
    den = jnp.sum(den, axis=1, keepdims=True)
    inverse = 1.0 / den
    mean = jnp.sum(mass, axis=1, keepdims=True) * (inverse * SCALE)
    out = wide[:, :HD] * inverse
    t_out = (tilt * SCALE + wide[:, HD:]) * inverse - mean * out
    lane = lax.broadcasted_iota(jnp.int32, (rows, 128), 1)
    both = jnp.where(lane == 0, top + jnp.log2(den), mean)
    outs = list(outs)
    for i, goes in enumerate(sent):
        mine = slice(i * size, (i + 1) * size)
        ref = outs.pop(0)
        ref[0, :size, :HD] = out[mine].astype(ref.dtype)
        ref[0, :size, HD:] = t_out[mine].astype(ref.dtype)
        stats = jnp.transpose(both[mine])
        if not goes:
            outs.pop(0)[0] = stats[:8, :]
            continue
        stats = stats[:2, :]
        high = stats.astype(jnp.bfloat16).astype(jnp.float32)
        middle = (stats - high).astype(jnp.bfloat16).astype(jnp.float32)
        low = stats - high - middle
        terms = jnp.concatenate([high, middle, low, jnp.zeros_like(low)], axis=0)
        over = 2 * HD
        rest = jnp.concatenate(
            [terms[:, over:], jnp.zeros((8, 2 * over - size), jnp.float32)], axis=1
        )
        ref[0, size:, :] = jnp.concatenate([terms[:, :over], rest], axis=0).astype(jnp.bfloat16)


def attend(queries, first, kv, sent):
    rows = queries[0].shape[1]
    blocks, heads, size, _ = kv.shape
    keys = blocks * size

    def spec(r, c, at=0):
        return pl.BlockSpec((1, r, c), lambda h: (h + at, 0, 0))

    specs, shapes = [], []
    for goes in sent:
        if goes:
            specs += [spec(rows + 16, 2 * HD)]
            shapes += [jax.ShapeDtypeStruct((heads, rows + 16, 2 * HD), jnp.bfloat16)]
        else:
            specs += [spec(rows, 2 * HD), spec(8, rows)]
            shapes += [
                jax.ShapeDtypeStruct((heads, rows, 2 * HD), jnp.float32),
                jax.ShapeDtypeStruct((heads, 8, rows), jnp.float32),
            ]
    total = len(sent) * rows
    return pl.pallas_call(
        functools.partial(attend_kernel, sent),
        grid=(heads,),
        in_specs=[spec(rows, 2 * HD, first)] * len(sent)
        + [pl.BlockSpec((blocks, 1, size, 4 * HD), lambda h: (0, h, 0, 0))],
        out_specs=specs,
        out_shape=shapes,
        scratch_shapes=[
            pltpu.VMEM((keys, 2 * HD), jnp.bfloat16),
            pltpu.VMEM((keys, 2 * HD), jnp.bfloat16),
            pltpu.VMEM((total, keys), jnp.float32),
        ],
        compiler_params=pltpu.CompilerParams(vmem_limit_bytes=VMEM),
        cost_estimate=pl.CostEstimate(
            flops=heads * total * keys * HD * 12, bytes_accessed=1000, transcendentals=0
        ),
    )(*queries, kv)


def merge_kernel(me_ref, near_ref, near_stat, far_ref, *refs):
    before, (*outs, both) = refs[:-5], refs[-5:]
    heads, count, _ = near_ref.shape
    for h in range(heads):
        lse_a, mean_a = near_stat[h, 0:1, :], near_stat[h, 1:2, :]
        terms = far_ref[h, count:, :].astype(jnp.float32)
        terms = jnp.concatenate([terms[:8], terms[8:, : count - 2 * HD]], axis=1)
        lse_b = terms[0:1] + terms[2:3] + terms[4:5]
        mean_b = terms[1:2] + terms[3:4] + terms[5:6]
        top = jnp.maximum(lse_a, lse_b)
        wa = jnp.exp2(lse_a - top)
        wb = jnp.exp2(lse_b - top)
        inverse = 1.0 / (wa + wb)
        wa = wa * inverse
        wb = wb * inverse
        mean = wa * mean_a + wb * mean_b
        terms = [wa, wb, wa * (mean_a - mean), wb * (mean_b - mean)]
        terms = jnp.transpose(jnp.concatenate(terms + terms, axis=0))
        wa, wb, da, db = (terms[:, i : i + 1] for i in range(4))
        near = near_ref[h]
        far = far_ref[h, :count, :].astype(jnp.float32)
        oa, ob = near[:, :HD], far[:, :HD]
        out = wa * oa + wb * ob
        t_out = wa * near[:, HD:] + wb * far[:, HD:] + da * oa + db * ob
        both[0, :, h * HD : (h + 1) * HD] = out.astype(both.dtype)
        both[1, :, h * HD : (h + 1) * HD] = t_out.astype(both.dtype)
    rows = outs[0].shape[1]
    for step in range(4):
        at = pl.multiple_of(lax.rem(me_ref[0] + step, 4) * rows, 16)
        done = 0
        if before:
            done = before[step].shape[2]
            outs[step][:, :, :done] = before[step][...]
        outs[step][:, :, done:] = both[:, pl.ds(at, rows), :]


def merge(me, near, near_stat, far, *before):
    heads, rows, _ = near.shape
    width = heads * HD + (before[0].shape[2] if before else 0)
    whole = pl.BlockSpec(memory_space=pltpu.VMEM)
    return pl.pallas_call(
        merge_kernel,
        in_specs=[pl.BlockSpec(memory_space=pltpu.SMEM)] + [whole] * (3 + len(before)),
        out_specs=[whole] * 4,
        out_shape=[jax.ShapeDtypeStruct((2, rows // 4, width), jnp.bfloat16)] * 4,
        scratch_shapes=[pltpu.VMEM((2, rows, heads * HD), jnp.bfloat16)],
        compiler_params=pltpu.CompilerParams(vmem_limit_bytes=VMEM),
        cost_estimate=pl.CostEstimate(flops=1000, bytes_accessed=1000, transcendentals=0),
    )(me, near, near_stat, far, *before)


def pack_kernel(cut, q, t_q, k, t_k, v, t_v, first_ref, second_ref, q_ref):
    heads = q.shape[1] // HD
    for h in range(heads):
        cols = slice(h * HD, (h + 1) * HD)
        out, at = (first_ref, h) if h < cut else (second_ref, h - cut)
        for i, ref in enumerate((k, t_k, v, t_v)):
            out[at, :, i * HD : (i + 1) * HD] = ref[:, cols]
        q_ref[h, :, :HD] = q[:, cols]
        q_ref[h, :, HD:] = t_q[:, cols]


def pack(cut, *arrays):
    rows, width = arrays[0].shape
    heads = width // HD
    whole = pl.BlockSpec(memory_space=pltpu.VMEM)
    return pl.pallas_call(
        functools.partial(pack_kernel, cut),
        in_specs=[whole] * 6,
        out_specs=[whole] * 3,
        out_shape=[
            jax.ShapeDtypeStruct((cut, rows, 4 * HD), jnp.bfloat16),
            jax.ShapeDtypeStruct((heads - cut, rows, 4 * HD), jnp.bfloat16),
            jax.ShapeDtypeStruct((heads, rows, 2 * HD), jnp.bfloat16),
        ],
        compiler_params=pltpu.CompilerParams(vmem_limit_bytes=VMEM),
        cost_estimate=pl.CostEstimate(flops=1000, bytes_accessed=1000, transcendentals=0),
    )(*arrays)


def project_kernel(place_ref, *refs):
    atts, (gate, t_gate, stream_in, t_stream_in, weight) = refs[:4], refs[4:9]
    pieces = refs[9:29]
    result, t_result, att, streams, slots, stream_sems, sems = refs[29:]
    rows = stream_in.shape[0]
    depth = weight.shape[0]
    core = place_ref[0]

    def copy(slot, step, source):
        return pltpu.make_async_copy(
            source, slots.at[slot, pl.ds(step * depth, depth), :], sems.at[slot, step]
        )

    copies = []
    for slot in range(8):
        half, lot = divmod(slot, 4)
        mine = pieces[10 * half : 10 * half + 10]
        far = mine[6:]
        col = pl.multiple_of((lax.rem(core + half, 2) * 4 + lot) * WIDE, WIDE)
        copy(slot, 0, weight.at[:, pl.ds(col, WIDE)]).start()
        for way in range(2):
            chunk = mine[2 * ((lot + 1) // 2) + way]
            at = WIDE if lot == 2 else 0
            copy(slot, 1 + way, chunk.at[:, at : at + WIDE]).start()
        for i in range(4):

            @pl.when(place_ref[1 + i] == lot)
            def _():
                copy(slot, 3, far[i]).start()

        if slot == 0:
            moves = [
                pltpu.make_async_copy(source, streams.at[i], stream_sems.at[i])
                for i, source in enumerate((stream_in, t_stream_in))
            ]
            for move in moves:
                move.start()
        copies.append((slot, col, far[0]))
    at = 0
    for ref in atts:
        size = ref.shape[2]
        att[:rows, at : at + size] = ref[0]
        att[rows:, at : at + size] = ref[1]
        at += size
    for move in moves:
        move.wait()
    for slot, col, like in copies:
        for step in range(4):
            copy(slot, step, like).wait()
        sums = jnp.dot(att[...], slots[slot], preferred_element_type=jnp.float32)
        branch, t_branch = sums[:rows], sums[rows:]
        cols = pl.ds(col, WIDE)
        g = gate[:, cols].astype(jnp.float32)
        tg = t_gate[:, cols].astype(jnp.float32)
        result[:, cols] = (streams[0, :, cols].astype(jnp.float32) + g * branch).astype(
            result.dtype
        )
        t_result[:, cols] = (
            streams[1, :, cols].astype(jnp.float32) + tg * branch + g * t_branch
        ).astype(t_result.dtype)


def project(place, atts, stream, t_stream, gate, t_gate, weight, pieces):
    rows, columns = stream.shape
    depth = weight.shape[0]
    whole = pl.BlockSpec(memory_space=pltpu.VMEM)
    away = pl.BlockSpec(memory_space=pl.ANY)
    return pl.pallas_call(
        project_kernel,
        in_specs=[pl.BlockSpec(memory_space=pltpu.SMEM)]
        + [whole] * (len(atts) + 2)
        + [away] * (3 + len(pieces)),
        out_specs=[whole] * 2,
        out_shape=[jax.ShapeDtypeStruct((rows, columns), stream.dtype)] * 2,
        scratch_shapes=[
            pltpu.VMEM((2 * rows, 4 * depth), jnp.bfloat16),
            pltpu.VMEM((2, rows, columns), jnp.bfloat16),
            pltpu.VMEM((8, 4 * depth, WIDE), jnp.bfloat16),
            pltpu.SemaphoreType.DMA((2,)),
            pltpu.SemaphoreType.DMA((8, 4)),
        ],
        compiler_params=pltpu.CompilerParams(vmem_limit_bytes=VMEM),
        cost_estimate=pl.CostEstimate(flops=1000, bytes_accessed=1000, transcendentals=0),
    )(place, *atts, gate, t_gate, stream, t_stream, weight, *pieces)


def on_device(
    queries, keys, values, t_queries, t_keys, t_values, out_weight, stream, t_stream, gate, t_gate
):
    heads = queries.shape[1] // HD
    depth = out_weight.shape[0]
    half_width = out_weight.shape[1] // 2
    cut = heads - 1
    core, side, me = lax.axis_index("core"), lax.axis_index("xl"), lax.axis_index("head")
    x = 2 * lax.axis_index("dp") + side
    places = [x, x ^ 1, 3 - x, 3 - (x ^ 1)]

    def quarter(place, count=1):
        return lax.dynamic_slice(
            out_weight, (0, core * half_width + place * WIDE), (depth, count * WIDE)
        )

    def tie(value, *earlier):
        return lax.optimization_barrier((value, *earlier))[0]

    def neighbours(lot, *earlier, count=1):
        value = quarter(lot, count)
        if earlier:
            value = tie(value, *earlier)
        return shift(value, "head", 1), shift(value, "head", -1)

    def other_core(*pieces):
        return [shift(piece, "core", 1) for piece in pieces]

    lot_a, lot_b, near_q = pack(cut, queries, t_queries, keys, t_keys, values, t_values)
    kv_a = lax.all_gather(lot_a, ("z", "core"))
    kv_b = lax.all_gather(lot_b, ("z", "core"))
    far_q = shift(near_q, "xl", 1)
    gates = gate.reshape(1, -1), t_gate.reshape(1, -1)
    place = jnp.stack([core, *places]).astype(jnp.int32)
    where = me.astype(jnp.int32).reshape(1)

    far0 = tie(shift(quarter(places[0]), "head", 2), far_q)
    first = neighbours(0)
    far1, far2 = shift(far0, "xl", 1), swap_parts(far0)
    second = neighbours(1, *first, far1, far2, count=2)
    first2, fars = other_core(*first), other_core(far0)
    far3 = swap_parts(far1)

    (far_a,) = attend(
        [tie(far_q, *first2, *fars, far1, far2, *gates, place, where)], 0, kv_a, [True]
    )
    sent_a = shift(far_a, "xl", 1)
    near_a = attend([tie(near_q, far_a)], 0, kv_a, [False])
    fars += other_core(*tie((far1, far2), far_a))
    third = neighbours(3, *tie(second, near_a[1]))
    second2 = other_core(*tie(second, near_a[1]))
    far_b, *near_b = attend([tie(far_q, near_a[1], *second), near_q], cut, kv_b, [True, False])
    sent_b = shift(far_b, "xl", 1)
    fars += other_core(tie(far3, near_a[1]))
    owners_a = merge(tie(where, far_b), *near_a, sent_a)
    owners = merge(tie(where, *second2, *fars), *near_b, sent_b, *owners_a)
    moved = [owners[0]] + [shift(owners[step], "head", step) for step in (1, 2, 3)]
    third2 = other_core(*tie(third, owners[0]))
    atts = [moved[step] for step in (0, 1, 3, 2)]
    pieces = [*first, *second, *third, far0, far1, far2, far3]
    pieces += [*first2, *second2, *third2, *fars]
    return project(place, atts, stream, t_stream, *gates, out_weight, pieces)


def solution(mesh):
    fine = Mesh(
        mesh.devices.reshape(SIZES["xl"], SIZES["z"], SIZES["core"], SIZES["head"], -1),
        ("xl", "z", "core", "head", "dp"),
    )
    tokens = ("dp", "xl", "z", "core")
    spread = P(tokens, "head")
    rows = P((*tokens, "head"), None)
    return jax.shard_map(
        on_device,
        mesh=fine,
        in_specs=(spread,) * 6 + (P("head", None), rows, rows, P(), P()),
        out_specs=(rows, rows),
        check_vma=False,
    )
```

```python
import functools

import jax
import jax.numpy as jnp
from jax import lax
from jax.experimental import pallas as pl
from jax.experimental.pallas import tpu as pltpu
from jax.sharding import Mesh
from jax.sharding import PartitionSpec as P

HD = 128
LOG2E = 1.4426950408889634
SCALE = HD**-0.5
CHUNK = 512
SIZES = {"xl": 2, "z": 4, "core": 2, "head": 4}
WIDE = 640
VMEM = 60 * 1024 * 1024


def shift(value, axis, step):
    size = SIZES[axis]
    return lax.ppermute(value, axis, [(i, (i + step) % size) for i in range(size)])


def swap_parts(value):
    return lax.ppermute(value, ("xl", "dp"), [(1, 2), (2, 1), (3, 0), (0, 3)])


def attend_kernel(sent, *refs):
    count = len(sent)
    queries, kv = refs[:count], refs[count]
    *outs, kk, vv, scores = refs[count + 1 :]
    blocks, _, size, _ = kv.shape
    keys = blocks * size
    for i in range(blocks):
        kk[i * size : (i + 1) * size, :] = kv[i, 0, :, : 2 * HD]
        vv[i * size : (i + 1) * size, :] = kv[i, 0, :, 2 * HD :]
    across = (((1,), (1,)), ((), ()))
    size = queries[0].shape[1]
    rows = count * size
    query = jnp.concatenate([q[0, :, :HD] for q in queries], axis=0)
    mixed = jnp.concatenate([q[0, :, HD:] for q in queries], axis=0)
    mixed = jnp.concatenate([mixed, query], axis=1)
    peak = None
    for c in range(0, keys, CHUNK):
        s = lax.dot_general(
            query, kk[c : c + CHUNK, :HD], across, preferred_element_type=jnp.float32
        )
        scores[:, c : c + CHUNK] = s
        for lane in range(0, CHUNK, 128):
            part = s[:, lane : lane + 128]
            peak = part if peak is None else jnp.maximum(peak, part)
    top = jnp.max(peak, axis=1, keepdims=True) * (SCALE * LOG2E)
    den = jnp.zeros((rows, 128), jnp.float32)
    mass = jnp.zeros((rows, 128), jnp.float32)
    wide = jnp.zeros((rows, 2 * HD), jnp.float32)
    tilt = jnp.zeros((rows, HD), jnp.float32)
    for c in range(0, keys, CHUNK):
        slope = lax.dot_general(
            mixed, kk[c : c + CHUNK, :], across, preferred_element_type=jnp.float32
        )
        w = jnp.exp2(scores[:, c : c + CHUNK] * (SCALE * LOG2E) - top)
        g = w * slope
        for lane in range(0, CHUNK, 128):
            den = den + w[:, lane : lane + 128]
            mass = mass + g[:, lane : lane + 128]
        wide = wide + jnp.dot(
            w.astype(jnp.bfloat16), vv[c : c + CHUNK, :], preferred_element_type=jnp.float32
        )
        tilt = tilt + jnp.dot(
            g.astype(jnp.bfloat16), vv[c : c + CHUNK, :HD], preferred_element_type=jnp.float32
        )
    den = jnp.sum(den, axis=1, keepdims=True)
    inverse = 1.0 / den
    mean = jnp.sum(mass, axis=1, keepdims=True) * (inverse * SCALE)
    out = wide[:, :HD] * inverse
    t_out = (tilt * SCALE + wide[:, HD:]) * inverse - mean * out
    lane = lax.broadcasted_iota(jnp.int32, (rows, 128), 1)
    both = jnp.where(lane == 0, top + jnp.log2(den), mean)
    outs = list(outs)
    for i, goes in enumerate(sent):
        mine = slice(i * size, (i + 1) * size)
        ref = outs.pop(0)
        ref[0, :size, :HD] = out[mine].astype(ref.dtype)
        ref[0, :size, HD:] = t_out[mine].astype(ref.dtype)
        stats = jnp.transpose(both[mine])
        if not goes:
            outs.pop(0)[0] = stats[:8, :]
            continue
        stats = stats[:2, :]
        high = stats.astype(jnp.bfloat16).astype(jnp.float32)
        middle = (stats - high).astype(jnp.bfloat16).astype(jnp.float32)
        low = stats - high - middle
        terms = jnp.concatenate([high, middle, low, jnp.zeros_like(low)], axis=0)
        over = 2 * HD
        rest = jnp.concatenate(
            [terms[:, over:], jnp.zeros((8, 2 * over - size), jnp.float32)], axis=1
        )
        ref[0, size:, :] = jnp.concatenate([terms[:, :over], rest], axis=0).astype(jnp.bfloat16)


def attend(queries, first, kv, sent):
    rows = queries[0].shape[1]
    blocks, heads, size, _ = kv.shape
    keys = blocks * size

    def spec(r, c, at=0):
        return pl.BlockSpec((1, r, c), lambda h: (h + at, 0, 0))

    specs, shapes = [], []
    for goes in sent:
        if goes:
            specs += [spec(rows + 16, 2 * HD)]
            shapes += [jax.ShapeDtypeStruct((heads, rows + 16, 2 * HD), jnp.bfloat16)]
        else:
            specs += [spec(rows, 2 * HD), spec(8, rows)]
            shapes += [
                jax.ShapeDtypeStruct((heads, rows, 2 * HD), jnp.float32),
                jax.ShapeDtypeStruct((heads, 8, rows), jnp.float32),
            ]
    total = len(sent) * rows
    return pl.pallas_call(
        functools.partial(attend_kernel, sent),
        grid=(heads,),
        in_specs=[spec(rows, 2 * HD, first)] * len(sent)
        + [pl.BlockSpec((blocks, 1, size, 4 * HD), lambda h: (0, h, 0, 0))],
        out_specs=specs,
        out_shape=shapes,
        scratch_shapes=[
            pltpu.VMEM((keys, 2 * HD), jnp.bfloat16),
            pltpu.VMEM((keys, 2 * HD), jnp.bfloat16),
            pltpu.VMEM((total, keys), jnp.float32),
        ],
        compiler_params=pltpu.CompilerParams(vmem_limit_bytes=VMEM),
        cost_estimate=pl.CostEstimate(
            flops=heads * total * keys * HD * 12, bytes_accessed=1000, transcendentals=0
        ),
    )(*queries, kv)


def merge_kernel(me_ref, near_ref, near_stat, far_ref, *refs):
    before, (*outs, both) = refs[:-5], refs[-5:]
    heads, count, _ = near_ref.shape
    for h in range(heads):
        lse_a, mean_a = near_stat[h, 0:1, :], near_stat[h, 1:2, :]
        terms = far_ref[h, count:, :].astype(jnp.float32)
        terms = jnp.concatenate([terms[:8], terms[8:, : count - 2 * HD]], axis=1)
        lse_b = terms[0:1] + terms[2:3] + terms[4:5]
        mean_b = terms[1:2] + terms[3:4] + terms[5:6]
        top = jnp.maximum(lse_a, lse_b)
        wa = jnp.exp2(lse_a - top)
        wb = jnp.exp2(lse_b - top)
        inverse = 1.0 / (wa + wb)
        wa = wa * inverse
        wb = wb * inverse
        mean = wa * mean_a + wb * mean_b
        terms = [wa, wb, wa * (mean_a - mean), wb * (mean_b - mean)]
        terms = jnp.transpose(jnp.concatenate(terms + terms, axis=0))
        wa, wb, da, db = (terms[:, i : i + 1] for i in range(4))
        near = near_ref[h]
        far = far_ref[h, :count, :].astype(jnp.float32)
        oa, ob = near[:, :HD], far[:, :HD]
        out = wa * oa + wb * ob
        t_out = wa * near[:, HD:] + wb * far[:, HD:] + da * oa + db * ob
        both[0, :, h * HD : (h + 1) * HD] = out.astype(both.dtype)
        both[1, :, h * HD : (h + 1) * HD] = t_out.astype(both.dtype)
    rows = outs[0].shape[1]
    for step in range(4):
        at = pl.multiple_of(lax.rem(me_ref[0] + step, 4) * rows, 16)
        done = 0
        if before:
            done = before[step].shape[2]
            outs[step][:, :, :done] = before[step][...]
        outs[step][:, :, done:] = both[:, pl.ds(at, rows), :]


def merge(me, near, near_stat, far, *before):
    heads, rows, _ = near.shape
    width = heads * HD + (before[0].shape[2] if before else 0)
    whole = pl.BlockSpec(memory_space=pltpu.VMEM)
    return pl.pallas_call(
        merge_kernel,
        in_specs=[pl.BlockSpec(memory_space=pltpu.SMEM)] + [whole] * (3 + len(before)),
        out_specs=[whole] * 4,
        out_shape=[jax.ShapeDtypeStruct((2, rows // 4, width), jnp.bfloat16)] * 4,
        scratch_shapes=[pltpu.VMEM((2, rows, heads * HD), jnp.bfloat16)],
        compiler_params=pltpu.CompilerParams(vmem_limit_bytes=VMEM),
        cost_estimate=pl.CostEstimate(flops=1000, bytes_accessed=1000, transcendentals=0),
    )(me, near, near_stat, far, *before)


def pack_kernel(cut, q, t_q, k, t_k, v, t_v, first_ref, second_ref, q_ref):
    heads = q.shape[1] // HD
    for h in range(heads):
        cols = slice(h * HD, (h + 1) * HD)
        out, at = (first_ref, h) if h < cut else (second_ref, h - cut)
        for i, ref in enumerate((k, t_k, v, t_v)):
            out[at, :, i * HD : (i + 1) * HD] = ref[:, cols]
        q_ref[h, :, :HD] = q[:, cols]
        q_ref[h, :, HD:] = t_q[:, cols]


def pack(cut, *arrays):
    rows, width = arrays[0].shape
    heads = width // HD
    whole = pl.BlockSpec(memory_space=pltpu.VMEM)
    return pl.pallas_call(
        functools.partial(pack_kernel, cut),
        in_specs=[whole] * 6,
        out_specs=[whole] * 3,
        out_shape=[
            jax.ShapeDtypeStruct((cut, rows, 4 * HD), jnp.bfloat16),
            jax.ShapeDtypeStruct((heads - cut, rows, 4 * HD), jnp.bfloat16),
            jax.ShapeDtypeStruct((heads, rows, 2 * HD), jnp.bfloat16),
        ],
        compiler_params=pltpu.CompilerParams(vmem_limit_bytes=VMEM),
        cost_estimate=pl.CostEstimate(flops=1000, bytes_accessed=1000, transcendentals=0),
    )(*arrays)


def project_kernel(parts, place_ref, *refs):
    atts, refs = refs[:parts], refs[parts:]
    stream, t_stream, gate, t_gate, weight = refs[:5]
    pieces = refs[5:25]
    result, t_result, att, narrow, broad, sems = refs[25:]
    rows = stream.shape[0]
    depth = weight.shape[0]
    core = place_ref[0]
    steps = []
    for half in range(2):
        mine = pieces[10 * half : 10 * half + 10]
        far = mine[6:]
        for chunk, (lot, count) in enumerate(((0, 1), (1, 2), (3, 1))):
            slot = broad.at[half] if count == 2 else narrow.at[2 * half + chunk // 2]
            sem = sems.at[3 * half + chunk]
            col = pl.multiple_of((lax.rem(core + half, 2) * 4 + lot) * WIDE, WIDE)
            sources = (weight.at[:, pl.ds(col, count * WIDE)], *mine[2 * chunk : 2 * chunk + 2])
            group = [
                pltpu.make_async_copy(source, slot.at[pl.ds(i * depth, depth), :], sem.at[i])
                for i, source in enumerate(sources)
            ]
            for move in group:
                move.start()
            for j in range(count):
                to = slot.at[pl.ds(3 * depth, depth), pl.ds(j * WIDE, WIDE)]
                for i in range(4):

                    @pl.when(place_ref[1 + i] == lot + j)
                    def _():
                        pltpu.make_async_copy(far[i], to, sem.at[3 + j]).start()

                group.append(pltpu.make_async_copy(far[0], to, sem.at[3 + j]))
            steps.append((slot, col, count * WIDE, group))
    at = 0
    for ref in atts:
        size = ref.shape[2]
        att[:rows, at : at + size] = ref[0]
        att[rows:, at : at + size] = ref[1]
        at += size
    for slot, col, width, group in steps:
        for move in group:
            move.wait()
        sums = jnp.dot(att[...], slot[...], preferred_element_type=jnp.float32)
        branch, t_branch = sums[:rows], sums[rows:]
        cols = pl.ds(col, width)
        g = gate[:, cols].astype(jnp.float32)
        tg = t_gate[:, cols].astype(jnp.float32)
        result[:, cols] = (stream[:, cols].astype(jnp.float32) + g * branch).astype(result.dtype)
        t_result[:, cols] = (
            t_stream[:, cols].astype(jnp.float32) + tg * branch + g * t_branch
        ).astype(t_result.dtype)


def project(place, atts, stream, t_stream, gate, t_gate, weight, pieces):
    rows, columns = stream.shape
    depth = weight.shape[0]
    whole = pl.BlockSpec(memory_space=pltpu.VMEM)
    away = pl.BlockSpec(memory_space=pl.ANY)
    return pl.pallas_call(
        functools.partial(project_kernel, len(atts)),
        in_specs=[pl.BlockSpec(memory_space=pltpu.SMEM)]
        + [whole] * (len(atts) + 4)
        + [away] * (1 + len(pieces)),
        out_specs=[whole] * 2,
        out_shape=[jax.ShapeDtypeStruct((rows, columns), stream.dtype)] * 2,
        scratch_shapes=[
            pltpu.VMEM((2 * rows, 4 * depth), jnp.bfloat16),
            pltpu.VMEM((4, 4 * depth, WIDE), jnp.bfloat16),
            pltpu.VMEM((2, 4 * depth, 2 * WIDE), jnp.bfloat16),
            pltpu.SemaphoreType.DMA((6, 5)),
        ],
        compiler_params=pltpu.CompilerParams(vmem_limit_bytes=VMEM),
        cost_estimate=pl.CostEstimate(flops=1000, bytes_accessed=1000, transcendentals=0),
    )(place, *atts, stream, t_stream, gate, t_gate, weight, *pieces)


def on_device(
    queries, keys, values, t_queries, t_keys, t_values, out_weight, stream, t_stream, gate, t_gate
):
    heads = queries.shape[1] // HD
    depth = out_weight.shape[0]
    half_width = out_weight.shape[1] // 2
    cut = heads - 1
    core, side, me = lax.axis_index("core"), lax.axis_index("xl"), lax.axis_index("head")
    x = 2 * lax.axis_index("dp") + side
    places = [x, x ^ 1, 3 - x, 3 - (x ^ 1)]

    def quarter(place, count=1):
        return lax.dynamic_slice(
            out_weight, (0, core * half_width + place * WIDE), (depth, count * WIDE)
        )

    def tie(value, *earlier):
        return lax.optimization_barrier((value, *earlier))[0]

    def neighbours(lot, *earlier, count=1):
        value = quarter(lot, count)
        if earlier:
            value = tie(value, *earlier)
        return shift(value, "head", 1), shift(value, "head", -1)

    def other_core(*pieces):
        return [shift(piece, "core", 1) for piece in pieces]

    lot_a, lot_b, near_q = pack(cut, queries, t_queries, keys, t_keys, values, t_values)
    kv_a = lax.all_gather(lot_a, ("z", "core"))
    kv_b = lax.all_gather(lot_b, ("z", "core"))
    far_q = shift(near_q, "xl", 1)
    gates = gate.reshape(1, -1), t_gate.reshape(1, -1)
    place = jnp.stack([core, *places]).astype(jnp.int32)
    where = me.astype(jnp.int32).reshape(1)

    far0 = tie(shift(quarter(places[0]), "head", 2), far_q)
    first = neighbours(0)
    far1, far2 = shift(far0, "xl", 1), swap_parts(far0)
    second = neighbours(1, *first, far1, far2, count=2)
    first2, fars = other_core(*first), other_core(far0)
    far3 = swap_parts(far1)

    (far_a,) = attend(
        [tie(far_q, *first2, *fars, far1, far2, *gates, place, where)], 0, kv_a, [True]
    )
    sent_a = shift(far_a, "xl", 1)
    near_a = attend([tie(near_q, far_a)], 0, kv_a, [False])
    fars += other_core(*tie((far1, far2), far_a))
    third = neighbours(3, *tie(second, near_a[1]))
    second2 = other_core(*tie(second, near_a[1]))
    far_b, *near_b = attend([tie(far_q, near_a[1], *second), near_q], cut, kv_b, [True, False])
    sent_b = shift(far_b, "xl", 1)
    fars += other_core(tie(far3, near_a[1]))
    owners_a = merge(tie(where, far_b), *near_a, sent_a)
    owners = merge(tie(where, *second2, *fars), *near_b, sent_b, *owners_a)
    moved = [owners[0]] + [shift(owners[step], "head", step) for step in (1, 2, 3)]
    third2 = other_core(*tie(third, owners[0]))
    atts = [moved[step] for step in (0, 1, 3, 2)]
    pieces = [*first, *second, *third, far0, far1, far2, far3]
    pieces += [*first2, *second2, *third2, *fars]
    return project(place, atts, stream, t_stream, *gates, out_weight, pieces)


def solution(mesh):
    fine = Mesh(
        mesh.devices.reshape(SIZES["xl"], SIZES["z"], SIZES["core"], SIZES["head"], -1),
        ("xl", "z", "core", "head", "dp"),
    )
    tokens = ("dp", "xl", "z", "core")
    spread = P(tokens, "head")
    rows = P((*tokens, "head"), None)
    return jax.shard_map(
        on_device,
        mesh=fine,
        in_specs=(spread,) * 6 + (P("head", None), rows, rows, P(), P()),
        out_specs=(rows, rows),
        check_vma=False,
    )
```

```python
import functools

import jax
import jax.numpy as jnp
from jax import lax
from jax.experimental import pallas as pl
from jax.experimental.pallas import tpu as pltpu
from jax.sharding import Mesh
from jax.sharding import PartitionSpec as P

HD = 128
LOG2E = 1.4426950408889634
SCALE = HD**-0.5
CHUNK = 512
SIZES = {"xl": 2, "z": 4, "core": 2, "head": 4}
WIDE = 640
VMEM = 60 * 1024 * 1024


def shift(value, axis, step):
    size = SIZES[axis]
    return lax.ppermute(value, axis, [(i, (i + step) % size) for i in range(size)])


def swap_parts(value):
    return lax.ppermute(value, ("xl", "dp"), [(1, 2), (2, 1), (3, 0), (0, 3)])


def attend_kernel(sent, *refs):
    count = len(sent)
    queries, kv = refs[:count], refs[count]
    *outs, kk, vv, scores = refs[count + 1 :]
    blocks, _, size, _ = kv.shape
    keys = blocks * size
    for i in range(blocks):
        kk[i * size : (i + 1) * size, :] = kv[i, 0, :, : 2 * HD]
        vv[i * size : (i + 1) * size, :] = kv[i, 0, :, 2 * HD :]
    across = (((1,), (1,)), ((), ()))
    size = queries[0].shape[1]
    rows = count * size
    query = jnp.concatenate([q[0, :, :HD] for q in queries], axis=0)
    mixed = jnp.concatenate([q[0, :, HD:] for q in queries], axis=0)
    mixed = jnp.concatenate([mixed, query], axis=1)
    peak = None
    for c in range(0, keys, CHUNK):
        s = lax.dot_general(
            query, kk[c : c + CHUNK, :HD], across, preferred_element_type=jnp.float32
        )
        scores[:, c : c + CHUNK] = s
        for lane in range(0, CHUNK, 128):
            part = s[:, lane : lane + 128]
            peak = part if peak is None else jnp.maximum(peak, part)
    top = jnp.max(peak, axis=1, keepdims=True) * (SCALE * LOG2E)
    den = jnp.zeros((rows, 128), jnp.float32)
    mass = jnp.zeros((rows, 128), jnp.float32)
    wide = jnp.zeros((rows, 2 * HD), jnp.float32)
    tilt = jnp.zeros((rows, HD), jnp.float32)
    for c in range(0, keys, CHUNK):
        slope = lax.dot_general(
            mixed, kk[c : c + CHUNK, :], across, preferred_element_type=jnp.float32
        )
        w = jnp.exp2(scores[:, c : c + CHUNK] * (SCALE * LOG2E) - top)
        g = w * slope
        for lane in range(0, CHUNK, 128):
            den = den + w[:, lane : lane + 128]
            mass = mass + g[:, lane : lane + 128]
        wide = wide + jnp.dot(
            w.astype(jnp.bfloat16), vv[c : c + CHUNK, :], preferred_element_type=jnp.float32
        )
        tilt = tilt + jnp.dot(
            g.astype(jnp.bfloat16), vv[c : c + CHUNK, :HD], preferred_element_type=jnp.float32
        )
    den = jnp.sum(den, axis=1, keepdims=True)
    inverse = 1.0 / den
    mean = jnp.sum(mass, axis=1, keepdims=True) * (inverse * SCALE)
    out = wide[:, :HD] * inverse
    t_out = (tilt * SCALE + wide[:, HD:]) * inverse - mean * out
    lane = lax.broadcasted_iota(jnp.int32, (rows, 128), 1)
    both = jnp.where(lane == 0, top + jnp.log2(den), mean)
    outs = list(outs)
    for i, goes in enumerate(sent):
        mine = slice(i * size, (i + 1) * size)
        ref = outs.pop(0)
        ref[0, :size, :HD] = out[mine].astype(ref.dtype)
        ref[0, :size, HD:] = t_out[mine].astype(ref.dtype)
        stats = jnp.transpose(both[mine])
        if not goes:
            outs.pop(0)[0] = stats[:8, :]
            continue
        stats = stats[:2, :]
        high = stats.astype(jnp.bfloat16).astype(jnp.float32)
        middle = (stats - high).astype(jnp.bfloat16).astype(jnp.float32)
        low = stats - high - middle
        terms = jnp.concatenate([high, middle, low, jnp.zeros_like(low)], axis=0)
        over = 2 * HD
        rest = jnp.concatenate(
            [terms[:, over:], jnp.zeros((8, 2 * over - size), jnp.float32)], axis=1
        )
        ref[0, size:, :] = jnp.concatenate([terms[:, :over], rest], axis=0).astype(jnp.bfloat16)


def attend(queries, first, kv, sent):
    rows = queries[0].shape[1]
    blocks, heads, size, _ = kv.shape
    keys = blocks * size

    def spec(r, c, at=0):
        return pl.BlockSpec((1, r, c), lambda h: (h + at, 0, 0))

    specs, shapes = [], []
    for goes in sent:
        if goes:
            specs += [spec(rows + 16, 2 * HD)]
            shapes += [jax.ShapeDtypeStruct((heads, rows + 16, 2 * HD), jnp.bfloat16)]
        else:
            specs += [spec(rows, 2 * HD), spec(8, rows)]
            shapes += [
                jax.ShapeDtypeStruct((heads, rows, 2 * HD), jnp.float32),
                jax.ShapeDtypeStruct((heads, 8, rows), jnp.float32),
            ]
    total = len(sent) * rows
    return pl.pallas_call(
        functools.partial(attend_kernel, sent),
        grid=(heads,),
        in_specs=[spec(rows, 2 * HD, first)] * len(sent)
        + [pl.BlockSpec((blocks, 1, size, 4 * HD), lambda h: (0, h, 0, 0))],
        out_specs=specs,
        out_shape=shapes,
        scratch_shapes=[
            pltpu.VMEM((keys, 2 * HD), jnp.bfloat16),
            pltpu.VMEM((keys, 2 * HD), jnp.bfloat16),
            pltpu.VMEM((total, keys), jnp.float32),
        ],
        compiler_params=pltpu.CompilerParams(vmem_limit_bytes=VMEM),
        cost_estimate=pl.CostEstimate(
            flops=heads * total * keys * HD * 12, bytes_accessed=1000, transcendentals=0
        ),
    )(*queries, kv)


def merge_kernel(me_ref, near_ref, near_stat, far_ref, *refs):
    before, (*outs, both) = refs[:-5], refs[-5:]
    heads, count, _ = near_ref.shape
    for h in range(heads):
        lse_a, mean_a = near_stat[h, 0:1, :], near_stat[h, 1:2, :]
        terms = far_ref[h, count:, :].astype(jnp.float32)
        terms = jnp.concatenate([terms[:8], terms[8:, : count - 2 * HD]], axis=1)
        lse_b = terms[0:1] + terms[2:3] + terms[4:5]
        mean_b = terms[1:2] + terms[3:4] + terms[5:6]
        top = jnp.maximum(lse_a, lse_b)
        wa = jnp.exp2(lse_a - top)
        wb = jnp.exp2(lse_b - top)
        inverse = 1.0 / (wa + wb)
        wa = wa * inverse
        wb = wb * inverse
        mean = wa * mean_a + wb * mean_b
        terms = [wa, wb, wa * (mean_a - mean), wb * (mean_b - mean)]
        terms = jnp.transpose(jnp.concatenate(terms + terms, axis=0))
        wa, wb, da, db = (terms[:, i : i + 1] for i in range(4))
        near = near_ref[h]
        far = far_ref[h, :count, :].astype(jnp.float32)
        oa, ob = near[:, :HD], far[:, :HD]
        out = wa * oa + wb * ob
        t_out = wa * near[:, HD:] + wb * far[:, HD:] + da * oa + db * ob
        both[0, :, h * HD : (h + 1) * HD] = out.astype(both.dtype)
        both[1, :, h * HD : (h + 1) * HD] = t_out.astype(both.dtype)
    rows = outs[0].shape[1]
    for step in range(4):
        at = pl.multiple_of(lax.rem(me_ref[0] + step, 4) * rows, 16)
        done = 0
        if before:
            done = before[step].shape[2]
            outs[step][:, :, :done] = before[step][...]
        outs[step][:, :, done:] = both[:, pl.ds(at, rows), :]


def merge(me, near, near_stat, far, *before):
    heads, rows, _ = near.shape
    width = heads * HD + (before[0].shape[2] if before else 0)
    whole = pl.BlockSpec(memory_space=pltpu.VMEM)
    return pl.pallas_call(
        merge_kernel,
        in_specs=[pl.BlockSpec(memory_space=pltpu.SMEM)] + [whole] * (3 + len(before)),
        out_specs=[whole] * 4,
        out_shape=[jax.ShapeDtypeStruct((2, rows // 4, width), jnp.bfloat16)] * 4,
        scratch_shapes=[pltpu.VMEM((2, rows, heads * HD), jnp.bfloat16)],
        compiler_params=pltpu.CompilerParams(vmem_limit_bytes=VMEM),
        cost_estimate=pl.CostEstimate(flops=1000, bytes_accessed=1000, transcendentals=0),
    )(me, near, near_stat, far, *before)


def pack_kernel(cut, q, t_q, k, t_k, v, t_v, first_ref, second_ref, q_ref):
    heads = q.shape[1] // HD
    for h in range(heads):
        cols = slice(h * HD, (h + 1) * HD)
        out, at = (first_ref, h) if h < cut else (second_ref, h - cut)
        for i, ref in enumerate((k, t_k, v, t_v)):
            out[at, :, i * HD : (i + 1) * HD] = ref[:, cols]
        q_ref[h, :, :HD] = q[:, cols]
        q_ref[h, :, HD:] = t_q[:, cols]


def pack(cut, *arrays):
    rows, width = arrays[0].shape
    heads = width // HD
    whole = pl.BlockSpec(memory_space=pltpu.VMEM)
    return pl.pallas_call(
        functools.partial(pack_kernel, cut),
        in_specs=[whole] * 6,
        out_specs=[whole] * 3,
        out_shape=[
            jax.ShapeDtypeStruct((cut, rows, 4 * HD), jnp.bfloat16),
            jax.ShapeDtypeStruct((heads - cut, rows, 4 * HD), jnp.bfloat16),
            jax.ShapeDtypeStruct((heads, rows, 2 * HD), jnp.bfloat16),
        ],
        compiler_params=pltpu.CompilerParams(vmem_limit_bytes=VMEM),
        cost_estimate=pl.CostEstimate(flops=1000, bytes_accessed=1000, transcendentals=0),
    )(*arrays)


def project_kernel(parts, place_ref, *refs):
    atts, refs = refs[:parts], refs[parts:]
    stream, t_stream, gate, t_gate, weight = refs[:5]
    pieces = refs[5:25]
    result, t_result, att, narrow, broad, sems = refs[25:]
    rows = stream.shape[0]
    depth = weight.shape[0]
    core = place_ref[0]
    steps = []
    for half in range(2):
        mine = pieces[10 * half : 10 * half + 10]
        far = mine[6:]
        for chunk, (lot, count) in enumerate(((0, 1), (1, 2), (3, 1))):
            slot = broad.at[half] if count == 2 else narrow.at[2 * half + chunk // 2]
            sem = sems.at[3 * half + chunk]
            col = pl.multiple_of((lax.rem(core + half, 2) * 4 + lot) * WIDE, WIDE)
            sources = (weight.at[:, pl.ds(col, count * WIDE)], *mine[2 * chunk : 2 * chunk + 2])
            group = [
                pltpu.make_async_copy(source, slot.at[pl.ds(i * depth, depth), :], sem.at[i])
                for i, source in enumerate(sources)
            ]
            for move in group:
                move.start()
            for j in range(count):
                to = slot.at[pl.ds(3 * depth, depth), pl.ds(j * WIDE, WIDE)]
                for i in range(4):

                    @pl.when(place_ref[1 + i] == lot + j)
                    def _():
                        pltpu.make_async_copy(far[i], to, sem.at[3 + j]).start()

                group.append(pltpu.make_async_copy(far[0], to, sem.at[3 + j]))
            steps.append((slot, col, count * WIDE, group))
    at = 0
    for ref in atts:
        size = ref.shape[2]
        att[:rows, at : at + size] = ref[0]
        att[rows:, at : at + size] = ref[1]
        at += size
    for slot, col, width, group in steps:
        for move in group:
            move.wait()
        sums = jnp.dot(att[...], slot[...], preferred_element_type=jnp.float32)
        branch, t_branch = sums[:rows], sums[rows:]
        cols = pl.ds(col, width)
        g = gate[:, cols].astype(jnp.float32)
        tg = t_gate[:, cols].astype(jnp.float32)
        result[:, cols] = (stream[:, cols].astype(jnp.float32) + g * branch).astype(result.dtype)
        t_result[:, cols] = (
            t_stream[:, cols].astype(jnp.float32) + tg * branch + g * t_branch
        ).astype(t_result.dtype)


def project(place, atts, stream, t_stream, gate, t_gate, weight, pieces):
    rows, columns = stream.shape
    depth = weight.shape[0]
    whole = pl.BlockSpec(memory_space=pltpu.VMEM)
    away = pl.BlockSpec(memory_space=pl.ANY)
    return pl.pallas_call(
        functools.partial(project_kernel, len(atts)),
        in_specs=[pl.BlockSpec(memory_space=pltpu.SMEM)]
        + [whole] * (len(atts) + 4)
        + [away] * (1 + len(pieces)),
        out_specs=[whole] * 2,
        out_shape=[jax.ShapeDtypeStruct((rows, columns), stream.dtype)] * 2,
        scratch_shapes=[
            pltpu.VMEM((2 * rows, 4 * depth), jnp.bfloat16),
            pltpu.VMEM((4, 4 * depth, WIDE), jnp.bfloat16),
            pltpu.VMEM((2, 4 * depth, 2 * WIDE), jnp.bfloat16),
            pltpu.SemaphoreType.DMA((6, 5)),
        ],
        compiler_params=pltpu.CompilerParams(vmem_limit_bytes=VMEM),
        cost_estimate=pl.CostEstimate(flops=1000, bytes_accessed=1000, transcendentals=0),
    )(place, *atts, stream, t_stream, gate, t_gate, weight, *pieces)


def on_device(
    queries, keys, values, t_queries, t_keys, t_values, out_weight, stream, t_stream, gate, t_gate
):
    heads = queries.shape[1] // HD
    depth = out_weight.shape[0]
    half_width = out_weight.shape[1] // 2
    cut = heads - 1
    core, side, me = lax.axis_index("core"), lax.axis_index("xl"), lax.axis_index("head")
    x = 2 * lax.axis_index("dp") + side
    places = [x, x ^ 1, 3 - x, 3 - (x ^ 1)]

    def quarter(place, count=1):
        return lax.dynamic_slice(
            out_weight, (0, core * half_width + place * WIDE), (depth, count * WIDE)
        )

    def tie(value, *earlier):
        return lax.optimization_barrier((value, *earlier))[0]

    def neighbours(lot, *earlier, count=1):
        value = quarter(lot, count)
        if earlier:
            value = tie(value, *earlier)
        return shift(value, "head", 1), shift(value, "head", -1)

    def other_core(*pieces):
        return [shift(piece, "core", 1) for piece in pieces]

    lot_a, lot_b, near_q = pack(cut, queries, t_queries, keys, t_keys, values, t_values)
    kv_a = lax.all_gather(lot_a, ("z", "core"))
    kv_b = lax.all_gather(lot_b, ("z", "core"))
    far_q = shift(near_q, "xl", 1)
    gates = gate.reshape(1, -1), t_gate.reshape(1, -1)
    place = jnp.stack([core, *places]).astype(jnp.int32)
    where = me.astype(jnp.int32).reshape(1)

    far0 = tie(shift(quarter(places[0]), "head", 2), far_q)
    first = neighbours(0)
    far1, far2 = shift(far0, "xl", 1), swap_parts(far0)
    second = neighbours(1, *first, count=2)
    first2, fars = other_core(*first), other_core(far0)
    far3 = swap_parts(far1)

    (far_a,) = attend(
        [tie(far_q, *first2, *fars, *gates, place, where)], 0, kv_a, [True]
    )
    sent_a = shift(far_a, "xl", 1)
    near_a = attend([tie(near_q, far_a)], 0, kv_a, [False])
    fars += other_core(*tie((far1, far2), far_a))
    third = neighbours(3, *tie(second, near_a[1]))
    second2 = other_core(*tie(second, near_a[1]))
    far_b, *near_b = attend([tie(far_q, near_a[1], *second), near_q], cut, kv_b, [True, False])
    sent_b = shift(far_b, "xl", 1)
    fars += other_core(tie(far3, near_a[1]))
    owners_a = merge(tie(where, far_b), *near_a, sent_a)
    owners = merge(tie(where, *second2, *fars), *near_b, sent_b, *owners_a)
    moved = [owners[0]] + [shift(owners[step], "head", step) for step in (1, 2, 3)]
    third2 = other_core(*tie(third, owners[0]))
    atts = [moved[step] for step in (0, 1, 3, 2)]
    pieces = [*first, *second, *third, far0, far1, far2, far3]
    pieces += [*first2, *second2, *third2, *fars]
    return project(place, atts, stream, t_stream, *gates, out_weight, pieces)


def solution(mesh):
    fine = Mesh(
        mesh.devices.reshape(SIZES["xl"], SIZES["z"], SIZES["core"], SIZES["head"], -1),
        ("xl", "z", "core", "head", "dp"),
    )
    tokens = ("dp", "xl", "z", "core")
    spread = P(tokens, "head")
    rows = P((*tokens, "head"), None)
    return jax.shard_map(
        on_device,
        mesh=fine,
        in_specs=(spread,) * 6 + (P("head", None), rows, rows, P(), P()),
        out_specs=(rows, rows),
        check_vma=False,
    )
```

```python
import functools

import jax
import jax.numpy as jnp
from jax import lax
from jax.experimental import pallas as pl
from jax.experimental.pallas import tpu as pltpu
from jax.sharding import Mesh
from jax.sharding import PartitionSpec as P

HD = 128
LOG2E = 1.4426950408889634
SCALE = HD**-0.5
CHUNK = 512
SIZES = {"xl": 2, "z": 4, "core": 2, "head": 4}
WIDE = 640
VMEM = 60 * 1024 * 1024


def shift(value, axis, step):
    size = SIZES[axis]
    return lax.ppermute(value, axis, [(i, (i + step) % size) for i in range(size)])


def swap_parts(value):
    return lax.ppermute(value, ("xl", "dp"), [(1, 2), (2, 1), (3, 0), (0, 3)])


def attend_kernel(sent, *refs):
    count = len(sent)
    queries, kv = refs[:count], refs[count]
    *outs, kk, vv, scores = refs[count + 1 :]
    blocks, _, size, _ = kv.shape
    keys = blocks * size
    for i in range(blocks):
        kk[i * size : (i + 1) * size, :] = kv[i, 0, :, : 2 * HD]
        vv[i * size : (i + 1) * size, :] = kv[i, 0, :, 2 * HD :]
    across = (((1,), (1,)), ((), ()))
    size = queries[0].shape[1]
    rows = count * size
    query = jnp.concatenate([q[0, :, :HD] for q in queries], axis=0)
    mixed = jnp.concatenate([q[0, :, HD:] for q in queries], axis=0)
    mixed = jnp.concatenate([mixed, query], axis=1)
    peak = None
    for c in range(0, keys, CHUNK):
        s = lax.dot_general(
            query, kk[c : c + CHUNK, :HD], across, preferred_element_type=jnp.float32
        )
        scores[:, c : c + CHUNK] = s
        for lane in range(0, CHUNK, 128):
            part = s[:, lane : lane + 128]
            peak = part if peak is None else jnp.maximum(peak, part)
    top = jnp.max(peak, axis=1, keepdims=True) * (SCALE * LOG2E)
    den = jnp.zeros((rows, 128), jnp.float32)
    mass = jnp.zeros((rows, 128), jnp.float32)
    wide = jnp.zeros((rows, 2 * HD), jnp.float32)
    tilt = jnp.zeros((rows, HD), jnp.float32)
    for c in range(0, keys, CHUNK):
        slope = lax.dot_general(
            mixed, kk[c : c + CHUNK, :], across, preferred_element_type=jnp.float32
        )
        w = jnp.exp2(scores[:, c : c + CHUNK] * (SCALE * LOG2E) - top)
        g = w * slope
        for lane in range(0, CHUNK, 128):
            den = den + w[:, lane : lane + 128]
            mass = mass + g[:, lane : lane + 128]
        wide = wide + jnp.dot(
            w.astype(jnp.bfloat16), vv[c : c + CHUNK, :], preferred_element_type=jnp.float32
        )
        tilt = tilt + jnp.dot(
            g.astype(jnp.bfloat16), vv[c : c + CHUNK, :HD], preferred_element_type=jnp.float32
        )
    den = jnp.sum(den, axis=1, keepdims=True)
    inverse = 1.0 / den
    mean = jnp.sum(mass, axis=1, keepdims=True) * (inverse * SCALE)
    out = wide[:, :HD] * inverse
    t_out = (tilt * SCALE + wide[:, HD:]) * inverse - mean * out
    lane = lax.broadcasted_iota(jnp.int32, (rows, 128), 1)
    both = jnp.where(lane == 0, top + jnp.log2(den), mean)
    outs = list(outs)
    for i, goes in enumerate(sent):
        mine = slice(i * size, (i + 1) * size)
        ref = outs.pop(0)
        ref[0, :size, :HD] = out[mine].astype(ref.dtype)
        ref[0, :size, HD:] = t_out[mine].astype(ref.dtype)
        stats = jnp.transpose(both[mine])
        if not goes:
            outs.pop(0)[0] = stats[:8, :]
            continue
        stats = stats[:2, :]
        high = stats.astype(jnp.bfloat16).astype(jnp.float32)
        middle = (stats - high).astype(jnp.bfloat16).astype(jnp.float32)
        low = stats - high - middle
        terms = jnp.concatenate([high, middle, low, jnp.zeros_like(low)], axis=0)
        over = 2 * HD
        rest = jnp.concatenate(
            [terms[:, over:], jnp.zeros((8, 2 * over - size), jnp.float32)], axis=1
        )
        ref[0, size:, :] = jnp.concatenate([terms[:, :over], rest], axis=0).astype(jnp.bfloat16)


def attend(queries, first, kv, sent):
    rows = queries[0].shape[1]
    blocks, heads, size, _ = kv.shape
    keys = blocks * size

    def spec(r, c, at=0):
        return pl.BlockSpec((1, r, c), lambda h: (h + at, 0, 0))

    specs, shapes = [], []
    for goes in sent:
        if goes:
            specs += [spec(rows + 16, 2 * HD)]
            shapes += [jax.ShapeDtypeStruct((heads, rows + 16, 2 * HD), jnp.bfloat16)]
        else:
            specs += [spec(rows, 2 * HD), spec(8, rows)]
            shapes += [
                jax.ShapeDtypeStruct((heads, rows, 2 * HD), jnp.float32),
                jax.ShapeDtypeStruct((heads, 8, rows), jnp.float32),
            ]
    total = len(sent) * rows
    return pl.pallas_call(
        functools.partial(attend_kernel, sent),
        grid=(heads,),
        in_specs=[spec(rows, 2 * HD, first)] * len(sent)
        + [pl.BlockSpec((blocks, 1, size, 4 * HD), lambda h: (0, h, 0, 0))],
        out_specs=specs,
        out_shape=shapes,
        scratch_shapes=[
            pltpu.VMEM((keys, 2 * HD), jnp.bfloat16),
            pltpu.VMEM((keys, 2 * HD), jnp.bfloat16),
            pltpu.VMEM((total, keys), jnp.float32),
        ],
        compiler_params=pltpu.CompilerParams(vmem_limit_bytes=VMEM),
        cost_estimate=pl.CostEstimate(
            flops=heads * total * keys * HD * 12, bytes_accessed=1000, transcendentals=0
        ),
    )(*queries, kv)


def merge_kernel(me_ref, near_ref, near_stat, far_ref, *refs):
    before, (*outs, both) = refs[:-5], refs[-5:]
    heads, count, _ = near_ref.shape
    for h in range(heads):
        lse_a, mean_a = near_stat[h, 0:1, :], near_stat[h, 1:2, :]
        terms = far_ref[h, count:, :].astype(jnp.float32)
        terms = jnp.concatenate([terms[:8], terms[8:, : count - 2 * HD]], axis=1)
        lse_b = terms[0:1] + terms[2:3] + terms[4:5]
        mean_b = terms[1:2] + terms[3:4] + terms[5:6]
        top = jnp.maximum(lse_a, lse_b)
        wa = jnp.exp2(lse_a - top)
        wb = jnp.exp2(lse_b - top)
        inverse = 1.0 / (wa + wb)
        wa = wa * inverse
        wb = wb * inverse
        mean = wa * mean_a + wb * mean_b
        terms = [wa, wb, wa * (mean_a - mean), wb * (mean_b - mean)]
        terms = jnp.transpose(jnp.concatenate(terms + terms, axis=0))
        wa, wb, da, db = (terms[:, i : i + 1] for i in range(4))
        near = near_ref[h]
        far = far_ref[h, :count, :].astype(jnp.float32)
        oa, ob = near[:, :HD], far[:, :HD]
        out = wa * oa + wb * ob
        t_out = wa * near[:, HD:] + wb * far[:, HD:] + da * oa + db * ob
        both[0, :, h * HD : (h + 1) * HD] = out.astype(both.dtype)
        both[1, :, h * HD : (h + 1) * HD] = t_out.astype(both.dtype)
    rows = outs[0].shape[1]
    for step in range(4):
        at = pl.multiple_of(lax.rem(me_ref[0] + step, 4) * rows, 16)
        done = 0
        if before:
            done = before[step].shape[2]
            outs[step][:, :, :done] = before[step][...]
        outs[step][:, :, done:] = both[:, pl.ds(at, rows), :]


def merge(me, near, near_stat, far, *before):
    heads, rows, _ = near.shape
    width = heads * HD + (before[0].shape[2] if before else 0)
    whole = pl.BlockSpec(memory_space=pltpu.VMEM)
    return pl.pallas_call(
        merge_kernel,
        in_specs=[pl.BlockSpec(memory_space=pltpu.SMEM)] + [whole] * (3 + len(before)),
        out_specs=[whole] * 4,
        out_shape=[jax.ShapeDtypeStruct((2, rows // 4, width), jnp.bfloat16)] * 4,
        scratch_shapes=[pltpu.VMEM((2, rows, heads * HD), jnp.bfloat16)],
        compiler_params=pltpu.CompilerParams(vmem_limit_bytes=VMEM),
        cost_estimate=pl.CostEstimate(flops=1000, bytes_accessed=1000, transcendentals=0),
    )(me, near, near_stat, far, *before)


def pack_kernel(cut, q, t_q, k, t_k, v, t_v, first_ref, second_ref, q_ref):
    heads = q.shape[1] // HD
    for h in range(heads):
        cols = slice(h * HD, (h + 1) * HD)
        out, at = (first_ref, h) if h < cut else (second_ref, h - cut)
        for i, ref in enumerate((k, t_k, v, t_v)):
            out[at, :, i * HD : (i + 1) * HD] = ref[:, cols]
        q_ref[h, :, :HD] = q[:, cols]
        q_ref[h, :, HD:] = t_q[:, cols]


def pack(cut, *arrays):
    rows, width = arrays[0].shape
    heads = width // HD
    whole = pl.BlockSpec(memory_space=pltpu.VMEM)
    return pl.pallas_call(
        functools.partial(pack_kernel, cut),
        in_specs=[whole] * 6,
        out_specs=[whole] * 3,
        out_shape=[
            jax.ShapeDtypeStruct((cut, rows, 4 * HD), jnp.bfloat16),
            jax.ShapeDtypeStruct((heads - cut, rows, 4 * HD), jnp.bfloat16),
            jax.ShapeDtypeStruct((heads, rows, 2 * HD), jnp.bfloat16),
        ],
        compiler_params=pltpu.CompilerParams(vmem_limit_bytes=VMEM),
        cost_estimate=pl.CostEstimate(flops=1000, bytes_accessed=1000, transcendentals=0),
    )(*arrays)


def project_kernel(parts, place_ref, *refs):
    atts, refs = refs[:parts], refs[parts:]
    stream, t_stream, gate, t_gate, weight = refs[:5]
    pieces = refs[5:21]
    result, t_result, att, narrow, broad, sems = refs[21:]
    rows = stream.shape[0]
    depth = weight.shape[0]
    core = place_ref[0]
    steps = []
    for chunk, lot, count in ((1, 1, 3), (0, 0, 1)):
        for half in range(2):
            mine = pieces[8 * half : 8 * half + 8]
            far = mine[4:]
            slot = (narrow, broad)[chunk].at[half]
            sem = sems.at[2 * half + chunk]
            col = pl.multiple_of((lax.rem(core + half, 2) * 4 + lot) * WIDE, WIDE)
            sources = (weight.at[:, pl.ds(col, count * WIDE)], *mine[2 * chunk : 2 * chunk + 2])
            group = [
                pltpu.make_async_copy(source, slot.at[pl.ds(i * depth, depth), :], sem.at[i])
                for i, source in enumerate(sources)
            ]
            for move in group:
                move.start()
            for j in range(count):
                to = slot.at[pl.ds(3 * depth, depth), pl.ds(j * WIDE, WIDE)]
                for i in range(4):

                    @pl.when(place_ref[1 + i] == lot + j)
                    def _():
                        pltpu.make_async_copy(far[i], to, sem.at[3 + j]).start()

                group.append(pltpu.make_async_copy(far[0], to, sem.at[3 + j]))
            steps.append((slot, col, count * WIDE, group))
    at = 0
    for ref in atts:
        size = ref.shape[2]
        att[:rows, at : at + size] = ref[0]
        att[rows:, at : at + size] = ref[1]
        at += size
    for slot, col, width, group in steps:
        for move in group:
            move.wait()
        sums = jnp.dot(att[...], slot[...], preferred_element_type=jnp.float32)
        branch, t_branch = sums[:rows], sums[rows:]
        cols = pl.ds(col, width)
        g = gate[:, cols].astype(jnp.float32)
        tg = t_gate[:, cols].astype(jnp.float32)
        result[:, cols] = (stream[:, cols].astype(jnp.float32) + g * branch).astype(result.dtype)
        t_result[:, cols] = (
            t_stream[:, cols].astype(jnp.float32) + tg * branch + g * t_branch
        ).astype(t_result.dtype)


def project(place, atts, stream, t_stream, gate, t_gate, weight, pieces):
    rows, columns = stream.shape
    depth = weight.shape[0]
    whole = pl.BlockSpec(memory_space=pltpu.VMEM)
    away = pl.BlockSpec(memory_space=pl.ANY)
    return pl.pallas_call(
        functools.partial(project_kernel, len(atts)),
        in_specs=[pl.BlockSpec(memory_space=pltpu.SMEM)]
        + [whole] * (len(atts) + 4)
        + [away] * (1 + len(pieces)),
        out_specs=[whole] * 2,
        out_shape=[jax.ShapeDtypeStruct((rows, columns), stream.dtype)] * 2,
        scratch_shapes=[
            pltpu.VMEM((2 * rows, 4 * depth), jnp.bfloat16),
            pltpu.VMEM((2, 4 * depth, WIDE), jnp.bfloat16),
            pltpu.VMEM((2, 4 * depth, 3 * WIDE), jnp.bfloat16),
            pltpu.SemaphoreType.DMA((4, 6)),
        ],
        compiler_params=pltpu.CompilerParams(vmem_limit_bytes=VMEM),
        cost_estimate=pl.CostEstimate(flops=1000, bytes_accessed=1000, transcendentals=0),
    )(place, *atts, stream, t_stream, gate, t_gate, weight, *pieces)


def on_device(
    queries, keys, values, t_queries, t_keys, t_values, out_weight, stream, t_stream, gate, t_gate
):
    heads = queries.shape[1] // HD
    depth = out_weight.shape[0]
    half_width = out_weight.shape[1] // 2
    cut = heads - 1
    core, side, me = lax.axis_index("core"), lax.axis_index("xl"), lax.axis_index("head")
    x = 2 * lax.axis_index("dp") + side
    places = [x, x ^ 1, 3 - x, 3 - (x ^ 1)]

    def quarter(place, count=1):
        return lax.dynamic_slice(
            out_weight, (0, core * half_width + place * WIDE), (depth, count * WIDE)
        )

    def tie(value, *earlier):
        return lax.optimization_barrier((value, *earlier))[0]

    def neighbours(lot, *earlier, count=1):
        value = quarter(lot, count)
        if earlier:
            value = tie(value, *earlier)
        return shift(value, "head", 1), shift(value, "head", -1)

    def other_core(*pieces):
        return [shift(piece, "core", 1) for piece in pieces]

    lot_a, lot_b, near_q = pack(cut, queries, t_queries, keys, t_keys, values, t_values)
    kv_a = lax.all_gather(lot_a, ("z", "core"))
    kv_b = lax.all_gather(lot_b, ("z", "core"))
    far_q = shift(near_q, "xl", 1)
    gates = gate.reshape(1, -1), t_gate.reshape(1, -1)
    place = jnp.stack([core, *places]).astype(jnp.int32)
    where = me.astype(jnp.int32).reshape(1)

    far0 = tie(shift(quarter(places[0]), "head", 2), far_q)
    first = neighbours(0)
    far1, far2 = shift(far0, "xl", 1), swap_parts(far0)
    second = neighbours(1, *first, count=3)
    first2, fars = other_core(*first), other_core(far0)
    far3 = swap_parts(far1)

    (far_a,) = attend(
        [tie(far_q, *first2, *fars, *gates, place, where)], 0, kv_a, [True]
    )
    sent_a = shift(far_a, "xl", 1)
    near_a = attend([tie(near_q, far_a, far1, far2)], 0, kv_a, [False])
    fars += other_core(*tie((far1, far2), far_a))
    last = tie(far_q, near_a[1], far3, *fars)
    far_b, *near_b = attend([last, near_q], cut, kv_b, [True, False])
    sent_b = shift(far_b, "xl", 1)
    fars += other_core(tie(far3, far_b))
    owners_a = merge(tie(where, far_b), *near_a, sent_a)
    owners = merge(tie(where, *fars), *near_b, sent_b, *owners_a)
    second2 = other_core(*tie(second, owners_a[0], sent_b))
    moved = [owners[0]] + [shift(owners[step], "head", step) for step in (1, 2, 3)]
    atts = [moved[step] for step in (0, 1, 3, 2)]
    pieces = [*first, *second, far0, far1, far2, far3, *first2, *second2, *fars]
    return project(place, atts, stream, t_stream, *gates, out_weight, pieces)


def solution(mesh):
    fine = Mesh(
        mesh.devices.reshape(SIZES["xl"], SIZES["z"], SIZES["core"], SIZES["head"], -1),
        ("xl", "z", "core", "head", "dp"),
    )
    tokens = ("dp", "xl", "z", "core")
    spread = P(tokens, "head")
    rows = P((*tokens, "head"), None)
    return jax.shard_map(
        on_device,
        mesh=fine,
        in_specs=(spread,) * 6 + (P("head", None), rows, rows, P(), P()),
        out_specs=(rows, rows),
        check_vma=False,
    )
```

```python
import functools

import jax
import jax.numpy as jnp
from jax import lax
from jax.experimental import pallas as pl
from jax.experimental.pallas import tpu as pltpu
from jax.sharding import Mesh
from jax.sharding import PartitionSpec as P

HD = 128
LOG2E = 1.4426950408889634
SCALE = HD**-0.5
CHUNK = 512
SIZES = {"xl": 2, "z": 4, "core": 2, "head": 4}
WIDE = 640
VMEM = 60 * 1024 * 1024


def shift(value, axis, step):
    size = SIZES[axis]
    return lax.ppermute(value, axis, [(i, (i + step) % size) for i in range(size)])


def swap_parts(value):
    return lax.ppermute(value, ("xl", "dp"), [(1, 2), (2, 1), (3, 0), (0, 3)])


def attend_kernel(sent, *refs):
    count = len(sent)
    queries, kv = refs[:count], refs[count]
    *outs, kk, vv, scores = refs[count + 1 :]
    blocks, _, size, _ = kv.shape
    keys = blocks * size
    for i in range(blocks):
        kk[i * size : (i + 1) * size, :] = kv[i, 0, :, : 2 * HD]
        vv[i * size : (i + 1) * size, :] = kv[i, 0, :, 2 * HD :]
    across = (((1,), (1,)), ((), ()))
    size = queries[0].shape[1]
    rows = count * size
    query = jnp.concatenate([q[0, :, :HD] for q in queries], axis=0)
    mixed = jnp.concatenate([q[0, :, HD:] for q in queries], axis=0)
    mixed = jnp.concatenate([mixed, query], axis=1)
    peak = None
    for c in range(0, keys, CHUNK):
        s = lax.dot_general(
            query, kk[c : c + CHUNK, :HD], across, preferred_element_type=jnp.float32
        )
        scores[:, c : c + CHUNK] = s
        for lane in range(0, CHUNK, 128):
            part = s[:, lane : lane + 128]
            peak = part if peak is None else jnp.maximum(peak, part)
    top = jnp.max(peak, axis=1, keepdims=True) * (SCALE * LOG2E)
    den = jnp.zeros((rows, 128), jnp.float32)
    mass = jnp.zeros((rows, 128), jnp.float32)
    wide = jnp.zeros((rows, 2 * HD), jnp.float32)
    tilt = jnp.zeros((rows, HD), jnp.float32)
    for c in range(0, keys, CHUNK):
        slope = lax.dot_general(
            mixed, kk[c : c + CHUNK, :], across, preferred_element_type=jnp.float32
        )
        w = jnp.exp2(scores[:, c : c + CHUNK] * (SCALE * LOG2E) - top)
        g = w * slope
        for lane in range(0, CHUNK, 128):
            den = den + w[:, lane : lane + 128]
            mass = mass + g[:, lane : lane + 128]
        wide = wide + jnp.dot(
            w.astype(jnp.bfloat16), vv[c : c + CHUNK, :], preferred_element_type=jnp.float32
        )
        tilt = tilt + jnp.dot(
            g.astype(jnp.bfloat16), vv[c : c + CHUNK, :HD], preferred_element_type=jnp.float32
        )
    den = jnp.sum(den, axis=1, keepdims=True)
    inverse = 1.0 / den
    mean = jnp.sum(mass, axis=1, keepdims=True) * (inverse * SCALE)
    out = wide[:, :HD] * inverse
    t_out = (tilt * SCALE + wide[:, HD:]) * inverse - mean * out
    lane = lax.broadcasted_iota(jnp.int32, (rows, 128), 1)
    both = jnp.where(lane == 0, top + jnp.log2(den), mean)
    outs = list(outs)
    for i, goes in enumerate(sent):
        mine = slice(i * size, (i + 1) * size)
        ref = outs.pop(0)
        ref[0, :size, :HD] = out[mine].astype(ref.dtype)
        ref[0, :size, HD:] = t_out[mine].astype(ref.dtype)
        stats = jnp.transpose(both[mine])
        if not goes:
            outs.pop(0)[0] = stats[:8, :]
            continue
        stats = stats[:2, :]
        high = stats.astype(jnp.bfloat16).astype(jnp.float32)
        middle = (stats - high).astype(jnp.bfloat16).astype(jnp.float32)
        low = stats - high - middle
        terms = jnp.concatenate([high, middle, low, jnp.zeros_like(low)], axis=0)
        over = 2 * HD
        rest = jnp.concatenate(
            [terms[:, over:], jnp.zeros((8, 2 * over - size), jnp.float32)], axis=1
        )
        ref[0, size:, :] = jnp.concatenate([terms[:, :over], rest], axis=0).astype(jnp.bfloat16)


def attend(queries, first, kv, sent):
    rows = queries[0].shape[1]
    blocks, heads, size, _ = kv.shape
    keys = blocks * size

    def spec(r, c, at=0):
        return pl.BlockSpec((1, r, c), lambda h: (h + at, 0, 0))

    specs, shapes = [], []
    for goes in sent:
        if goes:
            specs += [spec(rows + 16, 2 * HD)]
            shapes += [jax.ShapeDtypeStruct((heads, rows + 16, 2 * HD), jnp.bfloat16)]
        else:
            specs += [spec(rows, 2 * HD), spec(8, rows)]
            shapes += [
                jax.ShapeDtypeStruct((heads, rows, 2 * HD), jnp.float32),
                jax.ShapeDtypeStruct((heads, 8, rows), jnp.float32),
            ]
    total = len(sent) * rows
    return pl.pallas_call(
        functools.partial(attend_kernel, sent),
        grid=(heads,),
        in_specs=[spec(rows, 2 * HD, first)] * len(sent)
        + [pl.BlockSpec((blocks, 1, size, 4 * HD), lambda h: (0, h, 0, 0))],
        out_specs=specs,
        out_shape=shapes,
        scratch_shapes=[
            pltpu.VMEM((keys, 2 * HD), jnp.bfloat16),
            pltpu.VMEM((keys, 2 * HD), jnp.bfloat16),
            pltpu.VMEM((total, keys), jnp.float32),
        ],
        compiler_params=pltpu.CompilerParams(vmem_limit_bytes=VMEM),
        cost_estimate=pl.CostEstimate(
            flops=heads * total * keys * HD * 12, bytes_accessed=1000, transcendentals=0
        ),
    )(*queries, kv)


def merge_kernel(me_ref, near_ref, near_stat, far_ref, *refs):
    before, (*outs, both) = refs[:-5], refs[-5:]
    heads, count, _ = near_ref.shape
    for h in range(heads):
        lse_a, mean_a = near_stat[h, 0:1, :], near_stat[h, 1:2, :]
        terms = far_ref[h, count:, :].astype(jnp.float32)
        terms = jnp.concatenate([terms[:8], terms[8:, : count - 2 * HD]], axis=1)
        lse_b = terms[0:1] + terms[2:3] + terms[4:5]
        mean_b = terms[1:2] + terms[3:4] + terms[5:6]
        top = jnp.maximum(lse_a, lse_b)
        wa = jnp.exp2(lse_a - top)
        wb = jnp.exp2(lse_b - top)
        inverse = 1.0 / (wa + wb)
        wa = wa * inverse
        wb = wb * inverse
        mean = wa * mean_a + wb * mean_b
        terms = [wa, wb, wa * (mean_a - mean), wb * (mean_b - mean)]
        terms = jnp.transpose(jnp.concatenate(terms + terms, axis=0))
        wa, wb, da, db = (terms[:, i : i + 1] for i in range(4))
        near = near_ref[h]
        far = far_ref[h, :count, :].astype(jnp.float32)
        oa, ob = near[:, :HD], far[:, :HD]
        out = wa * oa + wb * ob
        t_out = wa * near[:, HD:] + wb * far[:, HD:] + da * oa + db * ob
        both[0, :, h * HD : (h + 1) * HD] = out.astype(both.dtype)
        both[1, :, h * HD : (h + 1) * HD] = t_out.astype(both.dtype)
    rows = outs[0].shape[1]
    for step in range(4):
        at = pl.multiple_of(lax.rem(me_ref[0] + step, 4) * rows, 16)
        done = 0
        if before:
            done = before[step].shape[2]
            outs[step][:, :, :done] = before[step][...]
        outs[step][:, :, done:] = both[:, pl.ds(at, rows), :]


def merge(me, near, near_stat, far, *before):
    heads, rows, _ = near.shape
    width = heads * HD + (before[0].shape[2] if before else 0)
    whole = pl.BlockSpec(memory_space=pltpu.VMEM)
    return pl.pallas_call(
        merge_kernel,
        in_specs=[pl.BlockSpec(memory_space=pltpu.SMEM)] + [whole] * (3 + len(before)),
        out_specs=[whole] * 4,
        out_shape=[jax.ShapeDtypeStruct((2, rows // 4, width), jnp.bfloat16)] * 4,
        scratch_shapes=[pltpu.VMEM((2, rows, heads * HD), jnp.bfloat16)],
        compiler_params=pltpu.CompilerParams(vmem_limit_bytes=VMEM),
        cost_estimate=pl.CostEstimate(flops=1000, bytes_accessed=1000, transcendentals=0),
    )(me, near, near_stat, far, *before)


def pack_kernel(cut, q, t_q, k, t_k, v, t_v, first_ref, second_ref, q_ref):
    heads = q.shape[1] // HD
    for h in range(heads):
        cols = slice(h * HD, (h + 1) * HD)
        out, at = (first_ref, h) if h < cut else (second_ref, h - cut)
        for i, ref in enumerate((k, t_k, v, t_v)):
            out[at, :, i * HD : (i + 1) * HD] = ref[:, cols]
        q_ref[h, :, :HD] = q[:, cols]
        q_ref[h, :, HD:] = t_q[:, cols]


def pack(cut, *arrays):
    rows, width = arrays[0].shape
    heads = width // HD
    whole = pl.BlockSpec(memory_space=pltpu.VMEM)
    return pl.pallas_call(
        functools.partial(pack_kernel, cut),
        in_specs=[whole] * 6,
        out_specs=[whole] * 3,
        out_shape=[
            jax.ShapeDtypeStruct((cut, rows, 4 * HD), jnp.bfloat16),
            jax.ShapeDtypeStruct((heads - cut, rows, 4 * HD), jnp.bfloat16),
            jax.ShapeDtypeStruct((heads, rows, 2 * HD), jnp.bfloat16),
        ],
        compiler_params=pltpu.CompilerParams(vmem_limit_bytes=VMEM),
        cost_estimate=pl.CostEstimate(flops=1000, bytes_accessed=1000, transcendentals=0),
    )(*arrays)


def project_kernel(parts, place_ref, *refs):
    atts, refs = refs[:parts], refs[parts:]
    stream, t_stream, gate, t_gate, weight = refs[:5]
    pieces = refs[5:21]
    result, t_result, att, narrow, broad, sems = refs[21:]
    rows = stream.shape[0]
    depth = weight.shape[0]
    core = place_ref[0]
    steps = []
    for chunk, lot, count in ((1, 1, 3), (0, 0, 1)):
        for half in range(2):
            mine = pieces[8 * half : 8 * half + 8]
            far = mine[4:]
            slot = (narrow, broad)[chunk].at[half]
            sem = sems.at[2 * half + chunk]
            col = pl.multiple_of((lax.rem(core + half, 2) * 4 + lot) * WIDE, WIDE)
            sources = (weight.at[:, pl.ds(col, count * WIDE)], *mine[2 * chunk : 2 * chunk + 2])
            group = [
                pltpu.make_async_copy(source, slot.at[pl.ds(i * depth, depth), :], sem.at[i])
                for i, source in enumerate(sources)
            ]
            for move in group:
                move.start()
            for j in range(count):
                to = slot.at[pl.ds(3 * depth, depth), pl.ds(j * WIDE, WIDE)]
                for i in range(4):

                    @pl.when(place_ref[1 + i] == lot + j)
                    def _():
                        pltpu.make_async_copy(far[i], to, sem.at[3 + j]).start()

                group.append(pltpu.make_async_copy(far[0], to, sem.at[3 + j]))
            steps.append((slot, col, count * WIDE, group))
    at = 0
    for ref in atts:
        size = ref.shape[2]
        att[:rows, at : at + size] = ref[0]
        att[rows:, at : at + size] = ref[1]
        at += size
    for slot, col, width, group in steps:
        for move in group:
            move.wait()
        sums = jnp.dot(att[...], slot[...], preferred_element_type=jnp.float32)
        branch, t_branch = sums[:rows], sums[rows:]
        cols = pl.ds(col, width)
        g = gate[:, cols].astype(jnp.float32)
        tg = t_gate[:, cols].astype(jnp.float32)
        result[:, cols] = (stream[:, cols].astype(jnp.float32) + g * branch).astype(result.dtype)
        t_result[:, cols] = (
            t_stream[:, cols].astype(jnp.float32) + tg * branch + g * t_branch
        ).astype(t_result.dtype)


def project(place, atts, stream, t_stream, gate, t_gate, weight, pieces):
    rows, columns = stream.shape
    depth = weight.shape[0]
    whole = pl.BlockSpec(memory_space=pltpu.VMEM)
    away = pl.BlockSpec(memory_space=pl.ANY)
    return pl.pallas_call(
        functools.partial(project_kernel, len(atts)),
        in_specs=[pl.BlockSpec(memory_space=pltpu.SMEM)]
        + [whole] * (len(atts) + 4)
        + [away] * (1 + len(pieces)),
        out_specs=[whole] * 2,
        out_shape=[jax.ShapeDtypeStruct((rows, columns), stream.dtype)] * 2,
        scratch_shapes=[
            pltpu.VMEM((2 * rows, 4 * depth), jnp.bfloat16),
            pltpu.VMEM((2, 4 * depth, WIDE), jnp.bfloat16),
            pltpu.VMEM((2, 4 * depth, 3 * WIDE), jnp.bfloat16),
            pltpu.SemaphoreType.DMA((4, 6)),
        ],
        compiler_params=pltpu.CompilerParams(vmem_limit_bytes=VMEM),
        cost_estimate=pl.CostEstimate(flops=1000, bytes_accessed=1000, transcendentals=0),
    )(place, *atts, stream, t_stream, gate, t_gate, weight, *pieces)


def on_device(
    queries, keys, values, t_queries, t_keys, t_values, out_weight, stream, t_stream, gate, t_gate
):
    heads = queries.shape[1] // HD
    depth = out_weight.shape[0]
    half_width = out_weight.shape[1] // 2
    cut = heads - 1
    core, side, me = lax.axis_index("core"), lax.axis_index("xl"), lax.axis_index("head")
    x = 2 * lax.axis_index("dp") + side
    places = [x, x ^ 1, 3 - x, 3 - (x ^ 1)]

    def quarter(place, count=1):
        return lax.dynamic_slice(
            out_weight, (0, core * half_width + place * WIDE), (depth, count * WIDE)
        )

    def tie(value, *earlier):
        return lax.optimization_barrier((value, *earlier))[0]

    def neighbours(lot, *earlier, count=1):
        value = quarter(lot, count)
        if earlier:
            value = tie(value, *earlier)
        return shift(value, "head", 1), shift(value, "head", -1)

    def other_core(*pieces):
        return [shift(piece, "core", 1) for piece in pieces]

    lot_a, lot_b, near_q = pack(cut, queries, t_queries, keys, t_keys, values, t_values)
    kv_a = lax.all_gather(lot_a, ("z", "core"))
    kv_b = lax.all_gather(lot_b, ("z", "core"))
    far_q = shift(near_q, "xl", 1)
    gates = gate.reshape(1, -1), t_gate.reshape(1, -1)
    place = jnp.stack([core, *places]).astype(jnp.int32)
    where = me.astype(jnp.int32).reshape(1)

    far0 = tie(shift(quarter(places[0]), "head", 2), far_q)
    first = neighbours(0)
    far1, far2 = shift(far0, "xl", 1), swap_parts(far0)
    second = neighbours(1, *first, far1, far2, count=3)
    first2, fars = other_core(*first), other_core(far0)
    far3 = swap_parts(far1)

    (far_a,) = attend(
        [tie(far_q, *first2, *fars, *gates, place, where)], 0, kv_a, [True]
    )
    sent_a = shift(far_a, "xl", 1)
    near_a = attend([tie(near_q, far_a, far1, far2)], 0, kv_a, [False])
    fars += other_core(*tie((far1, far2), far_a))
    last = tie(far_q, near_a[1], far3, *fars)
    far_b, *near_b = attend([last, near_q], cut, kv_b, [True, False])
    sent_b = shift(far_b, "xl", 1)
    fars += other_core(tie(far3, far_b))
    owners_a = merge(tie(where, far_b), *near_a, sent_a)
    owners = merge(tie(where, *fars), *near_b, sent_b, *owners_a)
    second2 = other_core(*tie(second, owners_a[0], sent_b))
    moved = [owners[0]] + [shift(owners[step], "head", step) for step in (1, 2, 3)]
    atts = [moved[step] for step in (0, 1, 3, 2)]
    pieces = [*first, *second, far0, far1, far2, far3, *first2, *second2, *fars]
    return project(place, atts, stream, t_stream, *gates, out_weight, pieces)


def solution(mesh):
    fine = Mesh(
        mesh.devices.reshape(SIZES["xl"], SIZES["z"], SIZES["core"], SIZES["head"], -1),
        ("xl", "z", "core", "head", "dp"),
    )
    tokens = ("dp", "xl", "z", "core")
    spread = P(tokens, "head")
    rows = P((*tokens, "head"), None)
    return jax.shard_map(
        on_device,
        mesh=fine,
        in_specs=(spread,) * 6 + (P("head", None), rows, rows, P(), P()),
        out_specs=(rows, rows),
        check_vma=False,
    )
```

```python
import functools

import jax
import jax.numpy as jnp
from jax import lax
from jax.experimental import pallas as pl
from jax.experimental.pallas import tpu as pltpu
from jax.sharding import Mesh
from jax.sharding import PartitionSpec as P

HD = 128
LOG2E = 1.4426950408889634
SCALE = HD**-0.5
CHUNK = 512
SIZES = {"xl": 2, "z": 4, "core": 2, "head": 4}
WIDE = 640
VMEM = 60 * 1024 * 1024


def shift(value, axis, step):
    size = SIZES[axis]
    return lax.ppermute(value, axis, [(i, (i + step) % size) for i in range(size)])


def swap_parts(value):
    return lax.ppermute(value, ("xl", "dp"), [(1, 2), (2, 1), (3, 0), (0, 3)])


def attend_kernel(sent, *refs):
    count = len(sent)
    queries, kv = refs[:count], refs[count]
    *outs, kk, vv, scores = refs[count + 1 :]
    blocks, _, size, _ = kv.shape
    keys = blocks * size
    for i in range(blocks):
        kk[i * size : (i + 1) * size, :] = kv[i, 0, :, : 2 * HD]
        vv[i * size : (i + 1) * size, :] = kv[i, 0, :, 2 * HD :]
    across = (((1,), (1,)), ((), ()))
    size = queries[0].shape[1]
    rows = count * size
    query = jnp.concatenate([q[0, :, :HD] for q in queries], axis=0)
    mixed = jnp.concatenate([q[0, :, HD:] for q in queries], axis=0)
    mixed = jnp.concatenate([mixed, query], axis=1)
    peak = None
    for c in range(0, keys, CHUNK):
        s = lax.dot_general(
            query, kk[c : c + CHUNK, :HD], across, preferred_element_type=jnp.float32
        )
        scores[:, c : c + CHUNK] = s
        for lane in range(0, CHUNK, 128):
            part = s[:, lane : lane + 128]
            peak = part if peak is None else jnp.maximum(peak, part)
    top = jnp.max(peak, axis=1, keepdims=True) * (SCALE * LOG2E)
    den = jnp.zeros((rows, 128), jnp.float32)
    mass = jnp.zeros((rows, 128), jnp.float32)
    wide = jnp.zeros((rows, 2 * HD), jnp.float32)
    tilt = jnp.zeros((rows, HD), jnp.float32)
    for c in range(0, keys, CHUNK):
        slope = lax.dot_general(
            mixed, kk[c : c + CHUNK, :], across, preferred_element_type=jnp.float32
        )
        w = jnp.exp2(scores[:, c : c + CHUNK] * (SCALE * LOG2E) - top)
        g = w * slope
        for lane in range(0, CHUNK, 128):
            den = den + w[:, lane : lane + 128]
            mass = mass + g[:, lane : lane + 128]
        wide = wide + jnp.dot(
            w.astype(jnp.bfloat16), vv[c : c + CHUNK, :], preferred_element_type=jnp.float32
        )
        tilt = tilt + jnp.dot(
            g.astype(jnp.bfloat16), vv[c : c + CHUNK, :HD], preferred_element_type=jnp.float32
        )
    den = jnp.sum(den, axis=1, keepdims=True)
    inverse = 1.0 / den
    mean = jnp.sum(mass, axis=1, keepdims=True) * (inverse * SCALE)
    out = wide[:, :HD] * inverse
    t_out = (tilt * SCALE + wide[:, HD:]) * inverse - mean * out
    lane = lax.broadcasted_iota(jnp.int32, (rows, 128), 1)
    both = jnp.where(lane == 0, top + jnp.log2(den), mean)
    outs = list(outs)
    for i, goes in enumerate(sent):
        mine = slice(i * size, (i + 1) * size)
        ref = outs.pop(0)
        ref[0, :size, :HD] = out[mine].astype(ref.dtype)
        ref[0, :size, HD:] = t_out[mine].astype(ref.dtype)
        stats = jnp.transpose(both[mine])
        if not goes:
            outs.pop(0)[0] = stats[:8, :]
            continue
        stats = stats[:2, :]
        high = stats.astype(jnp.bfloat16).astype(jnp.float32)
        middle = (stats - high).astype(jnp.bfloat16).astype(jnp.float32)
        low = stats - high - middle
        terms = jnp.concatenate([high, middle, low, jnp.zeros_like(low)], axis=0)
        over = 2 * HD
        rest = jnp.concatenate(
            [terms[:, over:], jnp.zeros((8, 2 * over - size), jnp.float32)], axis=1
        )
        ref[0, size:, :] = jnp.concatenate([terms[:, :over], rest], axis=0).astype(jnp.bfloat16)


def attend(queries, first, kv, sent):
    rows = queries[0].shape[1]
    blocks, heads, size, _ = kv.shape
    keys = blocks * size

    def spec(r, c, at=0):
        return pl.BlockSpec((1, r, c), lambda h: (h + at, 0, 0))

    specs, shapes = [], []
    for goes in sent:
        if goes:
            specs += [spec(rows + 16, 2 * HD)]
            shapes += [jax.ShapeDtypeStruct((heads, rows + 16, 2 * HD), jnp.bfloat16)]
        else:
            specs += [spec(rows, 2 * HD), spec(8, rows)]
            shapes += [
                jax.ShapeDtypeStruct((heads, rows, 2 * HD), jnp.float32),
                jax.ShapeDtypeStruct((heads, 8, rows), jnp.float32),
            ]
    total = len(sent) * rows
    return pl.pallas_call(
        functools.partial(attend_kernel, sent),
        grid=(heads,),
        in_specs=[spec(rows, 2 * HD, first)] * len(sent)
        + [pl.BlockSpec((blocks, 1, size, 4 * HD), lambda h: (0, h, 0, 0))],
        out_specs=specs,
        out_shape=shapes,
        scratch_shapes=[
            pltpu.VMEM((keys, 2 * HD), jnp.bfloat16),
            pltpu.VMEM((keys, 2 * HD), jnp.bfloat16),
            pltpu.VMEM((total, keys), jnp.float32),
        ],
        compiler_params=pltpu.CompilerParams(vmem_limit_bytes=VMEM),
        cost_estimate=pl.CostEstimate(
            flops=heads * total * keys * HD * 12, bytes_accessed=1000, transcendentals=0
        ),
    )(*queries, kv)


def merge_kernel(me_ref, near_ref, near_stat, far_ref, *refs):
    before, (*outs, both) = refs[:-5], refs[-5:]
    heads, count, _ = near_ref.shape
    for h in range(heads):
        lse_a, mean_a = near_stat[h, 0:1, :], near_stat[h, 1:2, :]
        terms = far_ref[h, count:, :].astype(jnp.float32)
        terms = jnp.concatenate([terms[:8], terms[8:, : count - 2 * HD]], axis=1)
        lse_b = terms[0:1] + terms[2:3] + terms[4:5]
        mean_b = terms[1:2] + terms[3:4] + terms[5:6]
        top = jnp.maximum(lse_a, lse_b)
        wa = jnp.exp2(lse_a - top)
        wb = jnp.exp2(lse_b - top)
        inverse = 1.0 / (wa + wb)
        wa = wa * inverse
        wb = wb * inverse
        mean = wa * mean_a + wb * mean_b
        terms = [wa, wb, wa * (mean_a - mean), wb * (mean_b - mean)]
        terms = jnp.transpose(jnp.concatenate(terms + terms, axis=0))
        wa, wb, da, db = (terms[:, i : i + 1] for i in range(4))
        near = near_ref[h]
        far = far_ref[h, :count, :].astype(jnp.float32)
        oa, ob = near[:, :HD], far[:, :HD]
        out = wa * oa + wb * ob
        t_out = wa * near[:, HD:] + wb * far[:, HD:] + da * oa + db * ob
        both[0, :, h * HD : (h + 1) * HD] = out.astype(both.dtype)
        both[1, :, h * HD : (h + 1) * HD] = t_out.astype(both.dtype)
    rows = outs[0].shape[1]
    for step in range(4):
        at = pl.multiple_of(lax.rem(me_ref[0] + step, 4) * rows, 16)
        done = 0
        if before:
            done = before[step].shape[2]
            outs[step][:, :, :done] = before[step][...]
        outs[step][:, :, done:] = both[:, pl.ds(at, rows), :]


def merge(me, near, near_stat, far, *before):
    heads, rows, _ = near.shape
    width = heads * HD + (before[0].shape[2] if before else 0)
    whole = pl.BlockSpec(memory_space=pltpu.VMEM)
    return pl.pallas_call(
        merge_kernel,
        in_specs=[pl.BlockSpec(memory_space=pltpu.SMEM)] + [whole] * (3 + len(before)),
        out_specs=[whole] * 4,
        out_shape=[jax.ShapeDtypeStruct((2, rows // 4, width), jnp.bfloat16)] * 4,
        scratch_shapes=[pltpu.VMEM((2, rows, heads * HD), jnp.bfloat16)],
        compiler_params=pltpu.CompilerParams(vmem_limit_bytes=VMEM),
        cost_estimate=pl.CostEstimate(flops=1000, bytes_accessed=1000, transcendentals=0),
    )(me, near, near_stat, far, *before)


def pack_kernel(cut, q, t_q, k, t_k, v, t_v, first_ref, second_ref, q_ref):
    heads = q.shape[1] // HD
    for h in range(heads):
        cols = slice(h * HD, (h + 1) * HD)
        out, at = (first_ref, h) if h < cut else (second_ref, h - cut)
        for i, ref in enumerate((k, t_k, v, t_v)):
            out[at, :, i * HD : (i + 1) * HD] = ref[:, cols]
        q_ref[h, :, :HD] = q[:, cols]
        q_ref[h, :, HD:] = t_q[:, cols]


def pack(cut, *arrays):
    rows, width = arrays[0].shape
    heads = width // HD
    whole = pl.BlockSpec(memory_space=pltpu.VMEM)
    return pl.pallas_call(
        functools.partial(pack_kernel, cut),
        in_specs=[whole] * 6,
        out_specs=[whole] * 3,
        out_shape=[
            jax.ShapeDtypeStruct((cut, rows, 4 * HD), jnp.bfloat16),
            jax.ShapeDtypeStruct((heads - cut, rows, 4 * HD), jnp.bfloat16),
            jax.ShapeDtypeStruct((heads, rows, 2 * HD), jnp.bfloat16),
        ],
        compiler_params=pltpu.CompilerParams(vmem_limit_bytes=VMEM),
        cost_estimate=pl.CostEstimate(flops=1000, bytes_accessed=1000, transcendentals=0),
    )(*arrays)


def project_kernel(parts, place_ref, *refs):
    atts, refs = refs[:parts], refs[parts:]
    stream, t_stream, gate, t_gate, weight = refs[:5]
    pieces = refs[5:21]
    result, t_result, att, narrow, broad, sems = refs[21:]
    rows = stream.shape[0]
    depth = weight.shape[0]
    core = place_ref[0]
    steps = []
    for chunk, lot, count in ((1, 1, 3), (0, 0, 1)):
        for half in range(2):
            mine = pieces[8 * half : 8 * half + 8]
            far = mine[4:]
            slot = (narrow, broad)[chunk].at[half]
            sem = sems.at[2 * half + chunk]
            col = pl.multiple_of((lax.rem(core + half, 2) * 4 + lot) * WIDE, WIDE)
            sources = (weight.at[:, pl.ds(col, count * WIDE)], *mine[2 * chunk : 2 * chunk + 2])
            group = [
                pltpu.make_async_copy(source, slot.at[pl.ds(i * depth, depth), :], sem.at[i])
                for i, source in enumerate(sources)
            ]
            for move in group:
                move.start()
            for j in range(count):
                to = slot.at[pl.ds(3 * depth, depth), pl.ds(j * WIDE, WIDE)]
                for i in range(4):

                    @pl.when(place_ref[1 + i] == lot + j)
                    def _():
                        pltpu.make_async_copy(far[i], to, sem.at[3 + j]).start()

                group.append(pltpu.make_async_copy(far[0], to, sem.at[3 + j]))
            steps.append((slot, col, count * WIDE, group))
    at = 0
    for ref in atts:
        size = ref.shape[2]
        att[:rows, at : at + size] = ref[0]
        att[rows:, at : at + size] = ref[1]
        at += size
    for slot, col, width, group in steps:
        for move in group:
            move.wait()
        sums = jnp.dot(att[...], slot[...], preferred_element_type=jnp.float32)
        branch, t_branch = sums[:rows], sums[rows:]
        cols = pl.ds(col, width)
        g = gate[:, cols].astype(jnp.float32)
        tg = t_gate[:, cols].astype(jnp.float32)
        result[:, cols] = (stream[:, cols].astype(jnp.float32) + g * branch).astype(result.dtype)
        t_result[:, cols] = (
            t_stream[:, cols].astype(jnp.float32) + tg * branch + g * t_branch
        ).astype(t_result.dtype)


def project(place, atts, stream, t_stream, gate, t_gate, weight, pieces):
    rows, columns = stream.shape
    depth = weight.shape[0]
    whole = pl.BlockSpec(memory_space=pltpu.VMEM)
    away = pl.BlockSpec(memory_space=pl.ANY)
    return pl.pallas_call(
        functools.partial(project_kernel, len(atts)),
        in_specs=[pl.BlockSpec(memory_space=pltpu.SMEM)]
        + [whole] * (len(atts) + 4)
        + [away] * (1 + len(pieces)),
        out_specs=[whole] * 2,
        out_shape=[jax.ShapeDtypeStruct((rows, columns), stream.dtype)] * 2,
        scratch_shapes=[
            pltpu.VMEM((2 * rows, 4 * depth), jnp.bfloat16),
            pltpu.VMEM((2, 4 * depth, WIDE), jnp.bfloat16),
            pltpu.VMEM((2, 4 * depth, 3 * WIDE), jnp.bfloat16),
            pltpu.SemaphoreType.DMA((4, 6)),
        ],
        compiler_params=pltpu.CompilerParams(vmem_limit_bytes=VMEM),
        cost_estimate=pl.CostEstimate(flops=1000, bytes_accessed=1000, transcendentals=0),
    )(place, *atts, stream, t_stream, gate, t_gate, weight, *pieces)


def on_device(
    queries, keys, values, t_queries, t_keys, t_values, out_weight, stream, t_stream, gate, t_gate
):
    heads = queries.shape[1] // HD
    depth = out_weight.shape[0]
    half_width = out_weight.shape[1] // 2
    cut = heads - 1
    core, side, me = lax.axis_index("core"), lax.axis_index("xl"), lax.axis_index("head")
    x = 2 * lax.axis_index("dp") + side
    places = [x, x ^ 1, 3 - x, 3 - (x ^ 1)]

    def quarter(place, count=1):
        return lax.dynamic_slice(
            out_weight, (0, core * half_width + place * WIDE), (depth, count * WIDE)
        )

    def tie(value, *earlier):
        return lax.optimization_barrier((value, *earlier))[0]

    def neighbours(lot, *earlier, count=1):
        value = quarter(lot, count)
        if earlier:
            value = tie(value, *earlier)
        return shift(value, "head", 1), shift(value, "head", -1)

    def other_core(*pieces):
        return [shift(piece, "core", 1) for piece in pieces]

    lot_a, lot_b, near_q = pack(cut, queries, t_queries, keys, t_keys, values, t_values)
    kv_a = lax.all_gather(lot_a, ("z", "core"))
    kv_b = lax.all_gather(lot_b, ("z", "core"))
    far_q = shift(near_q, "xl", 1)
    gates = gate.reshape(1, -1), t_gate.reshape(1, -1)
    place = jnp.stack([core, *places]).astype(jnp.int32)
    where = me.astype(jnp.int32).reshape(1)

    far0 = tie(shift(quarter(places[0]), "head", 2), far_q)
    first = neighbours(0)
    far1, far2 = shift(far0, "xl", 1), swap_parts(far0)
    second = neighbours(1, *first, far1, far2, count=3)
    first2, fars = other_core(*first), other_core(far0)
    far3 = swap_parts(far1)

    (far_a,) = attend(
        [tie(far_q, *first2, *fars, *gates, place, where)], 0, kv_a, [True]
    )
    sent_a = shift(far_a, "xl", 1)
    near_a = attend([tie(near_q, far_a, far1, far2)], 0, kv_a, [False])
    fars += other_core(*tie((far1, far2, far3), far_a))
    last = tie(far_q, near_a[1], *fars)
    far_b, *near_b = attend([last, near_q], cut, kv_b, [True, False])
    sent_b = shift(far_b, "xl", 1)
    owners_a = merge(tie(where, far_b), *near_a, sent_a)
    owners = merge(where, *near_b, sent_b, *owners_a)
    second2 = other_core(*tie(second, owners_a[0], sent_b))
    moved = [owners[0]] + [shift(owners[step], "head", step) for step in (1, 2, 3)]
    atts = [moved[step] for step in (0, 1, 3, 2)]
    pieces = [*first, *second, far0, far1, far2, far3, *first2, *second2, *fars]
    return project(place, atts, stream, t_stream, *gates, out_weight, pieces)


def solution(mesh):
    fine = Mesh(
        mesh.devices.reshape(SIZES["xl"], SIZES["z"], SIZES["core"], SIZES["head"], -1),
        ("xl", "z", "core", "head", "dp"),
    )
    tokens = ("dp", "xl", "z", "core")
    spread = P(tokens, "head")
    rows = P((*tokens, "head"), None)
    return jax.shard_map(
        on_device,
        mesh=fine,
        in_specs=(spread,) * 6 + (P("head", None), rows, rows, P(), P()),
        out_specs=(rows, rows),
        check_vma=False,
    )
```

```python
import functools

import jax
import jax.numpy as jnp
from jax import lax
from jax.experimental import pallas as pl
from jax.experimental.pallas import tpu as pltpu
from jax.sharding import Mesh
from jax.sharding import PartitionSpec as P

HD = 128
LOG2E = 1.4426950408889634
SCALE = HD**-0.5
CHUNK = 512
SIZES = {"xl": 2, "z": 4, "core": 2, "head": 4}
WIDE = 640
VMEM = 60 * 1024 * 1024


def shift(value, axis, step):
    size = SIZES[axis]
    return lax.ppermute(value, axis, [(i, (i + step) % size) for i in range(size)])


def swap_parts(value):
    return lax.ppermute(value, ("xl", "dp"), [(1, 2), (2, 1), (3, 0), (0, 3)])


def attend_kernel(sent, *refs):
    count = len(sent)
    queries, kv = refs[:count], refs[count]
    *outs, kk, vv, scores = refs[count + 1 :]
    blocks, _, size, _ = kv.shape
    keys = blocks * size
    for i in range(blocks):
        kk[i * size : (i + 1) * size, :] = kv[i, 0, :, : 2 * HD]
        vv[i * size : (i + 1) * size, :] = kv[i, 0, :, 2 * HD :]
    across = (((1,), (1,)), ((), ()))
    size = queries[0].shape[1]
    rows = count * size
    query = jnp.concatenate([q[0, :, :HD] for q in queries], axis=0)
    mixed = jnp.concatenate([q[0, :, HD:] for q in queries], axis=0)
    mixed = jnp.concatenate([mixed, query], axis=1)
    peak = None
    for c in range(0, keys, CHUNK):
        s = lax.dot_general(
            query, kk[c : c + CHUNK, :HD], across, preferred_element_type=jnp.float32
        )
        scores[:, c : c + CHUNK] = s
        for lane in range(0, CHUNK, 128):
            part = s[:, lane : lane + 128]
            peak = part if peak is None else jnp.maximum(peak, part)
    top = jnp.max(peak, axis=1, keepdims=True) * (SCALE * LOG2E)
    den = jnp.zeros((rows, 128), jnp.float32)
    mass = jnp.zeros((rows, 128), jnp.float32)
    wide = jnp.zeros((rows, 2 * HD), jnp.float32)
    tilt = jnp.zeros((rows, HD), jnp.float32)
    for c in range(0, keys, CHUNK):
        slope = lax.dot_general(
            mixed, kk[c : c + CHUNK, :], across, preferred_element_type=jnp.float32
        )
        w = jnp.exp2(scores[:, c : c + CHUNK] * (SCALE * LOG2E) - top)
        g = w * slope
        for lane in range(0, CHUNK, 128):
            den = den + w[:, lane : lane + 128]
            mass = mass + g[:, lane : lane + 128]
        wide = wide + jnp.dot(
            w.astype(jnp.bfloat16), vv[c : c + CHUNK, :], preferred_element_type=jnp.float32
        )
        tilt = tilt + jnp.dot(
            g.astype(jnp.bfloat16), vv[c : c + CHUNK, :HD], preferred_element_type=jnp.float32
        )
    den = jnp.sum(den, axis=1, keepdims=True)
    inverse = 1.0 / den
    mean = jnp.sum(mass, axis=1, keepdims=True) * (inverse * SCALE)
    out = wide[:, :HD] * inverse
    t_out = (tilt * SCALE + wide[:, HD:]) * inverse - mean * out
    lane = lax.broadcasted_iota(jnp.int32, (rows, 128), 1)
    both = jnp.where(lane == 0, top + jnp.log2(den), mean)
    outs = list(outs)
    for i, goes in enumerate(sent):
        mine = slice(i * size, (i + 1) * size)
        ref = outs.pop(0)
        ref[0, :size, :HD] = out[mine].astype(ref.dtype)
        ref[0, :size, HD:] = t_out[mine].astype(ref.dtype)
        stats = jnp.transpose(both[mine])
        if not goes:
            outs.pop(0)[0] = stats[:8, :]
            continue
        stats = stats[:2, :]
        high = stats.astype(jnp.bfloat16).astype(jnp.float32)
        middle = (stats - high).astype(jnp.bfloat16).astype(jnp.float32)
        low = stats - high - middle
        terms = jnp.concatenate([high, middle, low, jnp.zeros_like(low)], axis=0)
        over = 2 * HD
        rest = jnp.concatenate(
            [terms[:, over:], jnp.zeros((8, 2 * over - size), jnp.float32)], axis=1
        )
        ref[0, size:, :] = jnp.concatenate([terms[:, :over], rest], axis=0).astype(jnp.bfloat16)


def attend(queries, first, kv, sent):
    rows = queries[0].shape[1]
    blocks, heads, size, _ = kv.shape
    keys = blocks * size

    def spec(r, c, at=0):
        return pl.BlockSpec((1, r, c), lambda h: (h + at, 0, 0))

    specs, shapes = [], []
    for goes in sent:
        if goes:
            specs += [spec(rows + 16, 2 * HD)]
            shapes += [jax.ShapeDtypeStruct((heads, rows + 16, 2 * HD), jnp.bfloat16)]
        else:
            specs += [spec(rows, 2 * HD), spec(8, rows)]
            shapes += [
                jax.ShapeDtypeStruct((heads, rows, 2 * HD), jnp.float32),
                jax.ShapeDtypeStruct((heads, 8, rows), jnp.float32),
            ]
    total = len(sent) * rows
    return pl.pallas_call(
        functools.partial(attend_kernel, sent),
        grid=(heads,),
        in_specs=[spec(rows, 2 * HD, first)] * len(sent)
        + [pl.BlockSpec((blocks, 1, size, 4 * HD), lambda h: (0, h, 0, 0))],
        out_specs=specs,
        out_shape=shapes,
        scratch_shapes=[
            pltpu.VMEM((keys, 2 * HD), jnp.bfloat16),
            pltpu.VMEM((keys, 2 * HD), jnp.bfloat16),
            pltpu.VMEM((total, keys), jnp.float32),
        ],
        compiler_params=pltpu.CompilerParams(vmem_limit_bytes=VMEM),
        cost_estimate=pl.CostEstimate(
            flops=heads * total * keys * HD * 12, bytes_accessed=1000, transcendentals=0
        ),
    )(*queries, kv)


def merge_kernel(me_ref, near_ref, near_stat, far_ref, *refs):
    before, (*outs, both) = refs[:-5], refs[-5:]
    heads, count, _ = near_ref.shape
    for h in range(heads):
        lse_a, mean_a = near_stat[h, 0:1, :], near_stat[h, 1:2, :]
        terms = far_ref[h, count:, :].astype(jnp.float32)
        terms = jnp.concatenate([terms[:8], terms[8:, : count - 2 * HD]], axis=1)
        lse_b = terms[0:1] + terms[2:3] + terms[4:5]
        mean_b = terms[1:2] + terms[3:4] + terms[5:6]
        top = jnp.maximum(lse_a, lse_b)
        wa = jnp.exp2(lse_a - top)
        wb = jnp.exp2(lse_b - top)
        inverse = 1.0 / (wa + wb)
        wa = wa * inverse
        wb = wb * inverse
        mean = wa * mean_a + wb * mean_b
        terms = [wa, wb, wa * (mean_a - mean), wb * (mean_b - mean)]
        terms = jnp.transpose(jnp.concatenate(terms + terms, axis=0))
        wa, wb, da, db = (terms[:, i : i + 1] for i in range(4))
        near = near_ref[h]
        far = far_ref[h, :count, :].astype(jnp.float32)
        oa, ob = near[:, :HD], far[:, :HD]
        out = wa * oa + wb * ob
        t_out = wa * near[:, HD:] + wb * far[:, HD:] + da * oa + db * ob
        both[0, :, h * HD : (h + 1) * HD] = out.astype(both.dtype)
        both[1, :, h * HD : (h + 1) * HD] = t_out.astype(both.dtype)
    rows = outs[0].shape[1]
    for step in range(4):
        at = pl.multiple_of(lax.rem(me_ref[0] + step, 4) * rows, 16)
        done = 0
        if before:
            done = before[step].shape[2]
            outs[step][:, :, :done] = before[step][...]
        outs[step][:, :, done:] = both[:, pl.ds(at, rows), :]


def merge(me, near, near_stat, far, *before):
    heads, rows, _ = near.shape
    width = heads * HD + (before[0].shape[2] if before else 0)
    whole = pl.BlockSpec(memory_space=pltpu.VMEM)
    return pl.pallas_call(
        merge_kernel,
        in_specs=[pl.BlockSpec(memory_space=pltpu.SMEM)] + [whole] * (3 + len(before)),
        out_specs=[whole] * 4,
        out_shape=[jax.ShapeDtypeStruct((2, rows // 4, width), jnp.bfloat16)] * 4,
        scratch_shapes=[pltpu.VMEM((2, rows, heads * HD), jnp.bfloat16)],
        compiler_params=pltpu.CompilerParams(vmem_limit_bytes=VMEM),
        cost_estimate=pl.CostEstimate(flops=1000, bytes_accessed=1000, transcendentals=0),
    )(me, near, near_stat, far, *before)


def pack_kernel(cut, q, t_q, k, t_k, v, t_v, first_ref, second_ref, q_ref):
    heads = q.shape[1] // HD
    for h in range(heads):
        cols = slice(h * HD, (h + 1) * HD)
        out, at = (first_ref, h) if h < cut else (second_ref, h - cut)
        for i, ref in enumerate((k, t_k, v, t_v)):
            out[at, :, i * HD : (i + 1) * HD] = ref[:, cols]
        q_ref[h, :, :HD] = q[:, cols]
        q_ref[h, :, HD:] = t_q[:, cols]


def pack(cut, *arrays):
    rows, width = arrays[0].shape
    heads = width // HD
    whole = pl.BlockSpec(memory_space=pltpu.VMEM)
    return pl.pallas_call(
        functools.partial(pack_kernel, cut),
        in_specs=[whole] * 6,
        out_specs=[whole] * 3,
        out_shape=[
            jax.ShapeDtypeStruct((cut, rows, 4 * HD), jnp.bfloat16),
            jax.ShapeDtypeStruct((heads - cut, rows, 4 * HD), jnp.bfloat16),
            jax.ShapeDtypeStruct((heads, rows, 2 * HD), jnp.bfloat16),
        ],
        compiler_params=pltpu.CompilerParams(vmem_limit_bytes=VMEM),
        cost_estimate=pl.CostEstimate(flops=1000, bytes_accessed=1000, transcendentals=0),
    )(*arrays)


def project_kernel(parts, place_ref, *refs):
    atts, refs = refs[:parts], refs[parts:]
    gate, t_gate, stream_in, t_stream_in, weight = refs[:5]
    pieces = refs[5:21]
    result, t_result, att, streams, narrow, broad, stream_sems, sems = refs[21:]
    rows = stream_in.shape[0]
    depth = weight.shape[0]
    core = place_ref[0]
    steps = []
    for chunk, lot, count in ((1, 1, 3), (0, 0, 1)):
        for half in range(2):
            mine = pieces[8 * half : 8 * half + 8]
            far = mine[4:]
            slot = (narrow, broad)[chunk].at[half]
            sem = sems.at[2 * half + chunk]
            col = pl.multiple_of((lax.rem(core + half, 2) * 4 + lot) * WIDE, WIDE)
            sources = (weight.at[:, pl.ds(col, count * WIDE)], *mine[2 * chunk : 2 * chunk + 2])
            group = [
                pltpu.make_async_copy(source, slot.at[pl.ds(i * depth, depth), :], sem.at[i])
                for i, source in enumerate(sources)
            ]
            for move in group:
                move.start()
            for j in range(count):
                to = slot.at[pl.ds(3 * depth, depth), pl.ds(j * WIDE, WIDE)]
                for i in range(4):

                    @pl.when(place_ref[1 + i] == lot + j)
                    def _():
                        pltpu.make_async_copy(far[i], to, sem.at[3 + j]).start()

                group.append(pltpu.make_async_copy(far[0], to, sem.at[3 + j]))
            steps.append((slot, col, count * WIDE, group))
    moves = [
        pltpu.make_async_copy(source, streams.at[i], stream_sems.at[i])
        for i, source in enumerate((stream_in, t_stream_in))
    ]
    for move in moves:
        move.start()
    at = 0
    for ref in atts:
        size = ref.shape[2]
        att[:rows, at : at + size] = ref[0]
        att[rows:, at : at + size] = ref[1]
        at += size
    for i, (slot, col, width, group) in enumerate(steps):
        if i == 0:
            group = group + moves
        for move in group:
            move.wait()
        sums = jnp.dot(att[...], slot[...], preferred_element_type=jnp.float32)
        branch, t_branch = sums[:rows], sums[rows:]
        cols = pl.ds(col, width)
        g = gate[:, cols].astype(jnp.float32)
        tg = t_gate[:, cols].astype(jnp.float32)
        result[:, cols] = (streams[0, :, cols].astype(jnp.float32) + g * branch).astype(result.dtype)
        t_result[:, cols] = (
            streams[1, :, cols].astype(jnp.float32) + tg * branch + g * t_branch
        ).astype(t_result.dtype)


def project(place, atts, stream, t_stream, gate, t_gate, weight, pieces):
    rows, columns = stream.shape
    depth = weight.shape[0]
    whole = pl.BlockSpec(memory_space=pltpu.VMEM)
    away = pl.BlockSpec(memory_space=pl.ANY)
    return pl.pallas_call(
        functools.partial(project_kernel, len(atts)),
        in_specs=[pl.BlockSpec(memory_space=pltpu.SMEM)]
        + [whole] * (len(atts) + 2)
        + [away] * (3 + len(pieces)),
        out_specs=[whole] * 2,
        out_shape=[jax.ShapeDtypeStruct((rows, columns), stream.dtype)] * 2,
        scratch_shapes=[
            pltpu.VMEM((2 * rows, 4 * depth), jnp.bfloat16),
            pltpu.VMEM((2, rows, columns), jnp.bfloat16),
            pltpu.VMEM((2, 4 * depth, WIDE), jnp.bfloat16),
            pltpu.VMEM((2, 4 * depth, 3 * WIDE), jnp.bfloat16),
            pltpu.SemaphoreType.DMA((2,)),
            pltpu.SemaphoreType.DMA((4, 6)),
        ],
        compiler_params=pltpu.CompilerParams(vmem_limit_bytes=VMEM),
        cost_estimate=pl.CostEstimate(flops=1000, bytes_accessed=1000, transcendentals=0),
    )(place, *atts, gate, t_gate, stream, t_stream, weight, *pieces)


def on_device(
    queries, keys, values, t_queries, t_keys, t_values, out_weight, stream, t_stream, gate, t_gate
):
    heads = queries.shape[1] // HD
    depth = out_weight.shape[0]
    half_width = out_weight.shape[1] // 2
    cut = heads - 1
    core, side, me = lax.axis_index("core"), lax.axis_index("xl"), lax.axis_index("head")
    x = 2 * lax.axis_index("dp") + side
    places = [x, x ^ 1, 3 - x, 3 - (x ^ 1)]

    def quarter(place, count=1):
        return lax.dynamic_slice(
            out_weight, (0, core * half_width + place * WIDE), (depth, count * WIDE)
        )

    def tie(value, *earlier):
        return lax.optimization_barrier((value, *earlier))[0]

    def neighbours(lot, *earlier, count=1):
        value = quarter(lot, count)
        if earlier:
            value = tie(value, *earlier)
        return shift(value, "head", 1), shift(value, "head", -1)

    def other_core(*pieces):
        return [shift(piece, "core", 1) for piece in pieces]

    lot_a, lot_b, near_q = pack(cut, queries, t_queries, keys, t_keys, values, t_values)
    kv_a = lax.all_gather(lot_a, ("z", "core"))
    kv_b = lax.all_gather(lot_b, ("z", "core"))
    far_q = shift(near_q, "xl", 1)
    gates = gate.reshape(1, -1), t_gate.reshape(1, -1)
    place = jnp.stack([core, *places]).astype(jnp.int32)
    where = me.astype(jnp.int32).reshape(1)

    far0 = tie(shift(quarter(places[0]), "head", 2), far_q)
    first = neighbours(0)
    far1, far2 = shift(far0, "xl", 1), swap_parts(far0)
    second = neighbours(1, *first, far1, far2, count=3)
    first2, fars = other_core(*first), other_core(far0)
    far3 = swap_parts(far1)

    (far_a,) = attend(
        [tie(far_q, *first2, *fars, *gates, place, where)], 0, kv_a, [True]
    )
    sent_a = shift(far_a, "xl", 1)
    near_a = attend([tie(near_q, far_a, far1, far2)], 0, kv_a, [False])
    fars += other_core(*tie((far1, far2, far3), far_a))
    last = tie(far_q, near_a[1], *fars)
    far_b, *near_b = attend([last, near_q], cut, kv_b, [True, False])
    sent_b = shift(far_b, "xl", 1)
    owners_a = merge(tie(where, far_b), *near_a, sent_a)
    owners = merge(where, *near_b, sent_b, *owners_a)
    second2 = other_core(*tie(second, owners_a[0], sent_b))
    moved = [owners[0]] + [shift(owners[step], "head", step) for step in (1, 2, 3)]
    atts = [moved[step] for step in (0, 1, 3, 2)]
    pieces = [*first, *second, far0, far1, far2, far3, *first2, *second2, *fars]
    return project(place, atts, stream, t_stream, *gates, out_weight, pieces)


def solution(mesh):
    fine = Mesh(
        mesh.devices.reshape(SIZES["xl"], SIZES["z"], SIZES["core"], SIZES["head"], -1),
        ("xl", "z", "core", "head", "dp"),
    )
    tokens = ("dp", "xl", "z", "core")
    spread = P(tokens, "head")
    rows = P((*tokens, "head"), None)
    return jax.shard_map(
        on_device,
        mesh=fine,
        in_specs=(spread,) * 6 + (P("head", None), rows, rows, P(), P()),
        out_specs=(rows, rows),
        check_vma=False,
    )
```
